128 devices in a mesh: ctx: 16 (over y_lo, x, core), fsdp: 8 (over y_hi, z).
Axes of the slice: x: 4, y: 4 (y_hi: 2, y_lo: 2; y = y_hi * 2 + y_lo), z: 4, core: 2. Of those that a mesh axis runs over, the one named last changes fastest.
Arguments:
- inputs: bfloat16 [8, 2048, 960], P('fsdp', 'ctx'), may hold values from -6 to 6
- doc_offsets: int32 [8, 5], P('fsdp'), may hold values from 0 to 2048, as said below
- attn_gain: float32 [960], replicated, may hold values from 0.1 to 1.9
- query_weight: bfloat16 [960, 960], P('fsdp', 'ctx'), may hold values from -0.1875 to 0.1875
- key_weight: bfloat16 [960, 320], P('fsdp', 'ctx'), may hold values from -0.1875 to 0.1875
- value_weight: bfloat16 [960, 320], P('fsdp', 'ctx'), may hold values from -0.1875 to 0.1875
- proj_weight: bfloat16 [960, 960], P('fsdp', 'ctx'), may hold values from -3.5 to 3.5
- ffn_gain: float32 [960], replicated, may hold values from 0.1 to 1.9
- gate_weight: bfloat16 [960, 2560], P('fsdp', 'ctx'), may hold values from -0.1875 to 0.1875
- up_weight: bfloat16 [960, 2560], P('fsdp', 'ctx'), may hold values from -0.1875 to 0.1875
- down_weight: bfloat16 [2560, 960], P('fsdp', 'ctx'), may hold values from -0.125 to 0.125
- cotangent: bfloat16 [8, 2048, 960], P('fsdp', 'ctx'), may hold values from -6 to 6
Outputs:
- layer_out: bfloat16 [8, 2048, 960], P('fsdp', 'ctx')
- input_grad: bfloat16 [8, 2048, 960], P('fsdp', 'ctx')
- attn_gain_grad: float32 [960], replicated
- query_grad: float32 [960, 960], P('fsdp', 'ctx')
- key_grad: float32 [960, 320], P('fsdp', 'ctx')
- value_grad: float32 [960, 320], P('fsdp', 'ctx')
- proj_grad: float32 [960, 960], P('fsdp', 'ctx')
- ffn_gain_grad: float32 [960], replicated
- gate_grad: float32 [960, 2560], P('fsdp', 'ctx')
- up_grad: float32 [960, 2560], P('fsdp', 'ctx')
- down_grad: float32 [2560, 960], P('fsdp', 'ctx')
The draws below stay inside these ranges and needn't reach their ends.
Inputs may be any that keep to these rules, and one draw needn't show every extreme that they name: `doc_offsets`: per sequence, 5 strictly rising offsets, the first 0 and the last 2048; consecutive ones bound a document.
All inputs are finite; a program needn't handle non-finite values.
Results may differ from the reference program's by a relative error of at most 0.025.
Values may be sent and summed in bfloat16 or wider, within the bound.
A program may use at most 128 MiB of HBM per device.

```python
import jax
import jax.numpy as jnp
from jax import lax

D = 960
HEADS = 15
KVH = 5
HD = 64
FF = 2560
TOK_CTX = 128
NDOC = 4
QW = 960
KVW = 320
LEN = 2048
SEQS = 8


def draw_doc_offsets(key, part):
    key = jax.random.fold_in(key, 11)
    pick_key = jax.random.fold_in(key, 1)
    size_key = jax.random.fold_in(key, 2)
    upper = max(1, TOK_CTX // NDOC)
    small = jax.random.randint(size_key, (SEQS, NDOC), 1, upper + 1)
    chosen = jax.random.randint(pick_key, (SEQS, 1), 0, NDOC)
    which = jnp.arange(NDOC, dtype=jnp.int32)[None, :] == chosen
    others = jnp.sum(jnp.where(which, 0, small), axis=1, keepdims=True)
    sizes = jnp.where(which, LEN - others, small)
    return jnp.concatenate([jnp.zeros((SEQS, 1), jnp.int32), jnp.cumsum(sizes, axis=1)], axis=1).astype(jnp.int32)


def block_levels(key, dims, shards, smallest, high):
    level, own = 1.0, jax.random.fold_in(key, 6)
    for position, blocks in shards:
        steps = jnp.exp(jax.random.uniform(jax.random.fold_in(own, position), (blocks,), jnp.float32, smallest / len(shards), high / len(shards)))
        level = level * jnp.repeat(steps, dims[position] // blocks).reshape([-1 if axis == position else 1 for axis in range(len(dims))])
    return level


def bell_draw(own_key, shape, spread, bound, pieces=(), kind=jnp.bfloat16):
    level = block_levels(own_key, shape, pieces, -0.22, 0.18) if pieces else 1.0
    drawn = jax.random.normal(own_key, shape, jnp.float32) * spread * level
    return jnp.minimum(jnp.maximum(drawn, -bound), bound).astype(kind)


def setup_inputs(seed: int = 0) -> dict:
    arg_keys = jax.random.split(jax.random.key(seed), 13)
    return {
        "inputs": bell_draw(arg_keys[0], (SEQS, LEN, D), 1.0, 6.0, ((0, 8), (1, 16))),
        "doc_offsets": draw_doc_offsets(jax.random.fold_in(arg_keys[12], 71), 0),
        "attn_gain": jnp.clip(1.0 + 0.18 * jax.random.normal(arg_keys[2], (D,), jnp.float32), 0.1, 1.9),
        "query_weight": bell_draw(arg_keys[3], (D, QW), D ** -0.5, 0.1875, ((0, 8), (1, 16))),
        "key_weight": bell_draw(arg_keys[4], (D, KVW), D ** -0.5, 0.1875, ((0, 8), (1, 16))),
        "value_weight": bell_draw(arg_keys[5], (D, KVW), D ** -0.5, 0.1875, ((0, 8), (1, 16))),
        "proj_weight": bell_draw(arg_keys[6], (QW, D), (max(1, QW * 8 // LEN)) ** -0.5, 3.5, ((0, 8), (1, 16))),
        "ffn_gain": jnp.clip(1.0 + 0.18 * jax.random.normal(arg_keys[7], (D,), jnp.float32), 0.1, 1.9),
        "gate_weight": bell_draw(arg_keys[8], (D, FF), D ** -0.5, 0.1875, ((0, 8), (1, 16))),
        "up_weight": bell_draw(arg_keys[9], (D, FF), D ** -0.5, 0.1875, ((0, 8), (1, 16))),
        "down_weight": bell_draw(arg_keys[10], (FF, D), FF ** -0.5, 0.125, ((0, 8), (1, 16))),
        "cotangent": bell_draw(arg_keys[11], (SEQS, LEN, D), 1.0, 6.0, ((0, 8), (1, 16))),
    }


epsilon = 1e-05
highest = lax.Precision.HIGHEST

@jax.custom_vjp
def low(v):
    return lax.optimization_barrier(v.astype(jnp.bfloat16)).astype(jnp.float32)

@jax.custom_vjp
def low_back(v):
    return v

def low_keep(v):
    return (low(v), None)

def low_pass(kept, grad):
    return (grad,)

def back_keep(v):
    return (v, None)

def back_low(kept, grad):
    return (low(grad),)
low.defvjp(low_keep, low_pass)
low_back.defvjp(back_keep, back_low)

def layout(offsets, token_index):
    inner = offsets[1:NDOC]
    after = token_index[:, None] >= inner[None, :]
    segment = lax.optimization_barrier(jnp.sum(after.astype(jnp.int32), axis=1))
    starts = lax.optimization_barrier(jnp.max(jnp.where(after, inner[None, :], 0), axis=1))
    return (segment, token_index - starts)

def rotary(positions):
    half_dim = HD // 2
    rate_table = 10000.0 ** (-2.0 * jnp.arange(half_dim, dtype=jnp.float32) / HD)
    angles = positions.astype(jnp.float32)[:, None] * rate_table[None, :]
    cosine = jnp.cos(angles)
    sine_table = jnp.sin(angles)
    return (jnp.concatenate([cosine, cosine], axis=1), jnp.concatenate([sine_table, sine_table], axis=1))

def rotate(vectors, cosine, sine_table):
    half_dim = HD // 2
    turned = jnp.concatenate([-vectors[..., half_dim:], vectors[..., :half_dim]], axis=-1)
    return vectors * cosine[:, None, :] + turned * sine_table[:, None, :]

def attend(query_rot, key_rot, values, segment, token_index):
    block_size = min(512, LEN)
    block_count = LEN // block_size
    group_size = HEADS // KVH
    query_blocks = query_rot.reshape(block_count, block_size, KVH, group_size, HD)
    segment_blocks = segment.reshape(block_count, block_size)
    index_blocks = token_index.reshape(block_count, block_size)

    def one_block(element):
        block_query, block_segment, block_index = element
        scores = jnp.einsum('qhgd,khd->hgqk', block_query, key_rot, precision=highest) * HD ** (-0.5)
        scores = low_back(scores)
        allowed = (block_segment[:, None] == segment[None, :]) & (token_index[None, :] <= block_index[:, None])
        scores = jnp.where(allowed[None, None], scores, -1e+30)
        row_top = lax.optimization_barrier(jnp.max(scores, axis=-1, keepdims=True))
        raised = jnp.exp(scores - row_top)
        shares = raised / lax.optimization_barrier(jnp.sum(raised, axis=-1, keepdims=True))
        return jnp.einsum('hgqk,khd->qhgd', low(shares), values, precision=highest)
    mixed = lax.map(jax.checkpoint(one_block), (query_blocks, segment_blocks, index_blocks))
    return mixed.reshape(LEN, HEADS * HD)

def sequence_layer(tokens, offsets, weights):
    attn_gain, query_weight, key_weight, value_weight, proj_weight, ffn_gain, gate_weight, up_weight, down_weight = weights
    token_index = jnp.arange(LEN, dtype=jnp.int32)
    segment, positions = layout(offsets, token_index)
    cosine, sine_table = rotary(positions)
    attn_scale = lax.rsqrt(lax.optimization_barrier(jnp.mean(tokens * tokens, axis=-1, keepdims=True)) + epsilon)
    normed = low(tokens * attn_scale * attn_gain)
    queries = low_back(jnp.dot(normed, query_weight, precision=highest))
    keys_flat = low_back(jnp.dot(normed, key_weight, precision=highest))
    values = low(low_back(jnp.dot(normed, value_weight, precision=highest)))
    query_rot = low(rotate(queries.reshape(LEN, HEADS, HD), cosine, sine_table))
    key_rot = low(rotate(keys_flat.reshape(LEN, KVH, HD), cosine, sine_table))
    mixed = attend(query_rot.reshape(LEN, KVH, HEADS // KVH, HD), key_rot, values.reshape(LEN, KVH, HD), segment, token_index)
    attn_out = low(low_back(mixed))
    residual = tokens + low_back(jnp.dot(attn_out, proj_weight, precision=highest))
    ffn_scale = lax.rsqrt(lax.optimization_barrier(jnp.mean(residual * residual, axis=-1, keepdims=True)) + epsilon)
    normed_ffn = low(residual * ffn_scale * ffn_gain)
    gate_value = low_back(jnp.dot(normed_ffn, gate_weight, precision=highest))
    up_value = low_back(jnp.dot(normed_ffn, up_weight, precision=highest))
    hidden = low(gate_value * jax.nn.sigmoid(gate_value) * up_value)
    return residual + low_back(jnp.dot(hidden, down_weight, precision=highest))

def reference(inputs, doc_offsets, attn_gain, query_weight, key_weight, value_weight, proj_weight, ffn_gain, gate_weight, up_weight, down_weight, cotangent):
    weights = tuple((array.astype(jnp.float32) for array in (attn_gain, query_weight, key_weight, value_weight, proj_weight, ffn_gain, gate_weight, up_weight, down_weight)))

    def forward(tokens, *params):

        def per_sequence(element):
            return sequence_layer(element[0], element[1], params)
        return lax.map(jax.checkpoint(per_sequence), (tokens, doc_offsets))
    layer, pullback = jax.vjp(forward, inputs.astype(jnp.float32), *weights)
    grads = pullback(cotangent.astype(jnp.float32))
    return (layer.astype(jnp.bfloat16), grads[0].astype(jnp.bfloat16), grads[1], grads[2], grads[3], grads[4], grads[5], grads[6], grads[7], grads[8], grads[9])
```

```python
import functools

import jax
import jax.numpy as jnp
from jax import lax
from jax.experimental import pallas as pl
from jax.experimental.pallas import tpu as pltpu
from jax.sharding import PartitionSpec as P

D = 960
HEADS = 15
KVH = 5
HD = 64
NDOC = 4
QW = 960
KVW = 320
WIDE = 1024
TOK = 128

epsilon = 1e-05
block_rows = 512
masked_score = -1e30

MESH = pl.DeviceIdType.MESH
ANY = pl.BlockSpec(memory_space=pl.ANY)
VMEM = pl.BlockSpec(memory_space=pltpu.VMEM)
MIB = 1024 * 1024

ATTN_PARTS = ((0, 64), (64, 64), (128, 48))
ATTN_ROWS = 176
FFN_PARTS = ((0, 160), (160, 160), (320, 160))
FFN_ROWS = 480
HALF_FF = 1280
ORDERS = ((0, 1, 2), (1, 2, 0), (2, 0, 1))


def place():
    c = lax.axis_index("ctx")
    f = lax.axis_index("fsdp")
    x = lax.rem(lax.div(c, 2), 4)
    y = lax.div(f, 4) * 2 + lax.div(c, 8)
    return (x, y, lax.rem(f, 4)), lax.rem(c, 2)


def device(spot, core):
    x, y, z = spot
    return ((lax.rem(y, 2) * 4 + x) * 2 + core, lax.div(y, 2) * 4 + z)


def ring(value, by):
    return lax.rem(value + by + 4, 4)


def shifted(spot, axis, by):
    return tuple(ring(v, by) if i == axis else v for i, v in enumerate(spot))


def greet(devices):
    barrier = pltpu.get_barrier_semaphore()
    for target in devices:
        pl.semaphore_signal(barrier, inc=1, device_id=target, device_id_type=MESH)
    pl.semaphore_wait(barrier, len(devices))


def remote(src, dst, send, recv, target):
    copy = pltpu.make_async_remote_copy(
        src_ref=src, dst_ref=dst, send_sem=send, recv_sem=recv, device_id=target, device_id_type=MESH
    )
    copy.start()
    return copy


def view(ref, lead, spot, done, axis, position, rows, half=None):
    index = []
    cut = min(done) if (half is not None and done) else None
    for a in range(3):
        if a == cut:
            index.append(pl.ds(2 * half, 2))
        elif a in done:
            index.append(pl.ds(0, 4))
        elif a == axis:
            index.append(position)
        else:
            index.append(spot[a])
    low, count = rows
    if half is not None and not done:
        first = (count // 32) * 16
        low, count = (low, first) if half == 0 else (low + first, count - first)
    return ref.at[tuple(lead) + tuple(index) + (pl.ds(low, count),)]


def gather_kernel(
    attn_block, ffn_block, down_away, attn_all, ffn_all,
    ffn_own, down_in, send, recv, own_sem, pair_send, pair_recv,
):
    spot, core = place()
    sibling = device(spot, 1 - core)
    greet([device(shifted(spot, a, by), core) for a in range(3) for by in (1, -1)] + [sibling])
    down_copy = remote(down_away, down_in, pair_send.at[3], pair_recv.at[3], sibling)
    own_attn = pltpu.make_async_copy(attn_block, attn_all.at[core, spot[0], spot[1], spot[2]], own_sem.at[0])
    own_attn.start()
    ffn_own[...] = ffn_block[...]
    waiting, sent = {}, []

    def step(kind, stage, second):
        for part in (0, 1, 2):
            axis, done = ORDERS[part][stage], ORDERS[part][:stage]
            if kind == 0:
                whole, lead, rows, block = attn_all, (core,), ATTN_PARTS[part], attn_block
            else:
                whole, lead, rows, block = ffn_all, (), FFN_PARTS[part], ffn_own
            for copy in waiting.pop((kind, part), ()):
                copy.wait_recv()
            me = spot[axis]
            copies = []
            for way, by in enumerate((1, -1)):
                target = device(shifted(spot, axis, by), core)
                if second:
                    source = goal = view(whole, lead, spot, done, axis, ring(me, -by), rows, half=way)
                else:
                    source = goal = view(whole, lead, spot, done, axis, me, rows)
                    if stage == 0:
                        source = block.at[pl.ds(rows[0], rows[1])]
                copies.append(
                    remote(
                        source, goal,
                        send.at[kind, part, stage, second, way], recv.at[kind, part, stage, second, way], target,
                    )
                )
            waiting[kind, part] = copies
            sent.extend(copies)

    step(0, 0, 0)
    down_copy.wait_recv()
    ffn_own[pl.ds(320, 160)] = ffn_own[pl.ds(320, 160)] + down_in[...]
    own_ffn = pltpu.make_async_copy(ffn_own, ffn_all.at[spot[0], spot[1], spot[2]], own_sem.at[1])
    own_ffn.start()
    step(0, 0, 1)
    step(1, 0, 0)
    own_attn.wait()
    step(0, 1, 0)
    step(1, 0, 1)
    step(0, 1, 1)
    own_ffn.wait()
    step(1, 1, 0)
    step(0, 2, 0)
    step(1, 1, 1)
    step(0, 2, 1)
    step(1, 2, 0)
    pairs = []
    for part, rows in enumerate(ATTN_PARTS):
        for copy in waiting.pop((0, part)):
            copy.wait_recv()
        mine = attn_all.at[core, :, :, :, pl.ds(rows[0], rows[1])]
        pairs.append(remote(mine, mine, pair_send.at[part], pair_recv.at[part], sibling))
    step(1, 2, 1)
    for part in (0, 1, 2):
        for copy in waiting.pop((1, part)):
            copy.wait_recv()
    for copy in pairs:
        copy.wait()
    down_copy.wait_send()
    for copy in sent:
        copy.wait_send()


def gather_weights(attn_block, ffn_block, down_away):
    low = jnp.bfloat16
    return pl.pallas_call(
        gather_kernel,
        out_shape=(
            jax.ShapeDtypeStruct((2, 4, 4, 4, ATTN_ROWS, 128), low),
            jax.ShapeDtypeStruct((4, 4, 4, FFN_ROWS, 128), low),
        ),
        in_specs=[VMEM, VMEM, VMEM],
        out_specs=(ANY, ANY),
        scratch_shapes=[
            pltpu.VMEM((FFN_ROWS, 128), low),
            pltpu.VMEM((160, 128), low),
            pltpu.SemaphoreType.DMA((2, 3, 3, 2, 2)),
            pltpu.SemaphoreType.DMA((2, 3, 3, 2, 2)),
            pltpu.SemaphoreType.DMA((2,)),
            pltpu.SemaphoreType.DMA((4,)),
            pltpu.SemaphoreType.DMA((4,)),
        ],
        compiler_params=pltpu.CompilerParams(collective_id=1, has_side_effects=True, vmem_limit_bytes=16 * MIB),
        name="gather_weights",
    )(attn_block, ffn_block, down_away)


def add_into(target, terms):
    lead = target.shape[:-2]
    if not lead:
        total = target[...].astype(jnp.float32)
        for term in terms:
            total += term[...].astype(jnp.float32)
        target[...] = total.astype(target.dtype)
        return
    inner = lead[1] if len(lead) == 2 else 1

    def body(i, carry):
        at = (lax.div(i, inner), lax.rem(i, inner)) if len(lead) == 2 else (i,)
        total = target[at].astype(jnp.float32)
        for term in terms:
            total += term[at].astype(jnp.float32)
        target[at] = total.astype(target.dtype)
        return carry

    lax.fori_loop(0, lead[0] * inner, body, 0)


def reduce_shapes(rows):
    count = rows[1]
    first = (count // 32) * 16
    return (
        ((2, 4, count), (4, 4, count)),
        ((2, count), (4, count)),
        ((count - first,), (count,)),
    )


def reduce_kernel(attn_terms, ffn_terms, gain_terms, attn_out, ffn_out, down_out, gain_out, *scratch):
    attn, ffn, pair_in, gain_slots = scratch[:4]
    slots = scratch[4 : 4 + 36]
    load_sem, send, recv, pair_send, pair_recv, gain_send, gain_recv = scratch[40:]
    spot, core = place()
    sibling = device(spot, 1 - core)
    load_ffn = pltpu.make_async_copy(ffn_terms, ffn, load_sem.at[0])
    load_ffn.start()
    load_attn = pltpu.make_async_copy(attn_terms.at[core], attn, load_sem.at[1])
    load_attn.start()
    greet(
        [device(shifted(spot, a, by), core) for a in range(3) for by in (1, 2, 3)] + [sibling]
    )
    pair = remote(attn_terms.at[1 - core], pair_in, pair_send.at[0], pair_recv.at[0], sibling)
    waiting, sent = {}, [pair]

    def slot(kind, part, stage, second, way):
        ref = slots[((kind * 3 + part) * 3 + stage) * 2 + second]
        count = (ATTN_PARTS if kind == 0 else FFN_PARTS)[part][1]
        if stage == 2 and second == 0:
            first = (count // 32) * 16
            return ref.at[way, pl.ds(0, first if way == 0 else count - first)]
        return ref.at[way]

    def step(kind, stage, second):
        whole, parts = (attn, ATTN_PARTS) if kind == 0 else (ffn, FFN_PARTS)
        for part in (0, 1, 2):
            rows = parts[part]
            if stage < 3:
                axis, done = ORDERS[part][2 - stage], ORDERS[part][: 2 - stage]
            arrived = waiting.pop((kind, part), ())
            for copy in arrived:
                copy.wait_recv()
            if arrived and not second:
                before, full = ORDERS[part][3 - stage], ORDERS[part][: 3 - stage]
                add_into(
                    view(whole, (), spot, full, before, spot[before], rows),
                    [slot(kind, part, stage - 1, 1, way) for way in (0, 1)],
                )
            if stage == 3:
                goal = attn_out if kind == 0 else ffn_out
                goal[pl.ds(rows[0], rows[1])] = whole[spot[0], spot[1], spot[2], pl.ds(rows[0], rows[1])].astype(jnp.float32)
                continue
            me = spot[axis]
            copies = []
            for way, by in enumerate((1, -1)):
                target = device(shifted(spot, axis, by), core)
                if second:
                    add_into(
                        view(whole, (), spot, done, axis, ring(me, by), rows, half=way),
                        [slot(kind, part, stage, 0, way)],
                    )
                    source = view(whole, (), spot, done, axis, ring(me, by), rows)
                else:
                    source = view(whole, (), spot, done, axis, ring(me, 2), rows, half=way)
                copies.append(
                    remote(
                        source, slot(kind, part, stage, second, way),
                        send.at[kind, part, stage, second, way], recv.at[kind, part, stage, second, way], target,
                    )
                )
            waiting[kind, part] = copies
            sent.extend(copies)

    def gain_start(axis):
        me = spot[axis]
        gain_slots[axis, me] = gain_out[...]
        mine = gain_slots.at[axis, me]
        return [
            remote(mine, mine, gain_send.at[axis, by - 1], gain_recv.at[axis, by - 1], device(shifted(spot, axis, by), core))
            for by in (1, 2, 3)
        ]

    def gain_end(axis, copies):
        for copy in copies:
            copy.wait_recv()
        sent.extend(copies)
        gain_out[...] = (gain_slots[axis, 0] + gain_slots[axis, 1]) + (gain_slots[axis, 2] + gain_slots[axis, 3])

    gain_out[...] = gain_terms[...]
    load_ffn.wait()
    step(1, 0, 0)
    gains = gain_start(0)
    load_attn.wait()
    step(1, 0, 1)
    pair.wait_recv()
    for part in (0, 1, 2):
        rows = ATTN_PARTS[part]

        def add_pair(i, carry):
            at = (lax.div(i, 16), lax.rem(lax.div(i, 4), 4), lax.rem(i, 4), pl.ds(rows[0], rows[1]))
            attn[at] = (attn[at].astype(jnp.float32) + pair_in[at].astype(jnp.float32)).astype(attn.dtype)
            return carry

        lax.fori_loop(0, 64, add_pair, 0)
    step(0, 0, 0)
    gain_end(0, gains)
    gains = gain_start(1)
    step(1, 1, 0)
    step(0, 0, 1)
    step(1, 1, 1)
    gain_end(1, gains)
    gains = gain_start(2)
    step(0, 1, 0)
    step(1, 2, 0)
    step(0, 1, 1)
    step(1, 2, 1)
    gain_end(2, gains)
    gain_slots[3, core] = gain_out[...]
    mine = gain_slots.at[3, core]
    last = remote(mine, mine, pair_send.at[1], pair_recv.at[1], sibling)
    step(0, 2, 0)
    step(1, 3, 0)
    down_copy = remote(ffn_out.at[pl.ds(320, 160)], down_out, pair_send.at[2], pair_recv.at[2], sibling)
    step(0, 2, 1)
    last.wait_recv()
    gain_out[...] = gain_slots[3, 0] + gain_slots[3, 1]
    step(0, 3, 0)
    down_copy.wait_recv()
    sent.extend([last, down_copy])
    for copy in sent:
        copy.wait_send()


def reduce_grads(attn_terms, ffn_terms, gain_terms):
    low = jnp.bfloat16
    slots = []
    for parts in (ATTN_PARTS, FFN_PARTS):
        for rows in parts:
            for stage in reduce_shapes(rows):
                for shape in stage:
                    slots.append(pltpu.VMEM((2,) + shape + (128,), low))
    return pl.pallas_call(
        reduce_kernel,
        out_shape=(
            jax.ShapeDtypeStruct((ATTN_ROWS, 128), jnp.float32),
            jax.ShapeDtypeStruct((FFN_ROWS, 128), jnp.float32),
            jax.ShapeDtypeStruct((160, 128), jnp.float32),
            jax.ShapeDtypeStruct((16, 128), jnp.float32),
        ),
        in_specs=[ANY, ANY, VMEM],
        out_specs=(VMEM,) * 4,
        scratch_shapes=[
            pltpu.VMEM((4, 4, 4, ATTN_ROWS, 128), low),
            pltpu.VMEM((4, 4, 4, FFN_ROWS, 128), low),
            pltpu.VMEM((4, 4, 4, ATTN_ROWS, 128), low),
            pltpu.VMEM((4, 4, 16, 128), jnp.float32),
        ]
        + slots
        + [
            pltpu.SemaphoreType.DMA((2,)),
            pltpu.SemaphoreType.DMA((2, 3, 3, 2, 2)),
            pltpu.SemaphoreType.DMA((2, 3, 3, 2, 2)),
            pltpu.SemaphoreType.DMA((3,)),
            pltpu.SemaphoreType.DMA((3,)),
            pltpu.SemaphoreType.DMA((3, 3)),
            pltpu.SemaphoreType.DMA((3, 3)),
        ],
        compiler_params=pltpu.CompilerParams(collective_id=2, has_side_effects=True, vmem_limit_bytes=48 * MIB),
        name="reduce_grads",
    )(attn_terms, ffn_terms, gain_terms)


def keys_kernel(block, out, own_sem, send, recv, pair_send, pair_recv):
    spot, core = place()
    x, y, z = spot
    half = lax.rem(y, 2)
    sibling = device(spot, 1 - core)
    across = device((x, y + 1 - 2 * half, z), core)
    greet([device(shifted(spot, 0, by), core) for by in (1, -1)] + [across, sibling])
    mine = out.at[half, x, core]
    own = pltpu.make_async_copy(block, mine, own_sem)
    own.start()
    sent, pairs = [], []

    def pass_on(ref):
        pairs.append(remote(ref, ref, pair_send.at[len(pairs)], pair_recv.at[len(pairs)], sibling))

    over = remote(block, mine, send.at[0], recv.at[0], across)
    pairs.append(remote(block, mine, pair_send.at[0], pair_recv.at[0], sibling))
    first = [
        remote(block, mine, send.at[1 + way], recv.at[1 + way], device(shifted(spot, 0, by), core))
        for way, by in enumerate((1, -1))
    ]
    over.wait_recv()
    other = out.at[1 - half, x, core]
    second = [
        remote(other, other, send.at[3 + way], recv.at[3 + way], device(shifted(spot, 0, by), core))
        for way, by in enumerate((1, -1))
    ]
    pass_on(other)
    last = []
    for way, by in enumerate((1, -1)):
        first[way].wait_recv()
        if way == 0:
            ref = out.at[half, ring(x, -by), core]
            last.append(remote(ref, ref, send.at[5], recv.at[5], device(shifted(spot, 0, by), core)))
        pass_on(out.at[half, ring(x, -by), core])
    for way, by in enumerate((1, -1)):
        second[way].wait_recv()
        if way == 1:
            ref = out.at[1 - half, ring(x, -by), core]
            last.append(remote(ref, ref, send.at[6], recv.at[6], device(shifted(spot, 0, by), core)))
        pass_on(out.at[1 - half, ring(x, -by), core])
    last[0].wait_recv()
    pass_on(out.at[half, ring(x, 2), core])
    last[1].wait_recv()
    pass_on(out.at[1 - half, ring(x, 2), core])
    own.wait()
    for copy in pairs:
        copy.wait()
    for copy in [over] + first + second + last:
        copy.wait_send()


def gather_keys(block):
    return pl.pallas_call(
        keys_kernel,
        out_shape=jax.ShapeDtypeStruct((2, 4, 2, TOK, 2 * KVW), jnp.bfloat16),
        in_specs=[VMEM],
        out_specs=ANY,
        scratch_shapes=[
            pltpu.SemaphoreType.DMA,
            pltpu.SemaphoreType.DMA((7,)),
            pltpu.SemaphoreType.DMA((7,)),
            pltpu.SemaphoreType.DMA((8,)),
            pltpu.SemaphoreType.DMA((8,)),
        ],
        compiler_params=pltpu.CompilerParams(collective_id=3, has_side_effects=True),
        name="gather_keys",
    )(block)


def key_grads_kernel(terms, total, mine, pair_in, far_in, near_in, across_in, send, recv, load_sem):
    spot, core = place()
    x, y, z = spot
    half = lax.rem(y, 2)
    sibling = device(spot, 1 - core)
    across = device((x, y + 1 - 2 * half, z), core)
    loads = []
    for h in (0, 1):
        for i in range(4):
            load = pltpu.make_async_copy(terms.at[h, i, core], mine.at[h, i], load_sem.at[h, i])
            load.start()
            loads.append(load)
    greet([device(shifted(spot, 0, by), core) for by in (1, -1)] + [across, sibling])
    pairs = []
    for k, by in enumerate((2, 1, 3, 0)):
        for h in (0, 1):
            at = ring(x, by)
            pairs.append(
                remote(terms.at[h, at, 1 - core], pair_in.at[h, at], send.at[2 * k + h], recv.at[2 * k + h], sibling)
            )
    for load in loads:
        load.wait()

    def add(goal, *sources):
        sum_ = goal[...].astype(jnp.float32)
        for source in sources:
            sum_ += source[...].astype(jnp.float32)
        goal[...] = sum_.astype(goal.dtype)

    for h in (0, 1):
        pairs[h].wait_recv()
        add(mine.at[h, ring(x, 2)], pair_in.at[h, ring(x, 2)])
    far = [
        remote(mine.at[way, ring(x, 2)], far_in.at[way], send.at[8 + way], recv.at[8 + way], device(shifted(spot, 0, by), core))
        for way, by in enumerate((1, -1))
    ]
    for pair in pairs[2:]:
        pair.wait_recv()
    for by in (1, 3, 0):
        for h in (0, 1):
            add(mine.at[h, ring(x, by)], pair_in.at[h, ring(x, by)])
    near = []
    for way, by in enumerate((1, -1)):
        far[way].wait_recv()
        add(mine.at[way, ring(x, by)], far_in.at[way])
        near.append(
            remote(
                mine.at[:, ring(x, by)], near_in.at[way], send.at[10 + way], recv.at[10 + way],
                device(shifted(spot, 0, by), core),
            )
        )
    for copy in near:
        copy.wait_recv()
    add(mine.at[1 - half, x], near_in.at[0, 1 - half], near_in.at[1, 1 - half])
    last = remote(mine.at[1 - half, x], across_in, send.at[12], recv.at[12], across)
    add(mine.at[half, x], near_in.at[0, half], near_in.at[1, half])
    last.wait_recv()
    total[...] = mine[half, x].astype(jnp.float32) + across_in[...].astype(jnp.float32)
    for copy in pairs + far + near + [last]:
        copy.wait_send()


def reduce_keys(terms):
    low = jnp.bfloat16
    wide = 2 * KVW
    return pl.pallas_call(
        key_grads_kernel,
        out_shape=jax.ShapeDtypeStruct((TOK, wide), jnp.float32),
        in_specs=[ANY],
        out_specs=VMEM,
        scratch_shapes=[
            pltpu.VMEM((2, 4, TOK, wide), low),
            pltpu.VMEM((2, 4, TOK, wide), low),
            pltpu.VMEM((2, TOK, wide), low),
            pltpu.VMEM((2, 2, TOK, wide), low),
            pltpu.VMEM((TOK, wide), low),
            pltpu.SemaphoreType.DMA((13,)),
            pltpu.SemaphoreType.DMA((13,)),
            pltpu.SemaphoreType.DMA((2, 4)),
        ],
        compiler_params=pltpu.CompilerParams(collective_id=4, has_side_effects=True, vmem_limit_bytes=24 * MIB),
        name="reduce_keys",
    )(terms)


def dot(left, right, left_dim=1, right_dim=0):
    return lax.dot_general(left, right, (((left_dim,), (right_dim,)), ((), ())), preferred_element_type=jnp.float32)


def ffn_kernel(
    residual, gain, cot, weights,
    layer_out, d_residual, gain_term, grads,
    gate_w, up_w, down_w, tokens, cots, out_sum, norm_sum, out_in, norm_in, load_sem, send, recv,
):
    spot, core = place()
    sibling = device(spot, 1 - core)
    for part, goal in enumerate((gate_w, up_w, down_w)):

        def load(i, carry):
            x, y, z = lax.div(i, 16), lax.rem(lax.div(i, 4), 4), lax.rem(i, 4)
            rows = lax.rem(y, 2) * 4 + x
            lanes = lax.div(y, 2) * 4 + z
            if part == 2:
                rows, lanes = lanes, rows
            pltpu.make_async_copy(
                weights.at[x, y, z, pl.ds(160 * part, 160)],
                goal.at[pl.ds(pl.multiple_of(rows * 160, 32), 160), pl.ds(pl.multiple_of(lanes * 128, 128), 128)],
                load_sem.at[part],
            ).start()
            return carry

        lax.fori_loop(0, 64, load, 0)
    greet([sibling])
    cots[pl.ds(0, TOK)] = cot[...]
    cot_copy = remote(cot, cots.at[pl.ds(TOK, TOK)], send.at[0], recv.at[0], sibling)
    res = residual[...]
    scale = lax.rsqrt(jnp.sum(res * res, axis=-1, keepdims=True) * (1.0 / D) + epsilon)
    tokens[pl.ds(0, TOK)] = (res * scale * gain[...]).astype(jnp.bfloat16)
    token_copy = remote(tokens.at[pl.ds(0, TOK)], tokens.at[pl.ds(TOK, TOK)], send.at[1], recv.at[1], sibling)
    out_sum[...] = jnp.zeros_like(out_sum)
    norm_sum[...] = jnp.zeros_like(norm_sum)
    cot_copy.wait_recv()
    token_copy.wait_recv()
    for part, goal in enumerate((gate_w, up_w, down_w)):
        pltpu.make_async_copy(goal, goal, load_sem.at[part]).wait()

    def chunk(j, carry):
        rows = pl.ds(pl.multiple_of(j * 320, 320), 320)
        gate_rows, up_rows, down_rows = gate_w[rows, :], up_w[rows, :], down_w[rows, :]
        both, cot_both = tokens[...], cots[...]
        gate_value = dot(both, gate_rows, 1, 1)
        up_value = dot(both, up_rows, 1, 1)
        d_hidden = dot(cot_both, down_rows, 1, 1)
        sigmoid = 1.0 / (1.0 + jnp.exp(-gate_value))
        silu = gate_value * sigmoid
        hidden = (silu * up_value).astype(jnp.bfloat16)
        d_gate = (d_hidden * up_value * sigmoid * (1.0 + gate_value * (1.0 - sigmoid))).astype(jnp.bfloat16)
        d_up = (d_hidden * silu).astype(jnp.bfloat16)
        out_sum[...] += dot(hidden, down_rows)
        norm_sum[...] += dot(d_gate, gate_rows) + dot(d_up, up_rows)
        for part, (left, right) in enumerate(((d_gate, both), (d_up, both), (hidden, cot_both))):
            term = dot(left, right, 0, 0).astype(jnp.bfloat16)
            for u in range(2):
                for lane in range(8):
                    piece = term[160 * u : 160 * u + 160, 128 * lane : 128 * lane + 128]
                    block = 2 * j + u
                    if part == 2:
                        at = (lane % 4, lax.div(block, 4) * 2 + lane // 4, lax.rem(block, 4))
                    else:
                        at = (lax.rem(block, 4), (lane // 4) * 2 + lax.div(block, 4), lane % 4)
                    grads[at + (pl.ds(160 * part, 160),)] = piece
        return carry

    lax.fori_loop(0, 4, chunk, 0)
    theirs = pl.ds(TOK, TOK)
    norm_copy = remote(norm_sum.at[theirs], norm_in, send.at[2], recv.at[2], sibling)
    out_copy = remote(out_sum.at[theirs], out_in, send.at[3], recv.at[3], sibling)
    norm_copy.wait_recv()
    d_normed = norm_sum[pl.ds(0, TOK)] + norm_in[...]
    gain_term[...] = jnp.sum(d_normed * res * scale, axis=0, keepdims=True)
    u = d_normed * gain[...]
    d_residual[...] = cot[...].astype(jnp.float32) + scale * (
        u - res * scale * scale * (jnp.sum(u * res, axis=-1, keepdims=True) * (1.0 / D))
    )
    out_copy.wait_recv()
    layer_out[...] = (res + out_sum[pl.ds(0, TOK)] + out_in[...]).astype(jnp.bfloat16)
    for copy in (cot_copy, token_copy, norm_copy, out_copy):
        copy.wait_send()


def ffn(residual, gain, cot, weights):
    low = jnp.bfloat16
    return pl.pallas_call(
        ffn_kernel,
        out_shape=(
            jax.ShapeDtypeStruct((TOK, WIDE), low),
            jax.ShapeDtypeStruct((TOK, WIDE), jnp.float32),
            jax.ShapeDtypeStruct((1, WIDE), jnp.float32),
            jax.ShapeDtypeStruct((4, 4, 4, FFN_ROWS, 128), low),
        ),
        in_specs=[VMEM, VMEM, VMEM, ANY],
        out_specs=(VMEM,) * 4,
        scratch_shapes=[pltpu.VMEM((HALF_FF, WIDE), low)] * 3
        + [pltpu.VMEM((2 * TOK, WIDE), low)] * 2
        + [pltpu.VMEM((2 * TOK, WIDE), jnp.float32)] * 2
        + [pltpu.VMEM((TOK, WIDE), jnp.float32)] * 2
        + [
            pltpu.SemaphoreType.DMA((3,)),
            pltpu.SemaphoreType.DMA((4,)),
            pltpu.SemaphoreType.DMA((4,)),
        ],
        compiler_params=pltpu.CompilerParams(collective_id=5, has_side_effects=True, vmem_limit_bytes=48 * MIB),
        name="ffn",
    )(residual, gain, cot, weights)


def spread(array, axis):
    shape = array.shape
    split = array.reshape(shape[:axis] + (shape[axis] // 60, 60) + shape[axis + 1 :])
    pads = [(0, 0)] * split.ndim
    pads[axis + 1] = (0, 4)
    return jnp.pad(split, pads).reshape(shape[:axis] + (shape[axis] // 60 * 64,) + shape[axis + 1 :])


def squeeze(array, axis):
    shape = array.shape
    split = array.reshape(shape[:axis] + (shape[axis] // 64, 64) + shape[axis + 1 :])
    split = lax.slice_in_dim(split, 0, 60, axis=axis + 1)
    return split.reshape(shape[:axis] + (shape[axis] // 64 * 60,) + shape[axis + 1 :])


def layout(offsets, token_index):
    inner = offsets[1:NDOC]
    after = token_index[:, None] >= inner[None, :]
    segment = jnp.sum(after.astype(jnp.int32), axis=1)
    starts = jnp.max(jnp.where(after, inner[None, :], 0), axis=1)
    return (segment, token_index - starts)


def rotary(positions):
    half_dim = HD // 2
    rate_table = 10000.0 ** (-2.0 * jnp.arange(half_dim, dtype=jnp.float32) / HD)
    angles = positions.astype(jnp.float32)[:, None] * rate_table[None, :]
    cosine = jnp.cos(angles)
    sine_table = jnp.sin(angles)
    return (
        jnp.concatenate([cosine, cosine], axis=1),
        jnp.concatenate([sine_table, sine_table], axis=1),
    )


def turn_half(vectors):
    half_dim = HD // 2
    return jnp.concatenate([-vectors[..., half_dim:], vectors[..., :half_dim]], axis=-1)


def rotate(vectors, cosine, sine_table):
    return vectors * cosine[:, None, :] + turn_half(vectors) * sine_table[:, None, :]


def unrotate(vectors, cosine, sine_table):
    return vectors * cosine[:, None, :] - turn_half(vectors) * sine_table[:, None, :]


def pack_weights(query, key, value, proj, gate, up, down, core):
    columns = lambda a: spread(a.T, 1)
    zeros = jnp.zeros((4, 128), jnp.bfloat16)
    attn = jnp.concatenate(
        [columns(query), zeros, columns(proj), zeros, columns(key), columns(value), zeros, zeros], axis=0
    )
    left = jnp.pad(down, ((0, 0), (0, 68)))
    right = jnp.pad(down, ((0, 0), (64, 4)))
    placed = jnp.where(core == 0, left, right)
    keep = jnp.where(core == 0, placed[:160], placed[160:])
    away = jnp.where(core == 0, placed[160:], placed[:160])
    return attn, jnp.concatenate([columns(gate), columns(up), keep], axis=0), away


def per_device(
    inputs, doc_offsets, attn_gain, query_weight, key_weight, value_weight, proj_weight,
    ffn_gain, gate_weight, up_weight, down_weight, cotangent,
):
    low = jnp.bfloat16
    row_count = TOK
    length = row_count * 16
    group_size = HEADS // KVH
    score_scale = HD ** (-0.5)
    _, core = place()
    first_row = lax.axis_index("ctx") * row_count
    last_row = first_row + row_count - 1
    offsets = doc_offsets[0]
    token_index = first_row + jnp.arange(row_count, dtype=jnp.int32)
    segment, positions = layout(offsets, token_index)
    cosine, sine_table = rotary(positions)
    attn_all, ffn_all = gather_weights(
        *pack_weights(query_weight, key_weight, value_weight, proj_weight, gate_weight, up_weight, down_weight, core)
    )
    attn_wide = jnp.transpose(
        attn_all.reshape(2, 4, 2, 2, 4, ATTN_ROWS, 128), (3, 1, 0, 5, 2, 4, 6)
    ).reshape(16, ATTN_ROWS, WIDE)
    query_w = attn_wide[:, :64].reshape(WIDE, WIDE)
    proj_w = attn_wide[:, 64:128].reshape(WIDE, WIDE)
    key_value_w = attn_wide[:, 128:176].reshape(768, WIDE)

    tokens = spread(inputs[0], 1).astype(jnp.float32)
    gain_wide = spread(attn_gain[None], 1)
    ffn_gain_wide = spread(ffn_gain[None], 1)
    cot_low = spread(cotangent[0], 1)
    attn_scale = lax.rsqrt(jnp.sum(tokens * tokens, axis=-1, keepdims=True) * (1.0 / D) + epsilon)
    normed = (tokens * attn_scale * gain_wide).astype(low)
    queries = squeeze(dot(normed, query_w, 1, 1), 1)
    key_value = dot(normed, key_value_w, 1, 1).reshape(row_count, 16, 48)
    keys_flat = key_value[:, :, :20].reshape(row_count, KVW)
    value_rows = key_value[:, :, 20:40].reshape(row_count, KVW).astype(low)
    query_rot = (
        rotate(queries.reshape(row_count, HEADS, HD), cosine, sine_table)
        .astype(low)
        .reshape(row_count, KVH, group_size, HD)
    )
    key_rot = rotate(keys_flat.reshape(row_count, KVH, HD), cosine, sine_table).astype(low).reshape(row_count, KVW)
    gathered = gather_keys(jnp.concatenate([key_rot, value_rows], axis=1)).reshape(length, 2, KVH, HD)
    all_keys, all_values = gathered[:, 0], gathered[:, 1]

    def block_scores(key_block, key_start):
        key_index = key_start + jnp.arange(key_block.shape[0], dtype=jnp.int32)
        key_segment = layout(offsets, key_index)[0]
        allowed = (segment[:, None] == key_segment[None, :]) & (
            key_index[None, :] <= token_index[:, None]
        )
        scores = (
            jnp.einsum("qhgd,khd->hgqk", query_rot, key_block, preferred_element_type=jnp.float32)
            * score_scale
        )
        return jnp.where(allowed[None, None], scores, masked_score)

    def visit(carried, key_block, value_block, key_start):

        def update(current):
            row_top, row_total, weighted = current
            scores = block_scores(key_block, key_start)
            new_top = jnp.maximum(row_top, jnp.max(scores, axis=-1))
            factor = jnp.exp(row_top - new_top)
            raised = jnp.exp(scores - new_top[..., None])
            new_total = row_total * factor + jnp.sum(raised, axis=-1)
            added = jnp.einsum(
                "hgqk,khd->qhgd",
                raised.astype(low),
                value_block,
                preferred_element_type=jnp.float32,
            )
            return (
                new_top,
                new_total,
                weighted * jnp.transpose(factor, (2, 0, 1))[..., None] + added,
            )

        return lax.cond(key_start <= last_row, update, lambda current: current, carried)

    initial = (
        jnp.full((KVH, group_size, row_count), masked_score, jnp.float32),
        jnp.zeros((KVH, group_size, row_count), jnp.float32),
        jnp.zeros((row_count, KVH, group_size, HD), jnp.float32),
    )
    steps_count = length // block_rows

    def scan_step(current, element):
        return (visit(current, element[0], element[1], element[2] * block_rows), None)

    row_top, row_total, weighted = lax.scan(
        scan_step,
        initial,
        (
            all_keys.reshape(steps_count, block_rows, KVH, HD),
            all_values.reshape(steps_count, block_rows, KVH, HD),
            jnp.arange(steps_count, dtype=jnp.int32),
        ),
    )[0]
    log_total = row_top + jnp.log(row_total)
    mixed = weighted / jnp.transpose(row_total, (2, 0, 1))[..., None]
    attn_out = spread(mixed.astype(low).reshape(row_count, QW), 1)
    residual = tokens + dot(attn_out, proj_w, 1, 1)

    layer_out, d_residual, ffn_gain_term, ffn_terms = ffn(residual, ffn_gain_wide, cot_low, ffn_all)

    d_branch = d_residual.astype(low)
    d_mixed = squeeze(dot(d_branch, proj_w).astype(low), 1).reshape(row_count, KVH, group_size, HD)
    row_delta = jnp.transpose(jnp.sum(d_mixed.astype(jnp.float32) * mixed, axis=-1), (1, 2, 0))
    empty_block = jnp.zeros((block_rows, KVW), jnp.float32)

    def backward_step(d_query, element):
        key_block, value_block, block_index = element
        key_start = block_index * block_rows

        def contribute(pending):
            shares = jnp.exp(block_scores(key_block, key_start) - log_total[..., None])
            d_shares = jnp.einsum(
                "qhgd,khd->hgqk", d_mixed, value_block, preferred_element_type=jnp.float32
            )
            d_scores = (shares * (d_shares - row_delta[..., None])).astype(low)
            d_query_add = (
                jnp.einsum(
                    "hgqk,khd->qhgd", d_scores, key_block, preferred_element_type=jnp.float32
                )
                * score_scale
            )
            d_key_block = (
                jnp.einsum(
                    "hgqk,qhgd->khd", d_scores, query_rot, preferred_element_type=jnp.float32
                )
                * score_scale
            )
            d_value_block = jnp.einsum(
                "hgqk,qhgd->khd",
                shares.astype(low),
                d_mixed,
                preferred_element_type=jnp.float32,
            )
            return (
                pending + d_query_add,
                d_key_block.reshape(block_rows, KVW),
                d_value_block.reshape(block_rows, KVW),
            )

        def skipped(pending):
            return (pending, empty_block, empty_block)

        d_query, d_key_block, d_value_block = lax.cond(
            key_start <= last_row, contribute, skipped, d_query
        )
        return (d_query, (d_key_block, d_value_block))

    d_query_rot, stacked = lax.scan(
        backward_step,
        jnp.zeros((row_count, KVH, group_size, HD), jnp.float32),
        (
            all_keys.reshape(steps_count, block_rows, KVH, HD),
            all_values.reshape(steps_count, block_rows, KVH, HD),
            jnp.arange(steps_count, dtype=jnp.int32),
        ),
    )
    sums = reduce_keys(
        jnp.concatenate([stacked[0].reshape(length, KVW), stacked[1].reshape(length, KVW)], axis=1)
        .astype(low)
        .reshape(2, 4, 2, row_count, 2 * KVW)
    )
    d_queries = spread(
        unrotate(d_query_rot.reshape(row_count, HEADS, HD), cosine, sine_table).astype(low).reshape(row_count, QW), 1
    )
    d_keys = unrotate(sums[:, :KVW].reshape(row_count, KVH, HD), cosine, sine_table).astype(low)
    d_values = sums[:, KVW:].astype(low)
    d_key_value = jnp.concatenate(
        [d_keys.reshape(row_count, 16, 20), d_values.reshape(row_count, 16, 20), jnp.zeros((row_count, 16, 8), low)],
        axis=2,
    ).reshape(row_count, 768)
    d_normed = dot(d_queries, query_w) + dot(d_key_value, key_value_w)
    attn_gain_term = jnp.sum(d_normed * tokens * attn_scale, axis=0, keepdims=True)
    scaled_attn = d_normed * gain_wide
    d_tokens = d_residual + attn_scale * (
        scaled_attn
        - tokens * attn_scale * attn_scale * (jnp.sum(scaled_attn * tokens, axis=-1, keepdims=True) * (1.0 / D))
    )
    attn_terms = jnp.concatenate(
        [
            dot(d_queries, normed, 0, 0).astype(low).reshape(16, 64, 8, 128),
            dot(d_branch, attn_out, 0, 0).astype(low).reshape(16, 64, 8, 128),
            dot(d_key_value, normed, 0, 0).astype(low).reshape(16, 48, 8, 128),
        ],
        axis=1,
    )
    attn_terms = jnp.transpose(attn_terms.reshape(2, 4, 2, ATTN_ROWS, 2, 4, 128), (2, 1, 4, 0, 5, 3, 6)).reshape(
        2, 4, 4, 4, ATTN_ROWS, 128
    )
    gain_terms = jnp.concatenate([attn_gain_term.reshape(8, 128), ffn_gain_term.reshape(8, 128)], axis=0)
    attn_sum, ffn_sum, down_other, gains = reduce_grads(attn_terms, ffn_terms, gain_terms)
    columns = lambda a: squeeze(a, 1).T
    down_mine = ffn_sum[320:]
    down_both = jnp.concatenate(
        [jnp.where(core == 0, down_mine, down_other), jnp.where(core == 0, down_other, down_mine)], axis=0
    )
    return (
        squeeze(layer_out, 1)[None],
        squeeze(d_tokens.astype(low), 1)[None],
        squeeze(gains[:8].reshape(WIDE), 0),
        columns(attn_sum[:60]),
        columns(attn_sum[128:148]),
        columns(attn_sum[148:168]),
        columns(attn_sum[64:124]),
        squeeze(gains[8:].reshape(WIDE), 0),
        columns(ffn_sum[:160]),
        columns(ffn_sum[160:320]),
        jnp.where(core == 0, down_both[:, :60], down_both[:, 64:124]),
    )


def solution(mesh):
    split = P("fsdp", "ctx")
    rows = P("fsdp", "ctx", None)
    return jax.shard_map(
        per_device,
        mesh=mesh,
        in_specs=(rows, P("fsdp", None), P(), split, split, split, split, P(), split, split, split, rows),
        out_specs=(rows, rows, P(), split, split, split, split, P(), split, split, split),
        check_vma=False,
    )
```

```python
import functools

import jax
import jax.numpy as jnp
from jax import lax
from jax.experimental import pallas as pl
from jax.experimental.pallas import tpu as pltpu
from jax.sharding import PartitionSpec as P

D = 960
HEADS = 15
KVH = 5
HD = 64
NDOC = 4
KVW = 320
WIDE = 1024
TOK = 128

GROUP = HEADS // KVH
STACK = GROUP * TOK
WIDE_KV = 2 * KVW

epsilon = 1e-05
masked_score = -1e30

MESH = pl.DeviceIdType.MESH
ANY = pl.BlockSpec(memory_space=pl.ANY)
VMEM = pl.BlockSpec(memory_space=pltpu.VMEM)
MIB = 1024 * 1024

ATTN_PARTS = ((0, 64), (64, 64), (128, 48))
ATTN_ROWS = 176
FFN_PARTS = ((0, 160), (160, 160), (320, 160))
FFN_ROWS = 480
ORDERS = ((0, 1, 2), (1, 2, 0), (2, 0, 1))


def place():
    c = lax.axis_index("ctx")
    f = lax.axis_index("fsdp")
    x = lax.rem(lax.div(c, 2), 4)
    y = lax.div(f, 4) * 2 + lax.div(c, 8)
    return (x, y, lax.rem(f, 4)), lax.rem(c, 2)


def device(spot, core):
    x, y, z = spot
    return ((lax.rem(y, 2) * 4 + x) * 2 + core, lax.div(y, 2) * 4 + z)


def ring(value, by):
    return lax.rem(value + by + 4, 4)


def shifted(spot, axis, by):
    return tuple(ring(v, by) if i == axis else v for i, v in enumerate(spot))


def greet(devices):
    barrier = pltpu.get_barrier_semaphore()
    for target in devices:
        pl.semaphore_signal(barrier, inc=1, device_id=target, device_id_type=MESH)
    pl.semaphore_wait(barrier, len(devices))


def remote(src, dst, send, recv, target):
    copy = pltpu.make_async_remote_copy(
        src_ref=src, dst_ref=dst, send_sem=send, recv_sem=recv, device_id=target, device_id_type=MESH
    )
    copy.start()
    return copy


def view(ref, lead, spot, done, axis, position, rows, half=None):
    index = []
    cut = min(done) if (half is not None and done) else None
    for a in range(3):
        if a == cut:
            index.append(pl.ds(2 * half, 2))
        elif a in done:
            index.append(pl.ds(0, 4))
        elif a == axis:
            index.append(position)
        else:
            index.append(spot[a])
    low, count = rows
    if half is not None and not done:
        first = (count // 32) * 16
        low, count = (low, first) if half == 0 else (low + first, count - first)
    return ref.at[tuple(lead) + tuple(index) + (pl.ds(low, count),)]


def add_into(target, terms):
    lead = target.shape[:-2]
    if not lead:
        total = target[...].astype(jnp.float32)
        for term in terms:
            total += term[...].astype(jnp.float32)
        target[...] = total.astype(target.dtype)
        return
    inner = lead[1] if len(lead) == 2 else 1

    def body(i, carry):
        at = (lax.div(i, inner), lax.rem(i, inner)) if len(lead) == 2 else (i,)
        total = target[at].astype(jnp.float32)
        for term in terms:
            total += term[at].astype(jnp.float32)
        target[at] = total.astype(target.dtype)
        return carry

    lax.fori_loop(0, lead[0] * inner, body, 0)


def reduce_shapes(rows):
    count = rows[1]
    first = (count // 32) * 16
    return (
        ((2, 4, count), (4, 4, count)),
        ((2, count), (4, count)),
        ((count - first,), (count,)),
    )


def dot(left, right, left_dim=1, right_dim=0):
    return lax.dot_general(left, right, (((left_dim,), (right_dim,)), ((), ())), preferred_element_type=jnp.float32)


def layer_kernel(
    inputs, doc_offsets, attn_gain_in, ffn_gain_in, query_weight, key_weight, value_weight, proj_weight, gate_weight, up_weight, down_weight, cotangent,
    layer_out, input_grad, query_grad, key_grad, value_grad, proj_grad, gate_grad, up_grad, down_grad, gain_sums,
    attn_w, ffn_w, attn_block, ffn_own, down_away, down_in, pads, wide_in, gain_rows, cosine, sine, segments,
    attn_out, ffn_out, down_out, gain_out,
    normed, normed_t, rows_f32, query_t, query, key_own, keys, scores, mixed, mixed_t, residual,
    tokens, cots, out_sum, norm_sum, out_in, norm_in,
    d_mixed_t, d_mixed, d_query, d_query_t, key_terms, key_pair, key_far, key_near, key_across, d_key_t,
    attn_g, pair_in, gain_slots,
    *scratch,
):
    slots = scratch[:36]
    (
        send, recv, own_sem, down_sem, pair_send, pair_recv,
        key_own_sem, key_send, key_recv, kpair_send, kpair_recv,
        ffn_send, ffn_recv, kg_send, kg_recv, r_send, r_recv, gain_send, gain_recv, last_send, last_recv,
    ) = scratch[36:]
    low = jnp.bfloat16
    spot, core = place()
    x, y, z = spot
    half = lax.rem(y, 2)
    sibling = device(spot, 1 - core)
    across = device((x, y + 1 - 2 * half, z), core)
    chunks = half * 2 + lax.div(x, 2) + 1
    sent = []

    def hot(rows, columns, shift):
        row = lax.broadcasted_iota(jnp.int32, (rows, columns), 0)
        column = lax.broadcasted_iota(jnp.int32, (rows, columns), 1)
        return column == row + shift(row)

    by_sixty = lambda row: lax.shift_right_logical(row * 1093, 16) * 4
    columns_of = hot(120, 128, by_sixty).astype(low)
    zeros = lambda rows: jnp.zeros((rows, 128), jnp.float32)
    turn = lambda ref: dot(ref[...], columns_of)
    attn_block[pl.ds(128, 48)] = jnp.concatenate([turn(key_weight), turn(value_weight), zeros(8)], axis=0).astype(low)
    attn_block[pl.ds(0, 64)] = jnp.concatenate([turn(query_weight), zeros(4)], axis=0).astype(low)
    attn_block[pl.ds(64, 64)] = jnp.concatenate([turn(proj_weight), zeros(4)], axis=0).astype(low)
    ffn_own[pl.ds(0, 160)] = turn(gate_weight).astype(low)
    ffn_own[pl.ds(160, 160)] = turn(up_weight).astype(low)
    placed = hot(60, 128, lambda row: 64 * core).astype(low)
    down_both = dot(down_weight[...], placed, 0, 0)
    down_away[...] = jnp.where(core == 0, down_both[160:], down_both[:160]).astype(low)
    ffn_own[pl.ds(320, 160)] = jnp.where(core == 0, down_both[:160], down_both[160:]).astype(low)

    greet([device(shifted(spot, a, by), core) for a in range(3) for by in (1, 2, 3)] + [sibling])
    down_copy = remote(down_away, down_in, down_sem.at[0], down_sem.at[1], sibling)
    sent.append(down_copy)
    own_attn = pltpu.make_async_copy(attn_block, attn_w.at[core, x, y, z], own_sem.at[0])
    own_attn.start()
    waiting, gathered, paired = {}, [], {}

    def pass_on(part, number, position):
        order = ORDERS[part]
        piece = view(attn_w, (core,), spot, order[:2], order[2], position, ATTN_PARTS[part])
        paired[part, number] = remote(piece, piece, pair_send.at[part, number], pair_recv.at[part, number], sibling)

    def direct(kind, stage):
        return stage < 2 - kind

    def gather_step(kind, stage, second, some=(2, 0, 1)):
        for part in some:
            axis, done = ORDERS[part][stage], ORDERS[part][:stage]
            if kind == 0:
                whole, lead, rows, block = attn_w, (core,), ATTN_PARTS[part], attn_block
            else:
                whole, lead, rows, block = ffn_w, (), FFN_PARTS[part], ffn_own
            for copy in waiting.pop((kind, part), ()):
                copy.wait_recv()
            me = spot[axis]
            copies = []
            for way, by in enumerate((1, -1, 2) if direct(kind, stage) else (1, -1)):
                target = device(shifted(spot, axis, by), core)
                if second:
                    source = goal = view(whole, lead, spot, done, axis, ring(me, -by), rows, half=way)
                else:
                    source = goal = view(whole, lead, spot, done, axis, me, rows)
                    if stage == 0:
                        source = block.at[pl.ds(rows[0], rows[1])]
                copies.append(
                    remote(
                        source, goal,
                        send.at[kind, part, stage, second, way], recv.at[kind, part, stage, second, way], target,
                    )
                )
            waiting[kind, part] = copies
            (sent if kind == 0 else gathered).extend(copies)
            if kind == 0 and stage == 2:
                if second:
                    pass_on(part, 1, ring(me, 1))
                    pass_on(part, 2, ring(me, -1))
                else:
                    pass_on(part, 0, me)

    def settle(kind, part):
        for copy in waiting.pop((kind, part), ()):
            copy.wait_recv()

    gather_step(0, 0, 0)

    def fill_pads(i, carry):
        start = pl.multiple_of(i * 160, 160)
        pads[pl.ds(start, 160)] = hot(160, WIDE, lambda row: start + by_sixty(row + start)).astype(low)
        return carry

    lax.fori_loop(0, 6, fill_pads, 0)
    wide_in[...] = dot(inputs[...], pads[...], 0, 0)
    cots[pl.ds(0, TOK)] = dot(cotangent[...], pads[...], 0, 0).astype(low)
    cot_copy = remote(cots.at[pl.ds(0, TOK)], cots.at[pl.ds(TOK, TOK)], ffn_send.at[0], ffn_recv.at[0], sibling)

    def exact(array, places, dim):
        total = jnp.zeros((), jnp.float32)
        for _ in range(3):
            piece = array.astype(low)
            array = array - piece.astype(jnp.float32)
            total = total + dot(piece, places, 1, dim)
        return total

    gain_rows[...] = exact(
        jnp.concatenate([attn_gain_in[...], ffn_gain_in[...], jnp.zeros((6, D), jnp.float32)], axis=0), pads[...], 0
    )
    attn_gain, ffn_gain = gain_rows[0:1, :], gain_rows[1:2, :]
    down_copy.wait_recv()
    ffn_own[pl.ds(320, 160)] = ffn_own[pl.ds(320, 160)] + down_in[...]
    own_ffn = pltpu.make_async_copy(ffn_own, ffn_w.at[x, y, z], own_sem.at[1])
    own_ffn.start()
    own_attn.wait()
    gather_step(0, 1, 0)
    gather_step(1, 0, 0)
    tok = wide_in[...]
    attn_scale = lax.rsqrt(jnp.sum(tok * tok, axis=-1, keepdims=True) * (1.0 / D) + epsilon)
    wide_normed = tok * attn_scale * attn_gain
    normed[...] = wide_normed.astype(low)
    normed_t[...] = wide_normed.T.astype(low)
    own_ffn.wait()
    gather_step(0, 2, 0)

    first_row = (half * 8 + x * 2 + core) * TOK

    def document(index):
        number, start = jnp.zeros_like(index), jnp.zeros_like(index)
        for i in range(1, NDOC):
            after = index >= doc_offsets[0, i]
            number += jnp.where(after, 1, 0)
            start = jnp.where(after, doc_offsets[0, i], start)
        return number, start

    table_token = first_row + lax.broadcasted_iota(jnp.int32, (HD // 2, TOK), 1)
    row = lax.broadcasted_iota(jnp.int32, (HD // 2, TOK), 0)
    rates = jnp.zeros((HD // 2, TOK), jnp.float32)
    for i in range(HD // 2):
        rates = jnp.where(row == i, 10000.0 ** (-2.0 * i / HD), rates)
    angles = (table_token - document(table_token)[1]).astype(jnp.float32) * rates
    cosine[...] = jnp.cos(angles)
    sine[...] = jnp.sin(angles)
    row = lax.broadcasted_iota(jnp.int32, (16, 512), 0)
    for j in range(4):
        number = document(512 * j + lax.broadcasted_iota(jnp.int32, (16, 512), 1))[0]
        segments[j] = jnp.where(number == row, 1.0, 0.0).astype(low)
    row = lax.broadcasted_iota(jnp.int32, (16, STACK), 0)
    own_token = first_row + jnp.bitwise_and(lax.broadcasted_iota(jnp.int32, (16, STACK), 1), TOK - 1)
    apart = jnp.where((document(own_token)[0] != row) & (row < NDOC), masked_score, 0.0)
    last_key = first_row + jnp.bitwise_and(lax.broadcasted_iota(jnp.int32, (STACK, 512), 0), TOK - 1)

    gather_step(0, 2, 1)
    gather_step(1, 1, 0)
    for part in (2, 0, 1):
        settle(0, part)
        pass_on(part, 3, ring(spot[ORDERS[part][2]], 2))
    sent.extend(paired.values())

    def settle_pairs(part):
        for number in range(4):
            paired[part, number].wait_recv()

    def weight_rows(where, rows):
        y_lo, p = where
        return jnp.concatenate(
            [
                jnp.concatenate([attn_w[p, i, 2 * (f // 4) + y_lo, f % 4, rows] for f in range(8)], axis=1)
                for i in range(4)
            ],
            axis=0,
        )

    groups = [(y_lo, p) for y_lo in (0, 1) for p in (0, 1)]

    def shard(where, i):
        return (where[0] * 4 + i) * 2 + where[1]

    def turned(v1, v2, back):
        c, s = cosine[...], (-sine[...] if back else sine[...])
        return v1 * c - v2 * s, v2 * c + v1 * s

    settle_pairs(2)
    for where in groups:
        term = dot(weight_rows(where, pl.ds(128, 48)), normed_t[...])
        for i in range(4):
            c = shard(where, i)
            rows_f32[pl.ds(20 * c, 20)] = term[48 * i : 48 * i + 20]
            rows_f32[pl.ds(KVW + 20 * c, 20)] = term[48 * i + 20 : 48 * i + 40]
    for h in range(KVH):
        v1, v2 = turned(rows_f32[pl.ds(64 * h, 32)], rows_f32[pl.ds(64 * h + 32, 32)], False)
        key_own[pl.ds(64 * h, 32)] = v1.astype(low)
        key_own[pl.ds(64 * h + 32, 32)] = v2.astype(low)
    key_own[pl.ds(KVW, KVW)] = rows_f32[pl.ds(KVW, KVW)].astype(low)

    mine = keys.at[half, x, core]
    own_keys = pltpu.make_async_copy(key_own, mine, key_own_sem)
    own_keys.start()
    kpairs = []

    def pass_keys(ref):
        kpairs.append(remote(ref, ref, kpair_send.at[len(kpairs)], kpair_recv.at[len(kpairs)], sibling))

    def key_copy(source, goal, number, target):
        return remote(source, goal, key_send.at[number], key_recv.at[number], target)

    neighbours = [device(shifted(spot, 0, by), core) for by in (1, -1)]
    over = key_copy(key_own, mine, 0, across)
    first = [key_copy(key_own, mine, 1 + way, neighbours[way]) for way in (0, 1)]
    kpairs.append(remote(key_own, mine, kpair_send.at[0], kpair_recv.at[0], sibling))

    gather_step(1, 1, 1)
    settle_pairs(0)
    for where in groups:
        term = dot(weight_rows(where, pl.ds(0, 64)), normed_t[...])
        for i in range(4):
            rows_f32[pl.ds(60 * shard(where, i), 60)] = term[64 * i : 64 * i + 60]

    over.wait_recv()
    other = keys.at[1 - half, x, core]
    second = [key_copy(other, other, 3 + way, neighbours[way]) for way in (0, 1)]
    pass_keys(other)

    def heads(h, carry):
        pieces = []
        for g in range(GROUP):
            at = pl.multiple_of((h * GROUP + g) * HD, HD)
            v1, v2 = turned(rows_f32[pl.ds(at, 32)], rows_f32[pl.ds(pl.multiple_of(at + 32, 32), 32)], False)
            pieces.append(jnp.concatenate([v1, v2], axis=0) * (HD ** -0.5))
        wide = jnp.concatenate(pieces, axis=1)
        query_t[h] = wide.astype(low)
        query[h] = jnp.concatenate([wide, apart], axis=0).T.astype(low)
        return carry

    lax.fori_loop(0, KVH, heads, 0)
    gather_step(1, 2, 0, (0,))

    last = []
    for way, by in enumerate((1, -1)):
        first[way].wait_recv()
        ref = keys.at[half, ring(x, -by), core]
        if way == 0:
            last.append(key_copy(ref, ref, 5, neighbours[0]))
        pass_keys(ref)
    for way, by in enumerate((1, -1)):
        second[way].wait_recv()
        ref = keys.at[1 - half, ring(x, -by), core]
        if way == 1:
            last.append(key_copy(ref, ref, 6, neighbours[1]))
        pass_keys(ref)
    gather_step(1, 2, 0, (1, 2))
    for h in (0, 1):
        last[h].wait_recv()
        pass_keys(keys.at[(half, 1 - half)[h], ring(x, 2), core])
    own_keys.wait()
    for copy in kpairs:
        copy.wait_recv()
    sent.extend([over] + first + second + last + kpairs)

    def key_chunk(j, at):
        rows = pl.ds(pl.multiple_of(at, HD), HD)
        y_lo, i = lax.div(j, 2), 2 * lax.rem(j, 2)
        return jnp.concatenate([keys[y_lo, i + n // 2, n % 2, rows, :] for n in range(4)], axis=1)

    def block_scores(h, j, newest):
        block = dot(query[h], jnp.concatenate([key_chunk(j, h * HD), segments[j]], axis=0))
        if newest:
            index = j * 512 + lax.broadcasted_iota(jnp.int32, (STACK, 512), 1)
            block = jnp.where(index <= last_key, block, masked_score)
        return block

    def quarters(block, joined):
        return joined(
            joined(block[:, :128], block[:, 128:256]), joined(block[:, 256:384], block[:, 384:])
        )

    def forward_head(h, carry):
        def tops(newest, j, top):
            block = block_scores(h, j, newest)
            scores[j] = block
            return jnp.maximum(top, quarters(block, jnp.maximum))

        top = tops(True, chunks - 1, jnp.full((STACK, 128), masked_score, jnp.float32))
        top = lax.fori_loop(0, chunks - 1, functools.partial(tops, False), top)
        top = jnp.max(top, axis=1, keepdims=True)
        mixed[h, :, :HD] = jnp.zeros((STACK, HD), jnp.float32)

        def weigh(j, total):
            raised = jnp.exp(scores[j] - top)
            mixed[h, :, :HD] += dot(raised.astype(low), key_chunk(j, KVW + h * HD), 1, 1)
            return total + quarters(raised, jnp.add)

        total = lax.fori_loop(0, chunks, weigh, jnp.zeros((STACK, 128), jnp.float32))
        total = jnp.sum(total, axis=1, keepdims=True)
        mixed[h, :, HD : HD + 1] = top + jnp.log(total)
        out = mixed[h, :, :HD] / total
        mixed[h, :, :HD] = out
        out_t = out.T
        for g in range(GROUP):
            rows_f32[pl.ds(pl.multiple_of((h * GROUP + g) * HD, HD), HD)] = out_t[:, 128 * g : 128 * g + 128]
        return carry

    lax.fori_loop(0, 3, forward_head, 0)
    gather_step(1, 2, 1)
    lax.fori_loop(3, 5, forward_head, 0)

    def widen(goal):
        for c in range(16):
            piece = jnp.concatenate([rows_f32[pl.ds(60 * c, 60)], jnp.zeros((4, TOK), jnp.float32)], axis=0)
            goal[pl.ds(64 * c, 64)] = piece.astype(low)

    widen(mixed_t)
    settle_pairs(1)
    for where in groups:
        term = dot(weight_rows(where, pl.ds(64, 64)), mixed_t[...])
        for i in range(4):
            rows_f32[pl.ds(64 * shard(where, i), 64)] = term[64 * i : 64 * i + 64]
    residual[...] = wide_in[...] + rows_f32[...].T

    res = residual[...]
    ffn_scale = lax.rsqrt(jnp.sum(res * res, axis=-1, keepdims=True) * (1.0 / D) + epsilon)
    tokens[pl.ds(0, TOK)] = (res * ffn_scale * ffn_gain).astype(low)
    token_copy = remote(tokens.at[pl.ds(0, TOK)], tokens.at[pl.ds(TOK, TOK)], ffn_send.at[1], ffn_recv.at[1], sibling)
    out_sum[...] = jnp.zeros_like(out_sum)
    norm_sum[...] = jnp.zeros_like(norm_sum)
    cot_copy.wait_recv()
    for part in (0, 1, 2):
        settle(1, part)
    for copy in gathered:
        copy.wait_send()
    token_copy.wait_recv()

    def ffn_at(part, block, lane):
        high, slow = lax.div(block, 4), lax.rem(block, 4)
        if part == 2:
            return (lane % 4, high * 2 + lane // 4, slow, pl.ds(320, 160))
        return (slow, (lane // 4) * 2 + high, lane % 4, pl.ds(160 * part, 160))

    def ffn_chunk(j, carry):
        gate_rows, up_rows, down_rows = [
            jnp.concatenate(
                [
                    jnp.concatenate([ffn_w[ffn_at(part, 2 * j + u, lane)] for lane in range(8)], axis=1)
                    for u in (0, 1)
                ],
                axis=0,
            )
            for part in (0, 1, 2)
        ]
        both, cot_both = tokens[...], cots[...]
        gate_value = dot(both, gate_rows, 1, 1)
        up_value = dot(both, up_rows, 1, 1)
        d_hidden = dot(cot_both, down_rows, 1, 1)
        sigmoid = 1.0 / (1.0 + jnp.exp(-gate_value))
        silu = gate_value * sigmoid
        hidden = (silu * up_value).astype(low)
        d_gate = (d_hidden * up_value * sigmoid * (1.0 + gate_value * (1.0 - sigmoid))).astype(low)
        d_up = (d_hidden * silu).astype(low)
        out_sum[...] += dot(hidden, down_rows)
        norm_sum[...] += dot(d_gate, gate_rows) + dot(d_up, up_rows)
        for part, (left, right) in enumerate(((d_gate, both), (d_up, both), (hidden, cot_both))):
            term = dot(left, right, 0, 0).astype(low)
            for u in (0, 1):
                for lane in range(8):
                    ffn_w[ffn_at(part, 2 * j + u, lane)] = term[160 * u : 160 * u + 160, 128 * lane : 128 * lane + 128]
        return carry

    lax.fori_loop(0, 4, ffn_chunk, 0)
    theirs = pl.ds(TOK, TOK)
    norm_copy = remote(norm_sum.at[theirs], norm_in, ffn_send.at[2], ffn_recv.at[2], sibling)
    out_copy = remote(out_sum.at[theirs], out_in, ffn_send.at[3], ffn_recv.at[3], sibling)
    sent.extend([cot_copy, token_copy, norm_copy, out_copy])

    def slot(kind, part, stage, second, way):
        ref = slots[((kind * 3 + part) * 3 + stage) * 2 + second]
        return ref.at[way]

    def reduce_step(kind, stage, second, some=(0, 1, 2)):
        whole, lead, parts = (attn_g, (core,), ATTN_PARTS) if kind == 0 else (ffn_w, (), FFN_PARTS)
        for part in some:
            rows = parts[part]
            if stage < 3:
                axis, done = ORDERS[part][2 - stage], ORDERS[part][: 2 - stage]
            arrived = waiting.pop((2 + kind, part), ())
            for copy in arrived:
                copy.wait_recv()
            if arrived and not second:
                before, full = ORDERS[part][3 - stage], ORDERS[part][: 3 - stage]
                add_into(
                    view(whole, lead, spot, full, before, spot[before], rows),
                    [slot(kind, part, stage - 1, 1, way) for way in range(3 if direct(kind, 3 - stage) else 2)],
                )
            if stage == 3:
                goal = attn_out if kind == 0 else ffn_out
                goal[pl.ds(rows[0], rows[1])] = whole[lead + spot + (pl.ds(rows[0], rows[1]),)].astype(jnp.float32)
                continue
            straight = direct(kind, 2 - stage)
            me = spot[axis]
            copies = []
            for way, by in enumerate((1, -1, 2) if straight else (1, -1)):
                target = device(shifted(spot, axis, by), core)
                if straight:
                    source = view(whole, lead, spot, done, axis, ring(me, by), rows)
                elif second:
                    add_into(
                        view(whole, lead, spot, done, axis, ring(me, by), rows, half=way),
                        [slot(kind, part, stage, 0, way)],
                    )
                    source = view(whole, lead, spot, done, axis, ring(me, by), rows)
                else:
                    source = view(whole, lead, spot, done, axis, ring(me, 2), rows, half=way)
                copies.append(
                    remote(
                        source, slot(kind, part, stage, 1 if straight else second, way),
                        r_send.at[kind, part, stage, second, way], r_recv.at[kind, part, stage, second, way], target,
                    )
                )
            waiting[2 + kind, part] = copies
            sent.extend(copies)

    reduce_step(1, 0, 0)
    norm_copy.wait_recv()
    d_normed = norm_sum[pl.ds(0, TOK)] + norm_in[...]
    res = residual[...]
    ffn_scale = lax.rsqrt(jnp.sum(res * res, axis=-1, keepdims=True) * (1.0 / D) + epsilon)
    ffn_gain_term = jnp.sum(d_normed * res * ffn_scale, axis=0, keepdims=True)
    gain_out[...] = exact(jnp.concatenate([jnp.zeros_like(ffn_gain_term), ffn_gain_term, jnp.zeros((6, WIDE), jnp.float32)], axis=0), pads[...], 1)
    scaled = d_normed * ffn_gain
    d_residual = cots[pl.ds(0, TOK)].astype(jnp.float32) + ffn_scale * (
        scaled - res * ffn_scale * ffn_scale * (jnp.sum(scaled * res, axis=-1, keepdims=True) * (1.0 / D))
    )
    out_copy.wait_recv()
    layer_out[...] = dot(
        pads[...], (res + out_sum[pl.ds(0, TOK)] + out_in[...]).astype(low), 1, 1
    ).astype(low)
    residual[...] = d_residual
    d_branch = d_residual.astype(low)
    d_branch_t = d_residual.T.astype(low)

    norm_sum[pl.ds(0, TOK)] = jnp.zeros((TOK, WIDE), jnp.float32)
    for where in groups:
        picked = jnp.concatenate(
            [d_branch[:, 64 * shard(where, i) : 64 * shard(where, i) + 64] for i in range(4)], axis=1
        )
        norm_sum[pl.ds(0, TOK)] += dot(picked, weight_rows(where, pl.ds(64, 64)))
    d_wide = norm_sum[pl.ds(0, TOK)].T
    for c in range(16):
        rows_f32[pl.ds(60 * c, 60)] = d_wide[64 * c : 64 * c + 60]

    def attn_grad(left_t, right, offset, count, width):
        for where in groups:
            term = dot(
                jnp.concatenate([left_t[width * shard(where, i) : width * shard(where, i) + width] for i in range(4)], axis=0),
                right,
            ).astype(low)
            y_lo, p = where
            for i in range(4):
                for f in range(8):
                    attn_g[p, i, 2 * (f // 4) + y_lo, f % 4, pl.ds(offset, count)] = term[
                        width * i : width * i + count, 128 * f : 128 * f + 128
                    ]

    gpairs = []

    def share(part):
        rows = pl.ds(*ATTN_PARTS[part])
        gpairs.append(
            remote(
                attn_g.at[1 - core, :, :, :, rows], pair_in.at[:, :, :, rows], last_send.at[part], last_recv.at[part], sibling
            )
        )

    def shared(part):
        rows = pl.ds(*ATTN_PARTS[part])
        gpairs[0].wait_recv()
        sent.append(gpairs.pop(0))

        def body(i, carry):
            at = (lax.div(i, 16), lax.rem(lax.div(i, 4), 4), lax.rem(i, 4), rows)
            goal = (core,) + at
            attn_g[goal] = (attn_g[goal].astype(jnp.float32) + pair_in[at].astype(jnp.float32)).astype(low)
            return carry

        lax.fori_loop(0, 64, body, 0)

    def d_heads(h, carry):
        pieces = [rows_f32[pl.ds(pl.multiple_of((h * GROUP + g) * HD, HD), HD)] for g in range(GROUP)]
        wide = jnp.concatenate(pieces, axis=1)
        d_mixed_t[h] = wide.astype(low)
        d_mixed[h] = wide.T.astype(low)
        return carry

    lax.fori_loop(0, KVH, d_heads, 0)
    mixed_rows = mixed_t[...].astype(jnp.float32).T.astype(low)
    attn_grad(d_branch_t, mixed_rows, 64, 64, 64)
    share(1)
    reduce_step(1, 0, 1)

    def clear(j, carry):
        key_terms[lax.div(j, 4), lax.rem(j, 4)] = jnp.zeros((2, WIDE_KV, TOK), low)
        return carry

    lax.fori_loop(2 * chunks, 8, clear, 0)

    def backward_head(h, carry):
        delta = jnp.sum(d_mixed[h].astype(jnp.float32) * mixed[h, :, :HD], axis=1, keepdims=True)
        d_query[...] = jnp.zeros_like(d_query)

        def visit(newest, j, inner):
            shares = jnp.exp(block_scores(h, j, newest) - mixed[h, :, HD : HD + 1])
            d_shares = dot(d_mixed[h], key_chunk(j, KVW + h * HD))
            d_scores = (shares * (d_shares - delta)).astype(low)
            d_query[...] += dot(d_scores, key_chunk(j, h * HD), 1, 1)
            d_key = dot(query_t[h], d_scores).astype(low)
            d_value = dot(d_mixed_t[h], shares.astype(low)).astype(low)
            y_lo, i = lax.div(j, 2), 2 * lax.rem(j, 2)
            key_rows = pl.ds(pl.multiple_of(h * HD, HD), HD)
            value_rows = pl.ds(pl.multiple_of(KVW + h * HD, HD), HD)
            for n in range(4):
                key_terms[y_lo, i + n // 2, n % 2, key_rows] = d_key[:, 128 * n : 128 * n + 128]
                key_terms[y_lo, i + n // 2, n % 2, value_rows] = d_value[:, 128 * n : 128 * n + 128]
            return inner

        visit(True, chunks - 1, 0)
        lax.fori_loop(0, chunks - 1, functools.partial(visit, False), 0)
        d_wide = d_query[...].T * (HD ** -0.5)
        for g in range(GROUP):
            at = pl.multiple_of((h * GROUP + g) * HD, HD)
            v1, v2 = turned(d_wide[:32, 128 * g : 128 * g + 128], d_wide[32:, 128 * g : 128 * g + 128], True)
            rows_f32[pl.ds(at, 32)] = v1
            rows_f32[pl.ds(pl.multiple_of(at + 32, 32), 32)] = v2
        return carry

    lax.fori_loop(0, 2, backward_head, 0)
    shared(1)
    reduce_step(0, 0, 0, (1,))
    lax.fori_loop(2, 5, backward_head, 0)

    copies = []

    def kg(source, goal, target):
        number = len(copies)
        copies.append(remote(source, goal, kg_send.at[number], kg_recv.at[number], target))
        return copies[-1]

    for by in (2, 1, 3, 0):
        for h in (0, 1):
            kg(key_terms.at[h, ring(x, by), 1 - core], key_pair.at[h, ring(x, by)], sibling)

    def add(goal, *sources):
        total = goal[...].astype(jnp.float32)
        for source in sources:
            total += source[...].astype(jnp.float32)
        goal[...] = total.astype(low)

    def block(h, at):
        return key_terms.at[h, at, core]

    widen(d_query_t)
    attn_grad(d_query_t[...], normed[...], 0, 64, 64)
    share(0)
    reduce_step(1, 1, 0)
    for h in (0, 1):
        copies[h].wait_recv()
        add(block(h, ring(x, 2)), key_pair.at[h, ring(x, 2)])
    far = [kg(block(way, ring(x, 2)), key_far.at[way], neighbours[way]) for way in (0, 1)]
    for copy in copies[2:8]:
        copy.wait_recv()
    for by in (1, 3, 0):
        for h in (0, 1):
            add(block(h, ring(x, by)), key_pair.at[h, ring(x, by)])
    near = []
    for way, by in enumerate((1, -1)):
        far[way].wait_recv()
        add(block(way, ring(x, by)), key_far.at[way])
        near.append(kg(key_terms.at[:, ring(x, by), core], key_near.at[way], neighbours[way]))
    reduce_step(1, 1, 1)
    reduce_step(0, 0, 1, (1,))
    shared(0)
    reduce_step(0, 0, 0, (0,))
    for copy in near:
        copy.wait_recv()
    add(block(1 - half, x), key_near.at[0, 1 - half], key_near.at[1, 1 - half])
    final = kg(block(1 - half, x), key_across, across)
    add(block(half, x), key_near.at[0, half], key_near.at[1, half])
    reduce_step(1, 2, 0)
    norm_sum[pl.ds(0, TOK)] = jnp.zeros((TOK, WIDE), jnp.float32)

    def back_through(left_t, width, offset):
        for where in groups:
            picked = jnp.concatenate(
                [left_t[width * shard(where, i) : width * shard(where, i) + width] for i in range(4)], axis=0
            )
            norm_sum[pl.ds(0, TOK)] += dot(picked, weight_rows(where, pl.ds(offset, width)), 0, 0)

    back_through(d_query_t[...], 64, 0)
    final.wait_recv()
    sent.extend(copies)
    rows_f32[pl.ds(0, WIDE_KV)] = key_terms[half, x, core].astype(jnp.float32) + key_across[...].astype(jnp.float32)
    for h in range(KVH):
        v1, v2 = turned(rows_f32[pl.ds(64 * h, 32)], rows_f32[pl.ds(64 * h + 32, 32)], True)
        rows_f32[pl.ds(64 * h, 32)] = v1
        rows_f32[pl.ds(64 * h + 32, 32)] = v2
    for c in range(16):
        d_key_t[pl.ds(48 * c, 48)] = jnp.concatenate(
            [
                rows_f32[pl.ds(20 * c, 20)],
                rows_f32[pl.ds(KVW + 20 * c, 20)],
                jnp.zeros((8, TOK), jnp.float32),
            ],
            axis=0,
        ).astype(low)
    attn_grad(d_key_t[...], normed[...], 128, 48, 48)
    share(2)
    back_through(d_key_t[...], 48, 128)
    d_normed = norm_sum[pl.ds(0, TOK)]
    tok = wide_in[...]
    attn_scale = lax.rsqrt(jnp.sum(tok * tok, axis=-1, keepdims=True) * (1.0 / D) + epsilon)
    attn_gain_term = jnp.sum(d_normed * tok * attn_scale, axis=0, keepdims=True)
    gain_out[...] = gain_out[...] + exact(
        jnp.concatenate([attn_gain_term, jnp.zeros((7, WIDE), jnp.float32)], axis=0), pads[...], 1
    )

    def gain_start(axis):
        me = spot[axis]
        gain_slots[axis, me] = gain_out[...]
        own = gain_slots.at[axis, me]
        return [
            remote(own, own, gain_send.at[axis, by - 1], gain_recv.at[axis, by - 1], device(shifted(spot, axis, by), core))
            for by in (1, 2, 3)
        ]

    def gain_end(axis, started):
        for copy in started:
            copy.wait_recv()
        sent.extend(started)
        gain_out[...] = (gain_slots[axis, 0] + gain_slots[axis, 1]) + (gain_slots[axis, 2] + gain_slots[axis, 3])

    gains = gain_start(0)
    shared(2)
    reduce_step(0, 0, 0, (2,))
    reduce_step(0, 0, 1, (0,))
    reduce_step(0, 1, 0, (1,))
    gain_end(0, gains)
    gains = gain_start(1)
    reduce_step(0, 0, 1, (2,))
    scaled = d_normed * attn_gain
    d_input = residual[...] + attn_scale * (
        scaled - tok * attn_scale * attn_scale * (jnp.sum(scaled * tok, axis=-1, keepdims=True) * (1.0 / D))
    )
    input_grad[...] = dot(pads[...], d_input.astype(low), 1, 1).astype(low)
    reduce_step(0, 1, 0, (0,))
    reduce_step(0, 2, 0, (1,))
    gain_end(1, gains)
    gains = gain_start(2)
    reduce_step(0, 1, 0, (2,))
    reduce_step(1, 3, 0)
    down_back = remote(ffn_out.at[pl.ds(320, 160)], down_out, down_sem.at[2], down_sem.at[3], sibling)
    sent.append(down_back)
    reduce_step(0, 2, 0, (0,))

    def narrow(ref, low_row, rows):
        return exact(ref[pl.ds(low_row, rows)], columns_of, 1)

    gain_end(2, gains)
    gain_slots[3, core] = gain_out[...]
    own = gain_slots.at[3, core]
    joined = remote(own, own, last_send.at[3], last_recv.at[3], sibling)
    sent.append(joined)
    gate_grad[...] = narrow(ffn_out, 0, 160)
    up_grad[...] = narrow(ffn_out, 160, 160)
    reduce_step(0, 2, 0, (2,))
    reduce_step(0, 3, 0, (1, 0))
    query_grad[...] = narrow(attn_out, 0, 64)[:60]
    proj_grad[...] = narrow(attn_out, 64, 64)[:60]
    down_back.wait_recv()
    mine_down, their_down = ffn_out[pl.ds(320, 160)], down_out[...]
    all_down = jnp.concatenate(
        [jnp.where(core == 0, mine_down, their_down), jnp.where(core == 0, their_down, mine_down)], axis=0
    ).T
    down_grad[...] = jnp.where(core == 0, all_down[:64], all_down[64:])[:60]
    joined.wait_recv()
    gain_sums[...] = gain_slots[3, 0] + gain_slots[3, 1]
    reduce_step(0, 3, 0, (2,))
    both_grads = narrow(attn_out, 128, 48)
    key_grad[...] = both_grads[:20]
    value_grad[...] = both_grads[20:40]
    for copy in sent:
        copy.wait_send()


def run_layer(*operands):
    low, wide = jnp.bfloat16, jnp.float32
    slots = []
    for kind, parts in enumerate((ATTN_PARTS, FFN_PARTS)):
        for rows in parts:
            for stage, (half, full) in enumerate(reduce_shapes(rows)):
                if 2 - stage < 2 - kind:
                    slots += [pltpu.VMEM((16, 128), low), pltpu.VMEM((3,) + full + (128,), low)]
                else:
                    slots += [pltpu.VMEM((2,) + half + (128,), low), pltpu.VMEM((2,) + full + (128,), low)]
    dma = pltpu.SemaphoreType.DMA
    return pl.pallas_call(
        layer_kernel,
        out_shape=[jax.ShapeDtypeStruct((D, TOK), low)] * 2
        + [
            jax.ShapeDtypeStruct(shape, wide)
            for shape in ((60, 120), (20, 120), (20, 120), (60, 120), (160, 120), (160, 120), (60, 320), (8, D))
        ],
        in_specs=[pl.BlockSpec(memory_space=pltpu.SMEM) if i == 1 else VMEM for i in range(len(operands))],
        out_specs=[VMEM] * 10,
        scratch_shapes=[
            pltpu.VMEM((2, 4, 4, 4, ATTN_ROWS, 128), low),
            pltpu.VMEM((4, 4, 4, FFN_ROWS, 128), low),
            pltpu.VMEM((ATTN_ROWS, 128), low),
            pltpu.VMEM((FFN_ROWS, 128), low),
            pltpu.VMEM((160, 128), low),
            pltpu.VMEM((160, 128), low),
            pltpu.VMEM((D, WIDE), low),
            pltpu.VMEM((TOK, WIDE), wide),
            pltpu.VMEM((8, WIDE), wide),
            pltpu.VMEM((HD // 2, TOK), wide),
            pltpu.VMEM((HD // 2, TOK), wide),
            pltpu.VMEM((4, 16, 512), low),
            pltpu.VMEM((ATTN_ROWS, 128), wide),
            pltpu.VMEM((FFN_ROWS, 128), wide),
            pltpu.VMEM((160, 128), wide),
            pltpu.VMEM((8, D), wide),
            pltpu.VMEM((TOK, WIDE), low),
            pltpu.VMEM((WIDE, TOK), low),
            pltpu.VMEM((WIDE, TOK), wide),
            pltpu.VMEM((KVH, HD, STACK), low),
            pltpu.VMEM((KVH, STACK, HD + 16), low),
            pltpu.VMEM((WIDE_KV, TOK), low),
            pltpu.VMEM((2, 4, 2, WIDE_KV, TOK), low),
            pltpu.VMEM((4, STACK, 512), wide),
            pltpu.VMEM((KVH, STACK, 128), wide),
            pltpu.VMEM((WIDE, TOK), low),
            pltpu.VMEM((TOK, WIDE), wide),
            pltpu.VMEM((2 * TOK, WIDE), low),
            pltpu.VMEM((2 * TOK, WIDE), low),
            pltpu.VMEM((2 * TOK, WIDE), wide),
            pltpu.VMEM((2 * TOK, WIDE), wide),
            pltpu.VMEM((TOK, WIDE), wide),
            pltpu.VMEM((TOK, WIDE), wide),
            pltpu.VMEM((KVH, HD, STACK), low),
            pltpu.VMEM((KVH, STACK, HD), low),
            pltpu.VMEM((STACK, HD), wide),
            pltpu.VMEM((WIDE, TOK), low),
            pltpu.VMEM((2, 4, 2, WIDE_KV, TOK), low),
            pltpu.VMEM((2, 4, WIDE_KV, TOK), low),
            pltpu.VMEM((2, WIDE_KV, TOK), low),
            pltpu.VMEM((2, 2, WIDE_KV, TOK), low),
            pltpu.VMEM((WIDE_KV, TOK), low),
            pltpu.VMEM((768, TOK), low),
            pltpu.VMEM((2, 4, 4, 4, ATTN_ROWS, 128), low),
            pltpu.VMEM((4, 4, 4, ATTN_ROWS, 128), low),
            pltpu.VMEM((4, 4, 8, D), wide),
        ]
        + slots
        + [
            dma((2, 3, 3, 2, 3)),
            dma((2, 3, 3, 2, 3)),
            dma((2,)),
            dma((4,)),
            dma((3, 4)),
            dma((3, 4)),
            dma,
            dma((7,)),
            dma((7,)),
            dma((8,)),
            dma((8,)),
            dma((4,)),
            dma((4,)),
            dma((13,)),
            dma((13,)),
            dma((2, 3, 3, 2, 3)),
            dma((2, 3, 3, 2, 3)),
            dma((3, 3)),
            dma((3, 3)),
            dma((4,)),
            dma((4,)),
        ],
        compiler_params=pltpu.CompilerParams(collective_id=1, has_side_effects=True, vmem_limit_bytes=63 * MIB),
        name="layer",
    )(*operands)


def deliver_kernel(count, *refs):
    for i in range(count):
        refs[count + 1 + i][...] = refs[i][...]
    for i in (0, 1):
        refs[2 * count + 1 + i][...] = refs[count][i : i + 1, :]


def deliver(arrays, gains):
    count = len(arrays)
    return pl.pallas_call(
        functools.partial(deliver_kernel, count),
        out_shape=[jax.ShapeDtypeStruct(a.shape, a.dtype) for a in arrays] + [jax.ShapeDtypeStruct((1, D), gains.dtype)] * 2,
        in_specs=[VMEM] * (count + 1),
        out_specs=[VMEM] * (count + 2),
        name="deliver",
    )(*arrays, gains)


def per_device(
    inputs, doc_offsets, attn_gain, query_weight, key_weight, value_weight, proj_weight,
    ffn_gain, gate_weight, up_weight, down_weight, cotangent,
):
    *results, gain_sums = run_layer(
        inputs[0].T, doc_offsets, attn_gain[None], ffn_gain[None], query_weight.T, key_weight.T, value_weight.T,
        proj_weight.T, gate_weight.T, up_weight.T, down_weight.T, cotangent[0].T,
    )
    layer_out, input_grad, query_g, key_g, value_g, proj_g, gate_g, up_g, down_g, attn_gain_g, ffn_gain_g = deliver(
        results, gain_sums
    )
    return (
        layer_out.T[None], input_grad.T[None], attn_gain_g[0], query_g.T, key_g.T, value_g.T, proj_g.T,
        ffn_gain_g[0], gate_g.T, up_g.T, down_g.T,
    )


def solution(mesh):
    split = P("fsdp", "ctx")
    rows = P("fsdp", "ctx", None)
    return jax.shard_map(
        per_device,
        mesh=mesh,
        in_specs=(rows, P("fsdp", None), P(), split, split, split, split, P(), split, split, split, rows),
        out_specs=(rows, rows, P(), split, split, split, split, P(), split, split, split),
        check_vma=False,
    )
```

```python
import functools

import jax
import jax.numpy as jnp
from jax import lax
from jax.experimental import pallas as pl
from jax.experimental.pallas import tpu as pltpu
from jax.sharding import PartitionSpec as P

D = 960
HEADS = 15
KVH = 5
HD = 64
NDOC = 4
KVW = 320
WIDE = 1024
TOK = 128

GROUP = HEADS // KVH
STACK = GROUP * TOK
WIDE_KV = 2 * KVW

epsilon = 1e-05
masked_score = -1e30

MESH = pl.DeviceIdType.MESH
ANY = pl.BlockSpec(memory_space=pl.ANY)
VMEM = pl.BlockSpec(memory_space=pltpu.VMEM)
MIB = 1024 * 1024

ATTN_PARTS = ((0, 64), (64, 64), (128, 48))
ATTN_ROWS = 176
FFN_PARTS = ((0, 160), (160, 160), (320, 160))
FFN_ROWS = 480
ORDERS = ((0, 1, 2), (1, 2, 0), (2, 0, 1))


def place():
    c = lax.axis_index("ctx")
    f = lax.axis_index("fsdp")
    x = lax.rem(lax.div(c, 2), 4)
    y = lax.div(f, 4) * 2 + lax.div(c, 8)
    return (x, y, lax.rem(f, 4)), lax.rem(c, 2)


def device(spot, core):
    x, y, z = spot
    return ((lax.rem(y, 2) * 4 + x) * 2 + core, lax.div(y, 2) * 4 + z)


def ring(value, by):
    return lax.rem(value + by + 4, 4)


def shifted(spot, axis, by):
    return tuple(ring(v, by) if i == axis else v for i, v in enumerate(spot))


def greet(devices):
    barrier = pltpu.get_barrier_semaphore()
    for target in devices:
        pl.semaphore_signal(barrier, inc=1, device_id=target, device_id_type=MESH)
    pl.semaphore_wait(barrier, len(devices))


def remote(src, dst, send, recv, target):
    copy = pltpu.make_async_remote_copy(
        src_ref=src, dst_ref=dst, send_sem=send, recv_sem=recv, device_id=target, device_id_type=MESH
    )
    copy.start()
    return copy


def view(ref, lead, spot, done, axis, position, rows, half=None):
    index = []
    cut = min(done) if (half is not None and done) else None
    for a in range(3):
        if a == cut:
            index.append(pl.ds(2 * half, 2))
        elif a in done:
            index.append(pl.ds(0, 4))
        elif a == axis:
            index.append(position)
        else:
            index.append(spot[a])
    low, count = rows
    if half is not None and not done:
        first = (count // 32) * 16
        low, count = (low, first) if half == 0 else (low + first, count - first)
    return ref.at[tuple(lead) + tuple(index) + (pl.ds(low, count),)]


def add_into(target, terms):
    lead = target.shape[:-2]
    if not lead:
        total = target[...].astype(jnp.float32)
        for term in terms:
            total += term[...].astype(jnp.float32)
        target[...] = total.astype(target.dtype)
        return
    inner = lead[1] if len(lead) == 2 else 1

    def body(i, carry):
        at = (lax.div(i, inner), lax.rem(i, inner)) if len(lead) == 2 else (i,)
        total = target[at].astype(jnp.float32)
        for term in terms:
            total += term[at].astype(jnp.float32)
        target[at] = total.astype(target.dtype)
        return carry

    lax.fori_loop(0, lead[0] * inner, body, 0)


def reduce_shapes(rows):
    count = rows[1]
    first = (count // 32) * 16
    return (
        ((2, 4, count), (4, 4, count)),
        ((2, count), (4, count)),
        ((count - first,), (count,)),
    )


def dot(left, right, left_dim=1, right_dim=0):
    return lax.dot_general(left, right, (((left_dim,), (right_dim,)), ((), ())), preferred_element_type=jnp.float32)


def layer_kernel(
    inputs, doc_offsets, attn_gain_in, ffn_gain_in, query_weight, key_weight, value_weight, proj_weight, gate_weight, up_weight, down_weight, cotangent,
    layer_out, input_grad, query_grad, key_grad, value_grad, proj_grad, gate_grad, up_grad, down_grad, gain_sums,
    attn_w, ffn_w, attn_block, ffn_own, down_away, down_in, pads, wide_in, gain_rows, cosine, sine, segments,
    attn_out, ffn_out, down_out, gain_out,
    normed, normed_t, rows_f32, query_t, query, key_own, keys, scores, mixed, mixed_t, residual,
    tokens, cots, out_sum, norm_sum, out_in, norm_in,
    d_mixed_t, d_mixed, d_query, d_query_t, key_terms, key_pair, key_far, key_near, key_across, d_key_t,
    attn_g, pair_in, gain_slots,
    *scratch,
):
    slots = scratch[:36]
    (
        send, recv, own_sem, down_sem, pair_send, pair_recv,
        key_own_sem, key_send, key_recv, kpair_send, kpair_recv,
        ffn_send, ffn_recv, kg_send, kg_recv, r_send, r_recv, gain_send, gain_recv, last_send, last_recv,
    ) = scratch[36:]
    low = jnp.bfloat16
    spot, core = place()
    x, y, z = spot
    half = lax.rem(y, 2)
    sibling = device(spot, 1 - core)
    across = device((x, y + 1 - 2 * half, z), core)
    chunks = half * 2 + lax.div(x, 2) + 1
    sent = []

    def hot(rows, columns, shift):
        row = lax.broadcasted_iota(jnp.int32, (rows, columns), 0)
        column = lax.broadcasted_iota(jnp.int32, (rows, columns), 1)
        return column == row + shift(row)

    by_sixty = lambda row: lax.shift_right_logical(row * 1093, 16) * 4
    columns_of = hot(120, 128, by_sixty).astype(low)
    zeros = lambda rows: jnp.zeros((rows, 128), jnp.float32)
    turn = lambda ref: dot(ref[...], columns_of)
    attn_block[pl.ds(128, 48)] = jnp.concatenate([turn(key_weight), turn(value_weight), zeros(8)], axis=0).astype(low)
    attn_block[pl.ds(0, 64)] = jnp.concatenate([turn(query_weight), zeros(4)], axis=0).astype(low)
    attn_block[pl.ds(64, 64)] = jnp.concatenate([turn(proj_weight), zeros(4)], axis=0).astype(low)
    ffn_own[pl.ds(0, 160)] = turn(gate_weight).astype(low)
    ffn_own[pl.ds(160, 160)] = turn(up_weight).astype(low)
    placed = hot(60, 128, lambda row: 64 * core).astype(low)
    down_both = dot(down_weight[...], placed, 0, 0)
    down_away[...] = jnp.where(core == 0, down_both[160:], down_both[:160]).astype(low)
    ffn_own[pl.ds(320, 160)] = jnp.where(core == 0, down_both[:160], down_both[160:]).astype(low)

    greet([device(shifted(spot, a, by), core) for a in range(3) for by in (1, 2, 3)] + [sibling])
    down_copy = remote(down_away, down_in, down_sem.at[0], down_sem.at[1], sibling)
    sent.append(down_copy)
    own_attn = pltpu.make_async_copy(attn_block, attn_w.at[core, x, y, z], own_sem.at[0])
    own_attn.start()
    waiting, gathered, paired = {}, [], {}

    def pass_on(part, number, position):
        order = ORDERS[part]
        piece = view(attn_w, (core,), spot, order[:2], order[2], position, ATTN_PARTS[part])
        paired[part, number] = remote(piece, piece, pair_send.at[part, number], pair_recv.at[part, number], sibling)

    def direct(kind, stage):
        return stage < 2 - kind

    def gather_step(kind, stage, second, some=(2, 0, 1)):
        for part in some:
            axis, done = ORDERS[part][stage], ORDERS[part][:stage]
            if kind == 0:
                whole, lead, rows, block = attn_w, (core,), ATTN_PARTS[part], attn_block
            else:
                whole, lead, rows, block = ffn_w, (), FFN_PARTS[part], ffn_own
            for copy in waiting.pop((kind, part), ()):
                copy.wait_recv()
            me = spot[axis]
            copies = []
            for way, by in enumerate((1, -1, 2) if direct(kind, stage) else (1, -1)):
                target = device(shifted(spot, axis, by), core)
                if second:
                    source = goal = view(whole, lead, spot, done, axis, ring(me, -by), rows, half=way)
                else:
                    source = goal = view(whole, lead, spot, done, axis, me, rows)
                    if stage == 0:
                        source = block.at[pl.ds(rows[0], rows[1])]
                copies.append(
                    remote(
                        source, goal,
                        send.at[kind, part, stage, second, way], recv.at[kind, part, stage, second, way], target,
                    )
                )
            waiting[kind, part] = copies
            (sent if kind == 0 else gathered).extend(copies)
            if kind == 0 and stage == 2:
                if second:
                    pass_on(part, 1, ring(me, 1))
                    pass_on(part, 2, ring(me, -1))
                else:
                    pass_on(part, 0, me)

    def settle(kind, part):
        for copy in waiting.pop((kind, part), ()):
            copy.wait_recv()

    gather_step(0, 0, 0)

    def fill_pads(i, carry):
        start = pl.multiple_of(i * 160, 160)
        pads[pl.ds(start, 160)] = hot(160, WIDE, lambda row: start + by_sixty(row + start)).astype(low)
        return carry

    lax.fori_loop(0, 6, fill_pads, 0)
    wide_in[...] = dot(inputs[...], pads[...], 0, 0)
    cots[pl.ds(0, TOK)] = dot(cotangent[...], pads[...], 0, 0).astype(low)
    cot_copy = remote(cots.at[pl.ds(0, TOK)], cots.at[pl.ds(TOK, TOK)], ffn_send.at[0], ffn_recv.at[0], sibling)

    def exact(array, places, dim):
        total = jnp.zeros((), jnp.float32)
        for _ in range(3):
            piece = array.astype(low)
            array = array - piece.astype(jnp.float32)
            total = total + dot(piece, places, 1, dim)
        return total

    gain_rows[...] = exact(
        jnp.concatenate([attn_gain_in[...], ffn_gain_in[...], jnp.zeros((6, D), jnp.float32)], axis=0), pads[...], 0
    )
    attn_gain, ffn_gain = gain_rows[0:1, :], gain_rows[1:2, :]
    down_copy.wait_recv()
    ffn_own[pl.ds(320, 160)] = ffn_own[pl.ds(320, 160)] + down_in[...]
    own_ffn = pltpu.make_async_copy(ffn_own, ffn_w.at[x, y, z], own_sem.at[1])
    own_ffn.start()
    own_attn.wait()
    gather_step(0, 1, 0)
    gather_step(1, 0, 0)
    tok = wide_in[...]
    attn_scale = lax.rsqrt(jnp.sum(tok * tok, axis=-1, keepdims=True) * (1.0 / D) + epsilon)
    wide_normed = tok * attn_scale * attn_gain
    normed[...] = wide_normed.astype(low)
    normed_t[...] = wide_normed.T.astype(low)
    own_ffn.wait()
    gather_step(0, 2, 0)
    gather_step(1, 1, 0)

    first_row = (half * 8 + x * 2 + core) * TOK

    def document(index):
        number, start = jnp.zeros_like(index), jnp.zeros_like(index)
        for i in range(1, NDOC):
            after = index >= doc_offsets[0, i]
            number += jnp.where(after, 1, 0)
            start = jnp.where(after, doc_offsets[0, i], start)
        return number, start

    table_token = first_row + lax.broadcasted_iota(jnp.int32, (HD // 2, TOK), 1)
    row = lax.broadcasted_iota(jnp.int32, (HD // 2, TOK), 0)
    rates = jnp.zeros((HD // 2, TOK), jnp.float32)
    for i in range(HD // 2):
        rates = jnp.where(row == i, 10000.0 ** (-2.0 * i / HD), rates)
    angles = (table_token - document(table_token)[1]).astype(jnp.float32) * rates
    cosine[...] = jnp.cos(angles)
    sine[...] = jnp.sin(angles)
    row = lax.broadcasted_iota(jnp.int32, (16, 512), 0)
    for j in range(4):
        number = document(512 * j + lax.broadcasted_iota(jnp.int32, (16, 512), 1))[0]
        segments[j] = jnp.where(number == row, 1.0, 0.0).astype(low)
    row = lax.broadcasted_iota(jnp.int32, (16, STACK), 0)
    own_token = first_row + jnp.bitwise_and(lax.broadcasted_iota(jnp.int32, (16, STACK), 1), TOK - 1)
    apart = jnp.where((document(own_token)[0] != row) & (row < NDOC), masked_score, 0.0)
    last_key = first_row + jnp.bitwise_and(lax.broadcasted_iota(jnp.int32, (STACK, 512), 0), TOK - 1)

    gather_step(0, 2, 1)
    for part in (2, 0, 1):
        settle(0, part)
        pass_on(part, 3, ring(spot[ORDERS[part][2]], 2))
    sent.extend(paired.values())

    def settle_pairs(part):
        for number in range(4):
            paired[part, number].wait_recv()

    def weight_rows(where, rows):
        y_lo, p = where
        return jnp.concatenate(
            [
                jnp.concatenate([attn_w[p, i, 2 * (f // 4) + y_lo, f % 4, rows] for f in range(8)], axis=1)
                for i in range(4)
            ],
            axis=0,
        )

    groups = [(y_lo, p) for y_lo in (0, 1) for p in (0, 1)]

    def shard(where, i):
        return (where[0] * 4 + i) * 2 + where[1]

    def turned(v1, v2, back):
        c, s = cosine[...], (-sine[...] if back else sine[...])
        return v1 * c - v2 * s, v2 * c + v1 * s

    gather_step(1, 1, 1)
    settle_pairs(2)
    for where in groups:
        term = dot(weight_rows(where, pl.ds(128, 48)), normed_t[...])
        for i in range(4):
            c = shard(where, i)
            rows_f32[pl.ds(20 * c, 20)] = term[48 * i : 48 * i + 20]
            rows_f32[pl.ds(KVW + 20 * c, 20)] = term[48 * i + 20 : 48 * i + 40]
    for h in range(KVH):
        v1, v2 = turned(rows_f32[pl.ds(64 * h, 32)], rows_f32[pl.ds(64 * h + 32, 32)], False)
        key_own[pl.ds(64 * h, 32)] = v1.astype(low)
        key_own[pl.ds(64 * h + 32, 32)] = v2.astype(low)
    key_own[pl.ds(KVW, KVW)] = rows_f32[pl.ds(KVW, KVW)].astype(low)

    mine = keys.at[half, x, core]
    own_keys = pltpu.make_async_copy(key_own, mine, key_own_sem)
    own_keys.start()
    kpairs = []

    def pass_keys(ref):
        kpairs.append(remote(ref, ref, kpair_send.at[len(kpairs)], kpair_recv.at[len(kpairs)], sibling))

    def key_copy(source, goal, number, target):
        return remote(source, goal, key_send.at[number], key_recv.at[number], target)

    neighbours = [device(shifted(spot, 0, by), core) for by in (1, -1)]
    over = key_copy(key_own, mine, 0, across)
    first = [key_copy(key_own, mine, 1 + way, neighbours[way]) for way in (0, 1)]
    kpairs.append(remote(key_own, mine, kpair_send.at[0], kpair_recv.at[0], sibling))

    settle_pairs(0)
    for where in groups:
        term = dot(weight_rows(where, pl.ds(0, 64)), normed_t[...])
        for i in range(4):
            rows_f32[pl.ds(60 * shard(where, i), 60)] = term[64 * i : 64 * i + 60]

    gather_step(1, 2, 0, (0,))
    over.wait_recv()
    other = keys.at[1 - half, x, core]
    second = [key_copy(other, other, 3 + way, neighbours[way]) for way in (0, 1)]
    pass_keys(other)

    def heads(h, carry):
        pieces = []
        for g in range(GROUP):
            at = pl.multiple_of((h * GROUP + g) * HD, HD)
            v1, v2 = turned(rows_f32[pl.ds(at, 32)], rows_f32[pl.ds(pl.multiple_of(at + 32, 32), 32)], False)
            pieces.append(jnp.concatenate([v1, v2], axis=0) * (HD ** -0.5))
        wide = jnp.concatenate(pieces, axis=1)
        query_t[h] = wide.astype(low)
        query[h] = jnp.concatenate([wide, apart], axis=0).T.astype(low)
        return carry

    gather_step(1, 2, 0, (2,))
    lax.fori_loop(0, KVH, heads, 0)

    last = []
    for way, by in enumerate((1, -1)):
        first[way].wait_recv()
        ref = keys.at[half, ring(x, -by), core]
        if way == 0:
            last.append(key_copy(ref, ref, 5, neighbours[0]))
        pass_keys(ref)
    for way, by in enumerate((1, -1)):
        second[way].wait_recv()
        ref = keys.at[1 - half, ring(x, -by), core]
        if way == 1:
            last.append(key_copy(ref, ref, 6, neighbours[1]))
        pass_keys(ref)
    gather_step(1, 2, 0, (1,))
    for h in (0, 1):
        last[h].wait_recv()
        pass_keys(keys.at[(half, 1 - half)[h], ring(x, 2), core])
    own_keys.wait()
    for copy in kpairs:
        copy.wait_recv()
    sent.extend([over] + first + second + last + kpairs)

    def key_chunk(j, at):
        rows = pl.ds(pl.multiple_of(at, HD), HD)
        y_lo, i = lax.div(j, 2), 2 * lax.rem(j, 2)
        return jnp.concatenate([keys[y_lo, i + n // 2, n % 2, rows, :] for n in range(4)], axis=1)

    def block_scores(h, j, newest):
        block = dot(query[h], jnp.concatenate([key_chunk(j, h * HD), segments[j]], axis=0))
        if newest:
            index = j * 512 + lax.broadcasted_iota(jnp.int32, (STACK, 512), 1)
            block = jnp.where(index <= last_key, block, masked_score)
        return block

    def quarters(block, joined):
        return joined(
            joined(block[:, :128], block[:, 128:256]), joined(block[:, 256:384], block[:, 384:])
        )

    def forward_head(h, carry):
        def tops(newest, j, top):
            block = block_scores(h, j, newest)
            scores[j] = block
            return jnp.maximum(top, quarters(block, jnp.maximum))

        top = tops(True, chunks - 1, jnp.full((STACK, 128), masked_score, jnp.float32))
        top = lax.fori_loop(0, chunks - 1, functools.partial(tops, False), top)
        top = jnp.max(top, axis=1, keepdims=True)
        mixed[h, :, :HD] = jnp.zeros((STACK, HD), jnp.float32)

        def weigh(j, total):
            raised = jnp.exp(scores[j] - top)
            mixed[h, :, :HD] += dot(raised.astype(low), key_chunk(j, KVW + h * HD), 1, 1)
            return total + quarters(raised, jnp.add)

        total = lax.fori_loop(0, chunks, weigh, jnp.zeros((STACK, 128), jnp.float32))
        total = jnp.sum(total, axis=1, keepdims=True)
        mixed[h, :, HD : HD + 1] = top + jnp.log(total)
        out = mixed[h, :, :HD] / total
        mixed[h, :, :HD] = out
        out_t = out.T
        for g in range(GROUP):
            rows_f32[pl.ds(pl.multiple_of((h * GROUP + g) * HD, HD), HD)] = out_t[:, 128 * g : 128 * g + 128]
        return carry

    lax.fori_loop(0, 3, forward_head, 0)
    gather_step(1, 2, 1)
    lax.fori_loop(3, 5, forward_head, 0)

    def widen(goal):
        for c in range(16):
            piece = jnp.concatenate([rows_f32[pl.ds(60 * c, 60)], jnp.zeros((4, TOK), jnp.float32)], axis=0)
            goal[pl.ds(64 * c, 64)] = piece.astype(low)

    widen(mixed_t)
    settle_pairs(1)
    for where in groups:
        term = dot(weight_rows(where, pl.ds(64, 64)), mixed_t[...])
        for i in range(4):
            rows_f32[pl.ds(64 * shard(where, i), 64)] = term[64 * i : 64 * i + 64]
    residual[...] = wide_in[...] + rows_f32[...].T

    res = residual[...]
    ffn_scale = lax.rsqrt(jnp.sum(res * res, axis=-1, keepdims=True) * (1.0 / D) + epsilon)
    tokens[pl.ds(0, TOK)] = (res * ffn_scale * ffn_gain).astype(low)
    token_copy = remote(tokens.at[pl.ds(0, TOK)], tokens.at[pl.ds(TOK, TOK)], ffn_send.at[1], ffn_recv.at[1], sibling)
    out_sum[...] = jnp.zeros_like(out_sum)
    norm_sum[...] = jnp.zeros_like(norm_sum)
    cot_copy.wait_recv()
    for part in (0, 1, 2):
        settle(1, part)
    for copy in gathered:
        copy.wait_send()
    token_copy.wait_recv()

    def ffn_at(part, block, lane):
        high, slow = lax.div(block, 4), lax.rem(block, 4)
        if part == 2:
            return (lane % 4, high * 2 + lane // 4, slow, pl.ds(320, 160))
        return (slow, (lane // 4) * 2 + high, lane % 4, pl.ds(160 * part, 160))

    def ffn_chunk(j, carry):
        gate_rows, up_rows, down_rows = [
            jnp.concatenate(
                [
                    jnp.concatenate([ffn_w[ffn_at(part, 2 * j + u, lane)] for lane in range(8)], axis=1)
                    for u in (0, 1)
                ],
                axis=0,
            )
            for part in (0, 1, 2)
        ]
        both, cot_both = tokens[...], cots[...]
        gate_value = dot(both, gate_rows, 1, 1)
        up_value = dot(both, up_rows, 1, 1)
        d_hidden = dot(cot_both, down_rows, 1, 1)
        sigmoid = 1.0 / (1.0 + jnp.exp(-gate_value))
        silu = gate_value * sigmoid
        hidden = (silu * up_value).astype(low)
        d_gate = (d_hidden * up_value * sigmoid * (1.0 + gate_value * (1.0 - sigmoid))).astype(low)
        d_up = (d_hidden * silu).astype(low)
        out_sum[...] += dot(hidden, down_rows)
        norm_sum[...] += dot(d_gate, gate_rows) + dot(d_up, up_rows)
        for part, (left, right) in enumerate(((d_gate, both), (d_up, both), (hidden, cot_both))):
            term = dot(left, right, 0, 0).astype(low)
            for u in (0, 1):
                for lane in range(8):
                    ffn_w[ffn_at(part, 2 * j + u, lane)] = term[160 * u : 160 * u + 160, 128 * lane : 128 * lane + 128]
        return carry

    lax.fori_loop(0, 4, ffn_chunk, 0)
    theirs = pl.ds(TOK, TOK)
    norm_copy = remote(norm_sum.at[theirs], norm_in, ffn_send.at[2], ffn_recv.at[2], sibling)
    out_copy = remote(out_sum.at[theirs], out_in, ffn_send.at[3], ffn_recv.at[3], sibling)
    sent.extend([cot_copy, token_copy, norm_copy, out_copy])

    def slot(kind, part, stage, second, way):
        ref = slots[((kind * 3 + part) * 3 + stage) * 2 + second]
        return ref.at[way]

    def reduce_step(kind, stage, second, some=(0, 1, 2)):
        whole, lead, parts = (attn_g, (core,), ATTN_PARTS) if kind == 0 else (ffn_w, (), FFN_PARTS)
        for part in some:
            rows = parts[part]
            if stage < 3:
                axis, done = ORDERS[part][2 - stage], ORDERS[part][: 2 - stage]
            arrived = waiting.pop((2 + kind, part), ())
            for copy in arrived:
                copy.wait_recv()
            if arrived and not second:
                before, full = ORDERS[part][3 - stage], ORDERS[part][: 3 - stage]
                add_into(
                    view(whole, lead, spot, full, before, spot[before], rows),
                    [slot(kind, part, stage - 1, 1, way) for way in range(3 if direct(kind, 3 - stage) else 2)],
                )
            if stage == 3:
                goal = attn_out if kind == 0 else ffn_out
                goal[pl.ds(rows[0], rows[1])] = whole[lead + spot + (pl.ds(rows[0], rows[1]),)].astype(jnp.float32)
                continue
            straight = direct(kind, 2 - stage)
            me = spot[axis]
            copies = []
            for way, by in enumerate((1, -1, 2) if straight else (1, -1)):
                target = device(shifted(spot, axis, by), core)
                if straight:
                    source = view(whole, lead, spot, done, axis, ring(me, by), rows)
                elif second:
                    add_into(
                        view(whole, lead, spot, done, axis, ring(me, by), rows, half=way),
                        [slot(kind, part, stage, 0, way)],
                    )
                    source = view(whole, lead, spot, done, axis, ring(me, by), rows)
                else:
                    source = view(whole, lead, spot, done, axis, ring(me, 2), rows, half=way)
                copies.append(
                    remote(
                        source, slot(kind, part, stage, 1 if straight else second, way),
                        r_send.at[kind, part, stage, second, way], r_recv.at[kind, part, stage, second, way], target,
                    )
                )
            waiting[2 + kind, part] = copies
            sent.extend(copies)

    reduce_step(1, 0, 0)
    norm_copy.wait_recv()
    d_normed = norm_sum[pl.ds(0, TOK)] + norm_in[...]
    res = residual[...]
    ffn_scale = lax.rsqrt(jnp.sum(res * res, axis=-1, keepdims=True) * (1.0 / D) + epsilon)
    ffn_gain_term = jnp.sum(d_normed * res * ffn_scale, axis=0, keepdims=True)
    gain_out[...] = exact(jnp.concatenate([jnp.zeros_like(ffn_gain_term), ffn_gain_term, jnp.zeros((6, WIDE), jnp.float32)], axis=0), pads[...], 1)
    scaled = d_normed * ffn_gain
    d_residual = cots[pl.ds(0, TOK)].astype(jnp.float32) + ffn_scale * (
        scaled - res * ffn_scale * ffn_scale * (jnp.sum(scaled * res, axis=-1, keepdims=True) * (1.0 / D))
    )
    out_copy.wait_recv()
    layer_out[...] = dot(
        pads[...], (res + out_sum[pl.ds(0, TOK)] + out_in[...]).astype(low), 1, 1
    ).astype(low)
    residual[...] = d_residual
    d_branch = d_residual.astype(low)
    d_branch_t = d_residual.T.astype(low)

    norm_sum[pl.ds(0, TOK)] = jnp.zeros((TOK, WIDE), jnp.float32)
    for where in groups:
        picked = jnp.concatenate(
            [d_branch[:, 64 * shard(where, i) : 64 * shard(where, i) + 64] for i in range(4)], axis=1
        )
        norm_sum[pl.ds(0, TOK)] += dot(picked, weight_rows(where, pl.ds(64, 64)))
    d_wide = norm_sum[pl.ds(0, TOK)].T
    for c in range(16):
        rows_f32[pl.ds(60 * c, 60)] = d_wide[64 * c : 64 * c + 60]

    def attn_grad(left_t, right, offset, count, width):
        for where in groups:
            term = dot(
                jnp.concatenate([left_t[width * shard(where, i) : width * shard(where, i) + width] for i in range(4)], axis=0),
                right,
            ).astype(low)
            y_lo, p = where
            for i in range(4):
                for f in range(8):
                    attn_g[p, i, 2 * (f // 4) + y_lo, f % 4, pl.ds(offset, count)] = term[
                        width * i : width * i + count, 128 * f : 128 * f + 128
                    ]

    gpairs = []

    def share(part):
        rows = pl.ds(*ATTN_PARTS[part])
        gpairs.append(
            remote(
                attn_g.at[1 - core, :, :, :, rows], pair_in.at[:, :, :, rows], last_send.at[part], last_recv.at[part], sibling
            )
        )

    def shared(part):
        rows = pl.ds(*ATTN_PARTS[part])
        gpairs[0].wait_recv()
        sent.append(gpairs.pop(0))

        def body(i, carry):
            at = (lax.div(i, 16), lax.rem(lax.div(i, 4), 4), lax.rem(i, 4), rows)
            goal = (core,) + at
            attn_g[goal] = (attn_g[goal].astype(jnp.float32) + pair_in[at].astype(jnp.float32)).astype(low)
            return carry

        lax.fori_loop(0, 64, body, 0)

    def d_heads(h, carry):
        pieces = [rows_f32[pl.ds(pl.multiple_of((h * GROUP + g) * HD, HD), HD)] for g in range(GROUP)]
        wide = jnp.concatenate(pieces, axis=1)
        d_mixed_t[h] = wide.astype(low)
        d_mixed[h] = wide.T.astype(low)
        return carry

    lax.fori_loop(0, KVH, d_heads, 0)
    mixed_rows = mixed_t[...].astype(jnp.float32).T.astype(low)
    attn_grad(d_branch_t, mixed_rows, 64, 64, 64)
    share(1)
    reduce_step(1, 0, 1)

    def clear(j, carry):
        key_terms[lax.div(j, 4), lax.rem(j, 4)] = jnp.zeros((2, WIDE_KV, TOK), low)
        return carry

    lax.fori_loop(2 * chunks, 8, clear, 0)

    def backward_head(h, carry):
        delta = jnp.sum(d_mixed[h].astype(jnp.float32) * mixed[h, :, :HD], axis=1, keepdims=True)
        d_query[...] = jnp.zeros_like(d_query)

        def visit(newest, j, inner):
            shares = jnp.exp(block_scores(h, j, newest) - mixed[h, :, HD : HD + 1])
            d_shares = dot(d_mixed[h], key_chunk(j, KVW + h * HD))
            d_scores = (shares * (d_shares - delta)).astype(low)
            d_query[...] += dot(d_scores, key_chunk(j, h * HD), 1, 1)
            d_key = dot(query_t[h], d_scores).astype(low)
            d_value = dot(d_mixed_t[h], shares.astype(low)).astype(low)
            y_lo, i = lax.div(j, 2), 2 * lax.rem(j, 2)
            key_rows = pl.ds(pl.multiple_of(h * HD, HD), HD)
            value_rows = pl.ds(pl.multiple_of(KVW + h * HD, HD), HD)
            for n in range(4):
                key_terms[y_lo, i + n // 2, n % 2, key_rows] = d_key[:, 128 * n : 128 * n + 128]
                key_terms[y_lo, i + n // 2, n % 2, value_rows] = d_value[:, 128 * n : 128 * n + 128]
            return inner

        visit(True, chunks - 1, 0)
        lax.fori_loop(0, chunks - 1, functools.partial(visit, False), 0)
        d_wide = d_query[...].T * (HD ** -0.5)
        for g in range(GROUP):
            at = pl.multiple_of((h * GROUP + g) * HD, HD)
            v1, v2 = turned(d_wide[:32, 128 * g : 128 * g + 128], d_wide[32:, 128 * g : 128 * g + 128], True)
            rows_f32[pl.ds(at, 32)] = v1
            rows_f32[pl.ds(pl.multiple_of(at + 32, 32), 32)] = v2
        return carry

    lax.fori_loop(0, 2, backward_head, 0)
    shared(1)
    reduce_step(0, 0, 0, (1,))
    lax.fori_loop(2, 5, backward_head, 0)

    copies = []

    def kg(source, goal, target):
        number = len(copies)
        copies.append(remote(source, goal, kg_send.at[number], kg_recv.at[number], target))
        return copies[-1]

    for by in (2, 1, 3, 0):
        for h in (0, 1):
            kg(key_terms.at[h, ring(x, by), 1 - core], key_pair.at[h, ring(x, by)], sibling)

    def add(goal, *sources):
        total = goal[...].astype(jnp.float32)
        for source in sources:
            total += source[...].astype(jnp.float32)
        goal[...] = total.astype(low)

    def block(h, at):
        return key_terms.at[h, at, core]

    widen(d_query_t)
    for h in (0, 1):
        copies[h].wait_recv()
        add(block(h, ring(x, 2)), key_pair.at[h, ring(x, 2)])
    far = [kg(block(way, ring(x, 2)), key_far.at[way], neighbours[way]) for way in (0, 1)]
    attn_grad(d_query_t[...], normed[...], 0, 64, 64)
    for copy in copies[2:8]:
        copy.wait_recv()
    share(0)
    for by in (1, 3, 0):
        for h in (0, 1):
            add(block(h, ring(x, by)), key_pair.at[h, ring(x, by)])
    reduce_step(1, 1, 0)
    near = []
    for way, by in enumerate((1, -1)):
        far[way].wait_recv()
        add(block(way, ring(x, by)), key_far.at[way])
        near.append(kg(key_terms.at[:, ring(x, by), core], key_near.at[way], neighbours[way]))
    reduce_step(1, 1, 1)
    reduce_step(0, 0, 1, (1,))
    shared(0)
    reduce_step(0, 0, 0, (0,))
    for copy in near:
        copy.wait_recv()
    add(block(1 - half, x), key_near.at[0, 1 - half], key_near.at[1, 1 - half])
    final = kg(block(1 - half, x), key_across, across)
    add(block(half, x), key_near.at[0, half], key_near.at[1, half])
    reduce_step(1, 2, 0)
    norm_sum[pl.ds(0, TOK)] = jnp.zeros((TOK, WIDE), jnp.float32)

    def back_through(left_t, width, offset):
        for where in groups:
            picked = jnp.concatenate(
                [left_t[width * shard(where, i) : width * shard(where, i) + width] for i in range(4)], axis=0
            )
            norm_sum[pl.ds(0, TOK)] += dot(picked, weight_rows(where, pl.ds(offset, width)), 0, 0)

    back_through(d_query_t[...], 64, 0)
    final.wait_recv()
    sent.extend(copies)
    rows_f32[pl.ds(0, WIDE_KV)] = key_terms[half, x, core].astype(jnp.float32) + key_across[...].astype(jnp.float32)
    for h in range(KVH):
        v1, v2 = turned(rows_f32[pl.ds(64 * h, 32)], rows_f32[pl.ds(64 * h + 32, 32)], True)
        rows_f32[pl.ds(64 * h, 32)] = v1
        rows_f32[pl.ds(64 * h + 32, 32)] = v2
    for c in range(16):
        d_key_t[pl.ds(48 * c, 48)] = jnp.concatenate(
            [
                rows_f32[pl.ds(20 * c, 20)],
                rows_f32[pl.ds(KVW + 20 * c, 20)],
                jnp.zeros((8, TOK), jnp.float32),
            ],
            axis=0,
        ).astype(low)
    attn_grad(d_key_t[...], normed[...], 128, 48, 48)
    share(2)
    back_through(d_key_t[...], 48, 128)
    d_normed = norm_sum[pl.ds(0, TOK)]
    tok = wide_in[...]
    attn_scale = lax.rsqrt(jnp.sum(tok * tok, axis=-1, keepdims=True) * (1.0 / D) + epsilon)
    attn_gain_term = jnp.sum(d_normed * tok * attn_scale, axis=0, keepdims=True)
    gain_out[...] = gain_out[...] + exact(
        jnp.concatenate([attn_gain_term, jnp.zeros((7, WIDE), jnp.float32)], axis=0), pads[...], 1
    )

    def gain_start(axis):
        me = spot[axis]
        gain_slots[axis, me] = gain_out[...]
        own = gain_slots.at[axis, me]
        return [
            remote(own, own, gain_send.at[axis, by - 1], gain_recv.at[axis, by - 1], device(shifted(spot, axis, by), core))
            for by in (1, 2, 3)
        ]

    def gain_end(axis, started):
        for copy in started:
            copy.wait_recv()
        sent.extend(started)
        gain_out[...] = (gain_slots[axis, 0] + gain_slots[axis, 1]) + (gain_slots[axis, 2] + gain_slots[axis, 3])

    gains = gain_start(0)
    shared(2)
    reduce_step(0, 0, 0, (2,))
    reduce_step(0, 0, 1, (0,))
    reduce_step(0, 1, 0, (1,))
    gain_end(0, gains)
    gains = gain_start(1)
    reduce_step(0, 0, 1, (2,))
    scaled = d_normed * attn_gain
    d_input = residual[...] + attn_scale * (
        scaled - tok * attn_scale * attn_scale * (jnp.sum(scaled * tok, axis=-1, keepdims=True) * (1.0 / D))
    )
    input_grad[...] = dot(pads[...], d_input.astype(low), 1, 1).astype(low)
    reduce_step(0, 1, 0, (0,))
    reduce_step(0, 2, 0, (1,))
    gain_end(1, gains)
    gains = gain_start(2)
    reduce_step(0, 1, 0, (2,))
    reduce_step(1, 3, 0)
    down_back = remote(ffn_out.at[pl.ds(320, 160)], down_out, down_sem.at[2], down_sem.at[3], sibling)
    sent.append(down_back)
    reduce_step(0, 2, 0, (0,))

    def narrow(ref, low_row, rows):
        return exact(ref[pl.ds(low_row, rows)], columns_of, 1)

    gain_end(2, gains)
    gain_slots[3, core] = gain_out[...]
    own = gain_slots.at[3, core]
    joined = remote(own, own, last_send.at[3], last_recv.at[3], sibling)
    sent.append(joined)
    gate_grad[...] = narrow(ffn_out, 0, 160)
    up_grad[...] = narrow(ffn_out, 160, 160)
    reduce_step(0, 2, 0, (2,))
    reduce_step(0, 3, 0, (1, 0))
    query_grad[...] = narrow(attn_out, 0, 64)[:60]
    proj_grad[...] = narrow(attn_out, 64, 64)[:60]
    down_back.wait_recv()
    mine_down, their_down = ffn_out[pl.ds(320, 160)], down_out[...]
    all_down = jnp.concatenate(
        [jnp.where(core == 0, mine_down, their_down), jnp.where(core == 0, their_down, mine_down)], axis=0
    ).T
    down_grad[...] = jnp.where(core == 0, all_down[:64], all_down[64:])[:60]
    joined.wait_recv()
    gain_sums[...] = gain_slots[3, 0] + gain_slots[3, 1]
    reduce_step(0, 3, 0, (2,))
    both_grads = narrow(attn_out, 128, 48)
    key_grad[...] = both_grads[:20]
    value_grad[...] = both_grads[20:40]
    for copy in sent:
        copy.wait_send()


def run_layer(*operands):
    low, wide = jnp.bfloat16, jnp.float32
    slots = []
    for kind, parts in enumerate((ATTN_PARTS, FFN_PARTS)):
        for rows in parts:
            for stage, (half, full) in enumerate(reduce_shapes(rows)):
                if 2 - stage < 2 - kind:
                    slots += [pltpu.VMEM((16, 128), low), pltpu.VMEM((3,) + full + (128,), low)]
                else:
                    slots += [pltpu.VMEM((2,) + half + (128,), low), pltpu.VMEM((2,) + full + (128,), low)]
    dma = pltpu.SemaphoreType.DMA
    return pl.pallas_call(
        layer_kernel,
        out_shape=[jax.ShapeDtypeStruct((D, TOK), low)] * 2
        + [
            jax.ShapeDtypeStruct(shape, wide)
            for shape in ((60, 120), (20, 120), (20, 120), (60, 120), (160, 120), (160, 120), (60, 320), (8, D))
        ],
        in_specs=[pl.BlockSpec(memory_space=pltpu.SMEM) if i == 1 else VMEM for i in range(len(operands))],
        out_specs=[VMEM] * 10,
        scratch_shapes=[
            pltpu.VMEM((2, 4, 4, 4, ATTN_ROWS, 128), low),
            pltpu.VMEM((4, 4, 4, FFN_ROWS, 128), low),
            pltpu.VMEM((ATTN_ROWS, 128), low),
            pltpu.VMEM((FFN_ROWS, 128), low),
            pltpu.VMEM((160, 128), low),
            pltpu.VMEM((160, 128), low),
            pltpu.VMEM((D, WIDE), low),
            pltpu.VMEM((TOK, WIDE), wide),
            pltpu.VMEM((8, WIDE), wide),
            pltpu.VMEM((HD // 2, TOK), wide),
            pltpu.VMEM((HD // 2, TOK), wide),
            pltpu.VMEM((4, 16, 512), low),
            pltpu.VMEM((ATTN_ROWS, 128), wide),
            pltpu.VMEM((FFN_ROWS, 128), wide),
            pltpu.VMEM((160, 128), wide),
            pltpu.VMEM((8, D), wide),
            pltpu.VMEM((TOK, WIDE), low),
            pltpu.VMEM((WIDE, TOK), low),
            pltpu.VMEM((WIDE, TOK), wide),
            pltpu.VMEM((KVH, HD, STACK), low),
            pltpu.VMEM((KVH, STACK, HD + 16), low),
            pltpu.VMEM((WIDE_KV, TOK), low),
            pltpu.VMEM((2, 4, 2, WIDE_KV, TOK), low),
            pltpu.VMEM((4, STACK, 512), wide),
            pltpu.VMEM((KVH, STACK, 128), wide),
            pltpu.VMEM((WIDE, TOK), low),
            pltpu.VMEM((TOK, WIDE), wide),
            pltpu.VMEM((2 * TOK, WIDE), low),
            pltpu.VMEM((2 * TOK, WIDE), low),
            pltpu.VMEM((2 * TOK, WIDE), wide),
            pltpu.VMEM((2 * TOK, WIDE), wide),
            pltpu.VMEM((TOK, WIDE), wide),
            pltpu.VMEM((TOK, WIDE), wide),
            pltpu.VMEM((KVH, HD, STACK), low),
            pltpu.VMEM((KVH, STACK, HD), low),
            pltpu.VMEM((STACK, HD), wide),
            pltpu.VMEM((WIDE, TOK), low),
            pltpu.VMEM((2, 4, 2, WIDE_KV, TOK), low),
            pltpu.VMEM((2, 4, WIDE_KV, TOK), low),
            pltpu.VMEM((2, WIDE_KV, TOK), low),
            pltpu.VMEM((2, 2, WIDE_KV, TOK), low),
            pltpu.VMEM((WIDE_KV, TOK), low),
            pltpu.VMEM((768, TOK), low),
            pltpu.VMEM((2, 4, 4, 4, ATTN_ROWS, 128), low),
            pltpu.VMEM((4, 4, 4, ATTN_ROWS, 128), low),
            pltpu.VMEM((4, 4, 8, D), wide),
        ]
        + slots
        + [
            dma((2, 3, 3, 2, 3)),
            dma((2, 3, 3, 2, 3)),
            dma((2,)),
            dma((4,)),
            dma((3, 4)),
            dma((3, 4)),
            dma,
            dma((7,)),
            dma((7,)),
            dma((8,)),
            dma((8,)),
            dma((4,)),
            dma((4,)),
            dma((13,)),
            dma((13,)),
            dma((2, 3, 3, 2, 3)),
            dma((2, 3, 3, 2, 3)),
            dma((3, 3)),
            dma((3, 3)),
            dma((4,)),
            dma((4,)),
        ],
        compiler_params=pltpu.CompilerParams(collective_id=1, has_side_effects=True, vmem_limit_bytes=63 * MIB),
        name="layer",
    )(*operands)


def deliver_kernel(count, *refs):
    for i in range(count):
        refs[count + 1 + i][...] = refs[i][...]
    for i in (0, 1):
        refs[2 * count + 1 + i][...] = refs[count][i : i + 1, :]


def deliver(arrays, gains):
    count = len(arrays)
    return pl.pallas_call(
        functools.partial(deliver_kernel, count),
        out_shape=[jax.ShapeDtypeStruct(a.shape, a.dtype) for a in arrays] + [jax.ShapeDtypeStruct((1, D), gains.dtype)] * 2,
        in_specs=[VMEM] * (count + 1),
        out_specs=[VMEM] * (count + 2),
        name="deliver",
    )(*arrays, gains)


def per_device(
    inputs, doc_offsets, attn_gain, query_weight, key_weight, value_weight, proj_weight,
    ffn_gain, gate_weight, up_weight, down_weight, cotangent,
):
    *results, gain_sums = run_layer(
        inputs[0].T, doc_offsets, attn_gain[None], ffn_gain[None], query_weight.T, key_weight.T, value_weight.T,
        proj_weight.T, gate_weight.T, up_weight.T, down_weight.T, cotangent[0].T,
    )
    layer_out, input_grad, query_g, key_g, value_g, proj_g, gate_g, up_g, down_g, attn_gain_g, ffn_gain_g = deliver(
        results, gain_sums
    )
    return (
        layer_out.T[None], input_grad.T[None], attn_gain_g[0], query_g.T, key_g.T, value_g.T, proj_g.T,
        ffn_gain_g[0], gate_g.T, up_g.T, down_g.T,
    )


def solution(mesh):
    split = P("fsdp", "ctx")
    rows = P("fsdp", "ctx", None)
    return jax.shard_map(
        per_device,
        mesh=mesh,
        in_specs=(rows, P("fsdp", None), P(), split, split, split, split, P(), split, split, split, rows),
        out_specs=(rows, rows, P(), split, split, split, split, P(), split, split, split),
        check_vma=False,
    )
```

```python
import functools

import jax
import jax.numpy as jnp
from jax import lax
from jax.experimental import pallas as pl
from jax.experimental.pallas import tpu as pltpu
from jax.sharding import PartitionSpec as P

D = 960
HEADS = 15
KVH = 5
HD = 64
NDOC = 4
KVW = 320
WIDE = 1024
TOK = 128

GROUP = HEADS // KVH
STACK = GROUP * TOK
WIDE_KV = 2 * KVW

epsilon = 1e-05
masked_score = -1e30

MESH = pl.DeviceIdType.MESH
ANY = pl.BlockSpec(memory_space=pl.ANY)
VMEM = pl.BlockSpec(memory_space=pltpu.VMEM)
MIB = 1024 * 1024

ATTN_PARTS = ((0, 64), (64, 64), (128, 48))
ATTN_ROWS = 176
FFN_PARTS = ((0, 160), (160, 160), (320, 160))
FFN_ROWS = 480
ORDERS = ((0, 1, 2), (1, 2, 0), (2, 0, 1))


def place():
    c = lax.axis_index("ctx")
    f = lax.axis_index("fsdp")
    x = lax.rem(lax.div(c, 2), 4)
    y = lax.div(f, 4) * 2 + lax.div(c, 8)
    return (x, y, lax.rem(f, 4)), lax.rem(c, 2)


def device(spot, core):
    x, y, z = spot
    return ((lax.rem(y, 2) * 4 + x) * 2 + core, lax.div(y, 2) * 4 + z)


def ring(value, by):
    return lax.rem(value + by + 4, 4)


def shifted(spot, axis, by):
    return tuple(ring(v, by) if i == axis else v for i, v in enumerate(spot))


def greet(devices):
    barrier = pltpu.get_barrier_semaphore()
    for target in devices:
        pl.semaphore_signal(barrier, inc=1, device_id=target, device_id_type=MESH)
    pl.semaphore_wait(barrier, len(devices))


def remote(src, dst, send, recv, target):
    copy = pltpu.make_async_remote_copy(
        src_ref=src, dst_ref=dst, send_sem=send, recv_sem=recv, device_id=target, device_id_type=MESH
    )
    copy.start()
    return copy


def view(ref, lead, spot, done, axis, position, rows, half=None):
    index = []
    cut = min(done) if (half is not None and done) else None
    for a in range(3):
        if a == cut:
            index.append(pl.ds(2 * half, 2))
        elif a in done:
            index.append(pl.ds(0, 4))
        elif a == axis:
            index.append(position)
        else:
            index.append(spot[a])
    low, count = rows
    if half is not None and not done:
        first = (count // 32) * 16
        low, count = (low, first) if half == 0 else (low + first, count - first)
    return ref.at[tuple(lead) + tuple(index) + (pl.ds(low, count),)]


def add_into(target, terms):
    lead = target.shape[:-2]
    if not lead:
        total = target[...].astype(jnp.float32)
        for term in terms:
            total += term[...].astype(jnp.float32)
        target[...] = total.astype(target.dtype)
        return
    inner = lead[1] if len(lead) == 2 else 1

    def body(i, carry):
        at = (lax.div(i, inner), lax.rem(i, inner)) if len(lead) == 2 else (i,)
        total = target[at].astype(jnp.float32)
        for term in terms:
            total += term[at].astype(jnp.float32)
        target[at] = total.astype(target.dtype)
        return carry

    lax.fori_loop(0, lead[0] * inner, body, 0)


def reduce_shapes(rows):
    count = rows[1]
    first = (count // 32) * 16
    return (
        ((2, 4, count), (4, 4, count)),
        ((2, count), (4, count)),
        ((count - first,), (count,)),
    )


def dot(left, right, left_dim=1, right_dim=0):
    return lax.dot_general(left, right, (((left_dim,), (right_dim,)), ((), ())), preferred_element_type=jnp.float32)


def layer_kernel(
    inputs, doc_offsets, attn_gain_in, ffn_gain_in, query_weight, key_weight, value_weight, proj_weight, gate_weight, up_weight, down_weight, cotangent,
    layer_out, input_grad, query_grad, key_grad, value_grad, proj_grad, gate_grad, up_grad, down_grad, gain_sums,
    attn_w, ffn_w, attn_block, ffn_own, down_away, down_in, pads, wide_in, gain_rows, cosine, sine, segments,
    attn_out, ffn_out, down_out, gain_out,
    normed, normed_t, rows_f32, query_t, query, key_own, keys, scores, mixed, mixed_t, residual,
    tokens, cots, out_sum, norm_sum, out_in, norm_in,
    d_mixed_t, d_mixed, d_query, d_query_t, key_terms, key_pair, key_far, key_near, key_across, d_key_t,
    attn_g, pair_in, gain_slots,
    *scratch,
):
    slots = scratch[:36]
    (
        send, recv, own_sem, down_sem, pair_send, pair_recv,
        key_own_sem, key_send, key_recv, kpair_send, kpair_recv,
        ffn_send, ffn_recv, kg_send, kg_recv, r_send, r_recv, gain_send, gain_recv, last_send, last_recv,
    ) = scratch[36:]
    low = jnp.bfloat16
    spot, core = place()
    x, y, z = spot
    half = lax.rem(y, 2)
    sibling = device(spot, 1 - core)
    across = device((x, y + 1 - 2 * half, z), core)
    chunks = half * 2 + lax.div(x, 2) + 1
    sent = []

    def hot(rows, columns, shift):
        row = lax.broadcasted_iota(jnp.int32, (rows, columns), 0)
        column = lax.broadcasted_iota(jnp.int32, (rows, columns), 1)
        return column == row + shift(row)

    by_sixty = lambda row: lax.shift_right_logical(row * 1093, 16) * 4
    columns_of = hot(120, 128, by_sixty).astype(low)
    zeros = lambda rows: jnp.zeros((rows, 128), jnp.float32)
    turn = lambda ref: dot(ref[...], columns_of)
    attn_block[pl.ds(128, 48)] = jnp.concatenate([turn(key_weight), turn(value_weight), zeros(8)], axis=0).astype(low)
    attn_block[pl.ds(0, 64)] = jnp.concatenate([turn(query_weight), zeros(4)], axis=0).astype(low)
    attn_block[pl.ds(64, 64)] = jnp.concatenate([turn(proj_weight), zeros(4)], axis=0).astype(low)
    ffn_own[pl.ds(0, 160)] = turn(gate_weight).astype(low)
    ffn_own[pl.ds(160, 160)] = turn(up_weight).astype(low)
    placed = hot(60, 128, lambda row: 64 * core).astype(low)
    down_both = dot(down_weight[...], placed, 0, 0)
    down_away[...] = jnp.where(core == 0, down_both[160:], down_both[:160]).astype(low)
    ffn_own[pl.ds(320, 160)] = jnp.where(core == 0, down_both[:160], down_both[160:]).astype(low)

    greet([device(shifted(spot, a, by), core) for a in range(3) for by in (1, 2, 3)] + [sibling])
    down_copy = remote(down_away, down_in, down_sem.at[0], down_sem.at[1], sibling)
    sent.append(down_copy)
    own_attn = pltpu.make_async_copy(attn_block, attn_w.at[core, x, y, z], own_sem.at[0])
    own_attn.start()
    waiting, gathered, paired = {}, [], {}

    def pass_on(part, number, position):
        order = ORDERS[part]
        piece = view(attn_w, (core,), spot, order[:2], order[2], position, ATTN_PARTS[part])
        paired[part, number] = remote(piece, piece, pair_send.at[part, number], pair_recv.at[part, number], sibling)

    def direct(kind, stage):
        return stage < 2 - kind

    def gather_step(kind, stage, second, some=(2, 0, 1)):
        for part in some:
            axis, done = ORDERS[part][stage], ORDERS[part][:stage]
            if kind == 0:
                whole, lead, rows, block = attn_w, (core,), ATTN_PARTS[part], attn_block
            else:
                whole, lead, rows, block = ffn_w, (), FFN_PARTS[part], ffn_own
            for copy in waiting.pop((kind, part), ()):
                copy.wait_recv()
            me = spot[axis]
            copies = []
            for way, by in enumerate((1, -1, 2) if direct(kind, stage) else (1, -1)):
                target = device(shifted(spot, axis, by), core)
                if second:
                    source = goal = view(whole, lead, spot, done, axis, ring(me, -by), rows, half=way)
                else:
                    source = goal = view(whole, lead, spot, done, axis, me, rows)
                    if stage == 0:
                        source = block.at[pl.ds(rows[0], rows[1])]
                copies.append(
                    remote(
                        source, goal,
                        send.at[kind, part, stage, second, way], recv.at[kind, part, stage, second, way], target,
                    )
                )
            waiting[kind, part] = copies
            (sent if kind == 0 else gathered).extend(copies)
            if kind == 0 and stage == 2:
                if second:
                    pass_on(part, 1, ring(me, 1))
                    pass_on(part, 2, ring(me, -1))
                else:
                    pass_on(part, 0, me)

    def settle(kind, part):
        for copy in waiting.pop((kind, part), ()):
            copy.wait_recv()

    gather_step(0, 0, 0)

    def fill_pads(i, carry):
        start = pl.multiple_of(i * 160, 160)
        pads[pl.ds(start, 160)] = hot(160, WIDE, lambda row: start + by_sixty(row + start)).astype(low)
        return carry

    lax.fori_loop(0, 6, fill_pads, 0)
    wide_in[...] = dot(inputs[...], pads[...], 0, 0)
    cots[pl.ds(0, TOK)] = dot(cotangent[...], pads[...], 0, 0).astype(low)
    cot_copy = remote(cots.at[pl.ds(0, TOK)], cots.at[pl.ds(TOK, TOK)], ffn_send.at[0], ffn_recv.at[0], sibling)

    def exact(array, places, dim):
        total = jnp.zeros((), jnp.float32)
        for _ in range(3):
            piece = array.astype(low)
            array = array - piece.astype(jnp.float32)
            total = total + dot(piece, places, 1, dim)
        return total

    gain_rows[...] = exact(
        jnp.concatenate([attn_gain_in[...], ffn_gain_in[...], jnp.zeros((6, D), jnp.float32)], axis=0), pads[...], 0
    )
    attn_gain, ffn_gain = gain_rows[0:1, :], gain_rows[1:2, :]
    down_copy.wait_recv()
    ffn_own[pl.ds(320, 160)] = ffn_own[pl.ds(320, 160)] + down_in[...]
    own_ffn = pltpu.make_async_copy(ffn_own, ffn_w.at[x, y, z], own_sem.at[1])
    own_ffn.start()
    own_attn.wait()
    gather_step(0, 1, 0)
    gather_step(1, 0, 0)
    tok = wide_in[...]
    attn_scale = lax.rsqrt(jnp.sum(tok * tok, axis=-1, keepdims=True) * (1.0 / D) + epsilon)
    wide_normed = tok * attn_scale * attn_gain
    normed[...] = wide_normed.astype(low)
    normed_t[...] = wide_normed.T.astype(low)
    own_ffn.wait()
    gather_step(0, 2, 0)
    gather_step(1, 1, 0)

    first_row = (half * 8 + x * 2 + core) * TOK

    def document(index):
        number, start = jnp.zeros_like(index), jnp.zeros_like(index)
        for i in range(1, NDOC):
            after = index >= doc_offsets[0, i]
            number += jnp.where(after, 1, 0)
            start = jnp.where(after, doc_offsets[0, i], start)
        return number, start

    table_token = first_row + lax.broadcasted_iota(jnp.int32, (HD // 2, TOK), 1)
    row = lax.broadcasted_iota(jnp.int32, (HD // 2, TOK), 0)
    rates = jnp.zeros((HD // 2, TOK), jnp.float32)
    for i in range(HD // 2):
        rates = jnp.where(row == i, 10000.0 ** (-2.0 * i / HD), rates)
    angles = (table_token - document(table_token)[1]).astype(jnp.float32) * rates
    cosine[...] = jnp.cos(angles)
    sine[...] = jnp.sin(angles)
    row = lax.broadcasted_iota(jnp.int32, (16, 512), 0)
    for j in range(4):
        number = document(512 * j + lax.broadcasted_iota(jnp.int32, (16, 512), 1))[0]
        segments[j] = jnp.where(number == row, 1.0, 0.0).astype(low)
    row = lax.broadcasted_iota(jnp.int32, (16, STACK), 0)
    own_token = first_row + jnp.bitwise_and(lax.broadcasted_iota(jnp.int32, (16, STACK), 1), TOK - 1)
    apart = jnp.where((document(own_token)[0] != row) & (row < NDOC), masked_score, 0.0)
    last_key = first_row + jnp.bitwise_and(lax.broadcasted_iota(jnp.int32, (STACK, 512), 0), TOK - 1)

    gather_step(0, 2, 1)
    for part in (2, 0, 1):
        settle(0, part)
        pass_on(part, 3, ring(spot[ORDERS[part][2]], 2))
    sent.extend(paired.values())

    def settle_pairs(part):
        for number in range(4):
            paired[part, number].wait_recv()

    def weight_rows(where, rows):
        y_lo, p = where
        return jnp.concatenate(
            [
                jnp.concatenate([attn_w[p, i, 2 * (f // 4) + y_lo, f % 4, rows] for f in range(8)], axis=1)
                for i in range(4)
            ],
            axis=0,
        )

    groups = [(y_lo, p) for y_lo in (0, 1) for p in (0, 1)]

    def shard(where, i):
        return (where[0] * 4 + i) * 2 + where[1]

    def turned(v1, v2, back):
        c, s = cosine[...], (-sine[...] if back else sine[...])
        return v1 * c - v2 * s, v2 * c + v1 * s

    gather_step(1, 1, 1)
    settle_pairs(2)
    for where in groups:
        term = dot(weight_rows(where, pl.ds(128, 48)), normed_t[...])
        for i in range(4):
            c = shard(where, i)
            rows_f32[pl.ds(20 * c, 20)] = term[48 * i : 48 * i + 20]
            rows_f32[pl.ds(KVW + 20 * c, 20)] = term[48 * i + 20 : 48 * i + 40]
    for h in range(KVH):
        v1, v2 = turned(rows_f32[pl.ds(64 * h, 32)], rows_f32[pl.ds(64 * h + 32, 32)], False)
        key_own[pl.ds(64 * h, 32)] = v1.astype(low)
        key_own[pl.ds(64 * h + 32, 32)] = v2.astype(low)
    key_own[pl.ds(KVW, KVW)] = rows_f32[pl.ds(KVW, KVW)].astype(low)

    mine = keys.at[half, x, core]
    own_keys = pltpu.make_async_copy(key_own, mine, key_own_sem)
    own_keys.start()
    kpairs = []

    def pass_keys(ref):
        kpairs.append(remote(ref, ref, kpair_send.at[len(kpairs)], kpair_recv.at[len(kpairs)], sibling))

    def key_copy(source, goal, number, target):
        return remote(source, goal, key_send.at[number], key_recv.at[number], target)

    neighbours = [device(shifted(spot, 0, by), core) for by in (1, -1)]
    over = key_copy(key_own, mine, 0, across)
    first = [key_copy(key_own, mine, 1 + way, neighbours[way]) for way in (0, 1)]
    kpairs.append(remote(key_own, mine, kpair_send.at[0], kpair_recv.at[0], sibling))

    settle_pairs(0)
    for where in groups:
        term = dot(weight_rows(where, pl.ds(0, 64)), normed_t[...])
        for i in range(4):
            rows_f32[pl.ds(60 * shard(where, i), 60)] = term[64 * i : 64 * i + 60]

    gather_step(1, 2, 0, (0,))
    over.wait_recv()
    other = keys.at[1 - half, x, core]
    second = [key_copy(other, other, 3 + way, neighbours[way]) for way in (0, 1)]
    pass_keys(other)

    def heads(h, carry):
        pieces = []
        for g in range(GROUP):
            at = pl.multiple_of((h * GROUP + g) * HD, HD)
            v1, v2 = turned(rows_f32[pl.ds(at, 32)], rows_f32[pl.ds(pl.multiple_of(at + 32, 32), 32)], False)
            pieces.append(jnp.concatenate([v1, v2], axis=0) * (HD ** -0.5))
        wide = jnp.concatenate(pieces, axis=1)
        query_t[h] = wide.astype(low)
        query[h] = jnp.concatenate([wide, apart], axis=0).T.astype(low)
        return carry

    gather_step(1, 2, 0, (2,))
    lax.fori_loop(0, KVH, heads, 0)

    last = []
    for way, by in enumerate((1, -1)):
        first[way].wait_recv()
        ref = keys.at[half, ring(x, -by), core]
        if way == 0:
            last.append(key_copy(ref, ref, 5, neighbours[0]))
        pass_keys(ref)
    for way, by in enumerate((1, -1)):
        second[way].wait_recv()
        ref = keys.at[1 - half, ring(x, -by), core]
        if way == 1:
            last.append(key_copy(ref, ref, 6, neighbours[1]))
        pass_keys(ref)
    gather_step(1, 2, 0, (1,))
    for h in (0, 1):
        last[h].wait_recv()
        pass_keys(keys.at[(half, 1 - half)[h], ring(x, 2), core])
    own_keys.wait()
    for copy in kpairs:
        copy.wait_recv()
    sent.extend([over] + first + second + last + kpairs)

    def key_chunk(j, at):
        rows = pl.ds(pl.multiple_of(at, HD), HD)
        y_lo, i = lax.div(j, 2), 2 * lax.rem(j, 2)
        return jnp.concatenate([keys[y_lo, i + n // 2, n % 2, rows, :] for n in range(4)], axis=1)

    def block_scores(h, j, newest):
        block = dot(query[h], jnp.concatenate([key_chunk(j, h * HD), segments[j]], axis=0))
        if newest:
            index = j * 512 + lax.broadcasted_iota(jnp.int32, (STACK, 512), 1)
            block = jnp.where(index <= last_key, block, masked_score)
        return block

    def quarters(block, joined):
        return joined(
            joined(block[:, :128], block[:, 128:256]), joined(block[:, 256:384], block[:, 384:])
        )

    def forward_head(h, carry):
        def tops(newest, j, top):
            block = block_scores(h, j, newest)
            scores[j] = block
            return jnp.maximum(top, quarters(block, jnp.maximum))

        top = tops(True, chunks - 1, jnp.full((STACK, 128), masked_score, jnp.float32))
        top = lax.fori_loop(0, chunks - 1, functools.partial(tops, False), top)
        top = jnp.max(top, axis=1, keepdims=True)
        mixed[h, :, :HD] = jnp.zeros((STACK, HD), jnp.float32)

        def weigh(j, total):
            raised = jnp.exp(scores[j] - top)
            mixed[h, :, :HD] += dot(raised.astype(low), key_chunk(j, KVW + h * HD), 1, 1)
            return total + quarters(raised, jnp.add)

        total = lax.fori_loop(0, chunks, weigh, jnp.zeros((STACK, 128), jnp.float32))
        total = jnp.sum(total, axis=1, keepdims=True)
        mixed[h, :, HD : HD + 1] = top + jnp.log(total)
        out = mixed[h, :, :HD] / total
        mixed[h, :, :HD] = out
        out_t = out.T
        for g in range(GROUP):
            rows_f32[pl.ds(pl.multiple_of((h * GROUP + g) * HD, HD), HD)] = out_t[:, 128 * g : 128 * g + 128]
        return carry

    lax.fori_loop(0, 3, forward_head, 0)
    gather_step(1, 2, 1)
    lax.fori_loop(3, 5, forward_head, 0)

    def widen(goal):
        for c in range(16):
            piece = jnp.concatenate([rows_f32[pl.ds(60 * c, 60)], jnp.zeros((4, TOK), jnp.float32)], axis=0)
            goal[pl.ds(64 * c, 64)] = piece.astype(low)

    widen(mixed_t)
    settle_pairs(1)
    for where in groups:
        term = dot(weight_rows(where, pl.ds(64, 64)), mixed_t[...])
        for i in range(4):
            rows_f32[pl.ds(64 * shard(where, i), 64)] = term[64 * i : 64 * i + 64]
    residual[...] = wide_in[...] + rows_f32[...].T

    res = residual[...]
    ffn_scale = lax.rsqrt(jnp.sum(res * res, axis=-1, keepdims=True) * (1.0 / D) + epsilon)
    tokens[pl.ds(0, TOK)] = (res * ffn_scale * ffn_gain).astype(low)
    token_copy = remote(tokens.at[pl.ds(0, TOK)], tokens.at[pl.ds(TOK, TOK)], ffn_send.at[1], ffn_recv.at[1], sibling)
    out_sum[...] = jnp.zeros_like(out_sum)
    norm_sum[...] = jnp.zeros_like(norm_sum)
    cot_copy.wait_recv()
    for part in (0, 1, 2):
        settle(1, part)
    for copy in gathered:
        copy.wait_send()
    token_copy.wait_recv()

    def ffn_at(part, block, lane):
        high, slow = lax.div(block, 4), lax.rem(block, 4)
        if part == 2:
            return (lane % 4, high * 2 + lane // 4, slow, pl.ds(320, 160))
        return (slow, (lane // 4) * 2 + high, lane % 4, pl.ds(160 * part, 160))

    def ffn_chunk(j, carry):
        gate_rows, up_rows, down_rows = [
            jnp.concatenate(
                [
                    jnp.concatenate([ffn_w[ffn_at(part, 2 * j + u, lane)] for lane in range(8)], axis=1)
                    for u in (0, 1)
                ],
                axis=0,
            )
            for part in (0, 1, 2)
        ]
        both, cot_both = tokens[...], cots[...]
        gate_value = dot(both, gate_rows, 1, 1)
        up_value = dot(both, up_rows, 1, 1)
        d_hidden = dot(cot_both, down_rows, 1, 1)
        sigmoid = 1.0 / (1.0 + jnp.exp(-gate_value))
        silu = gate_value * sigmoid
        hidden = (silu * up_value).astype(low)
        d_gate = (d_hidden * up_value * sigmoid * (1.0 + gate_value * (1.0 - sigmoid))).astype(low)
        d_up = (d_hidden * silu).astype(low)
        out_sum[...] += dot(hidden, down_rows)
        norm_sum[...] += dot(d_gate, gate_rows) + dot(d_up, up_rows)
        for part, (left, right) in enumerate(((d_gate, both), (d_up, both), (hidden, cot_both))):
            term = dot(left, right, 0, 0).astype(low)
            for u in (0, 1):
                for lane in range(8):
                    ffn_w[ffn_at(part, 2 * j + u, lane)] = term[160 * u : 160 * u + 160, 128 * lane : 128 * lane + 128]
        return carry

    lax.fori_loop(0, 4, ffn_chunk, 0)
    theirs = pl.ds(TOK, TOK)
    norm_copy = remote(norm_sum.at[theirs], norm_in, ffn_send.at[2], ffn_recv.at[2], sibling)
    out_copy = remote(out_sum.at[theirs], out_in, ffn_send.at[3], ffn_recv.at[3], sibling)
    sent.extend([cot_copy, token_copy, norm_copy, out_copy])

    def slot(kind, part, stage, second, way):
        ref = slots[((kind * 3 + part) * 3 + stage) * 2 + second]
        return ref.at[way]

    def reduce_step(kind, stage, second, some=(0, 1, 2)):
        whole, lead, parts = (attn_g, (core,), ATTN_PARTS) if kind == 0 else (ffn_w, (), FFN_PARTS)
        for part in some:
            rows = parts[part]
            if stage < 3:
                axis, done = ORDERS[part][2 - stage], ORDERS[part][: 2 - stage]
            arrived = waiting.pop((2 + kind, part), ())
            for copy in arrived:
                copy.wait_recv()
            if arrived and not second:
                before, full = ORDERS[part][3 - stage], ORDERS[part][: 3 - stage]
                add_into(
                    view(whole, lead, spot, full, before, spot[before], rows),
                    [slot(kind, part, stage - 1, 1, way) for way in range(3 if direct(kind, 3 - stage) else 2)],
                )
            if stage == 3:
                goal = attn_out if kind == 0 else ffn_out
                goal[pl.ds(rows[0], rows[1])] = whole[lead + spot + (pl.ds(rows[0], rows[1]),)].astype(jnp.float32)
                continue
            straight = direct(kind, 2 - stage)
            me = spot[axis]
            copies = []
            for way, by in enumerate((1, -1, 2) if straight else (1, -1)):
                target = device(shifted(spot, axis, by), core)
                if straight:
                    source = view(whole, lead, spot, done, axis, ring(me, by), rows)
                elif second:
                    add_into(
                        view(whole, lead, spot, done, axis, ring(me, by), rows, half=way),
                        [slot(kind, part, stage, 0, way)],
                    )
                    source = view(whole, lead, spot, done, axis, ring(me, by), rows)
                else:
                    source = view(whole, lead, spot, done, axis, ring(me, 2), rows, half=way)
                copies.append(
                    remote(
                        source, slot(kind, part, stage, 1 if straight else second, way),
                        r_send.at[kind, part, stage, second, way], r_recv.at[kind, part, stage, second, way], target,
                    )
                )
            waiting[2 + kind, part] = copies
            sent.extend(copies)

    reduce_step(1, 0, 0)
    norm_copy.wait_recv()
    d_normed = norm_sum[pl.ds(0, TOK)] + norm_in[...]
    res = residual[...]
    ffn_scale = lax.rsqrt(jnp.sum(res * res, axis=-1, keepdims=True) * (1.0 / D) + epsilon)
    ffn_gain_term = jnp.sum(d_normed * res * ffn_scale, axis=0, keepdims=True)
    gain_out[...] = exact(jnp.concatenate([jnp.zeros_like(ffn_gain_term), ffn_gain_term, jnp.zeros((6, WIDE), jnp.float32)], axis=0), pads[...], 1)
    scaled = d_normed * ffn_gain
    d_residual = cots[pl.ds(0, TOK)].astype(jnp.float32) + ffn_scale * (
        scaled - res * ffn_scale * ffn_scale * (jnp.sum(scaled * res, axis=-1, keepdims=True) * (1.0 / D))
    )
    out_copy.wait_recv()
    layer_out[...] = dot(
        pads[...], (res + out_sum[pl.ds(0, TOK)] + out_in[...]).astype(low), 1, 1
    ).astype(low)
    residual[...] = d_residual
    d_branch = d_residual.astype(low)
    d_branch_t = d_residual.T.astype(low)

    norm_sum[pl.ds(0, TOK)] = jnp.zeros((TOK, WIDE), jnp.float32)
    for where in groups:
        picked = jnp.concatenate(
            [d_branch[:, 64 * shard(where, i) : 64 * shard(where, i) + 64] for i in range(4)], axis=1
        )
        norm_sum[pl.ds(0, TOK)] += dot(picked, weight_rows(where, pl.ds(64, 64)))
    d_wide = norm_sum[pl.ds(0, TOK)].T
    for c in range(16):
        rows_f32[pl.ds(60 * c, 60)] = d_wide[64 * c : 64 * c + 60]

    def attn_grad(left_t, right, offset, count, width):
        for where in groups:
            term = dot(
                jnp.concatenate([left_t[width * shard(where, i) : width * shard(where, i) + width] for i in range(4)], axis=0),
                right,
            ).astype(low)
            y_lo, p = where
            for i in range(4):
                for f in range(8):
                    attn_g[p, i, 2 * (f // 4) + y_lo, f % 4, pl.ds(offset, count)] = term[
                        width * i : width * i + count, 128 * f : 128 * f + 128
                    ]

    gpairs = []

    def share(part):
        rows = pl.ds(*ATTN_PARTS[part])
        gpairs.append(
            remote(
                attn_g.at[1 - core, :, :, :, rows], pair_in.at[:, :, :, rows], last_send.at[part], last_recv.at[part], sibling
            )
        )

    def shared(part):
        rows = pl.ds(*ATTN_PARTS[part])
        gpairs[0].wait_recv()
        sent.append(gpairs.pop(0))

        def body(i, carry):
            at = (lax.div(i, 16), lax.rem(lax.div(i, 4), 4), lax.rem(i, 4), rows)
            goal = (core,) + at
            attn_g[goal] = (attn_g[goal].astype(jnp.float32) + pair_in[at].astype(jnp.float32)).astype(low)
            return carry

        lax.fori_loop(0, 64, body, 0)

    def d_heads(h, carry):
        pieces = [rows_f32[pl.ds(pl.multiple_of((h * GROUP + g) * HD, HD), HD)] for g in range(GROUP)]
        wide = jnp.concatenate(pieces, axis=1)
        d_mixed_t[h] = wide.astype(low)
        d_mixed[h] = wide.T.astype(low)
        return carry

    lax.fori_loop(0, KVH, d_heads, 0)
    mixed_rows = mixed_t[...].astype(jnp.float32).T.astype(low)
    attn_grad(d_branch_t, mixed_rows, 64, 64, 64)
    share(1)
    reduce_step(1, 0, 1)

    def clear(j, carry):
        key_terms[lax.div(j, 4), lax.rem(j, 4)] = jnp.zeros((2, WIDE_KV, TOK), low)
        return carry

    lax.fori_loop(2 * chunks, 8, clear, 0)

    def backward_head(h, carry):
        delta = jnp.sum(d_mixed[h].astype(jnp.float32) * mixed[h, :, :HD], axis=1, keepdims=True)
        d_query[...] = jnp.zeros_like(d_query)

        def visit(newest, j, inner):
            shares = jnp.exp(block_scores(h, j, newest) - mixed[h, :, HD : HD + 1])
            d_shares = dot(d_mixed[h], key_chunk(j, KVW + h * HD))
            d_scores = (shares * (d_shares - delta)).astype(low)
            d_query[...] += dot(d_scores, key_chunk(j, h * HD), 1, 1)
            d_key = dot(query_t[h], d_scores).astype(low)
            d_value = dot(d_mixed_t[h], shares.astype(low)).astype(low)
            y_lo, i = lax.div(j, 2), 2 * lax.rem(j, 2)
            key_rows = pl.ds(pl.multiple_of(h * HD, HD), HD)
            value_rows = pl.ds(pl.multiple_of(KVW + h * HD, HD), HD)
            for n in range(4):
                key_terms[y_lo, i + n // 2, n % 2, key_rows] = d_key[:, 128 * n : 128 * n + 128]
                key_terms[y_lo, i + n // 2, n % 2, value_rows] = d_value[:, 128 * n : 128 * n + 128]
            return inner

        visit(True, chunks - 1, 0)
        lax.fori_loop(0, chunks - 1, functools.partial(visit, False), 0)
        d_wide = d_query[...].T * (HD ** -0.5)
        for g in range(GROUP):
            at = pl.multiple_of((h * GROUP + g) * HD, HD)
            v1, v2 = turned(d_wide[:32, 128 * g : 128 * g + 128], d_wide[32:, 128 * g : 128 * g + 128], True)
            rows_f32[pl.ds(at, 32)] = v1
            rows_f32[pl.ds(pl.multiple_of(at + 32, 32), 32)] = v2
        return carry

    lax.fori_loop(0, 2, backward_head, 0)
    shared(1)
    reduce_step(0, 0, 0, (1,))
    lax.fori_loop(2, 5, backward_head, 0)

    copies = []

    def kg(source, goal, target):
        number = len(copies)
        copies.append(remote(source, goal, kg_send.at[number], kg_recv.at[number], target))
        return copies[-1]

    for by in (2, 1, 3, 0):
        for h in (0, 1):
            kg(key_terms.at[h, ring(x, by), 1 - core], key_pair.at[h, ring(x, by)], sibling)

    def add(goal, *sources):
        total = goal[...].astype(jnp.float32)
        for source in sources:
            total += source[...].astype(jnp.float32)
        goal[...] = total.astype(low)

    def block(h, at):
        return key_terms.at[h, at, core]

    widen(d_query_t)
    for h in (0, 1):
        copies[h].wait_recv()
        add(block(h, ring(x, 2)), key_pair.at[h, ring(x, 2)])
    far = [kg(block(way, ring(x, 2)), key_far.at[way], neighbours[way]) for way in (0, 1)]
    attn_grad(d_query_t[...], normed[...], 0, 64, 64)
    for copy in copies[2:8]:
        copy.wait_recv()
    share(0)
    for by in (1, 3, 0):
        for h in (0, 1):
            add(block(h, ring(x, by)), key_pair.at[h, ring(x, by)])
    reduce_step(1, 1, 0)
    for way, by in enumerate((1, -1)):
        far[way].wait_recv()
        add(block(way, ring(x, by)), key_far.at[way])
    near = [
        kg(block(h, ring(x, by)), key_near.at[way, h], neighbours[way])
        for h in (1 - half, half)
        for way, by in enumerate((1, -1))
    ]
    reduce_step(0, 0, 1, (1,))
    for copy in near[:2]:
        copy.wait_recv()
    add(block(1 - half, x), key_near.at[0, 1 - half], key_near.at[1, 1 - half])
    final = kg(block(1 - half, x), key_across, across)
    reduce_step(1, 1, 1)
    shared(0)
    reduce_step(0, 0, 0, (0,))
    for copy in near[2:]:
        copy.wait_recv()
    add(block(half, x), key_near.at[0, half], key_near.at[1, half])
    reduce_step(1, 2, 0)
    norm_sum[pl.ds(0, TOK)] = jnp.zeros((TOK, WIDE), jnp.float32)

    def back_through(left_t, width, offset):
        for where in groups:
            picked = jnp.concatenate(
                [left_t[width * shard(where, i) : width * shard(where, i) + width] for i in range(4)], axis=0
            )
            norm_sum[pl.ds(0, TOK)] += dot(picked, weight_rows(where, pl.ds(offset, width)), 0, 0)

    back_through(d_query_t[...], 64, 0)
    final.wait_recv()
    sent.extend(copies)
    rows_f32[pl.ds(0, WIDE_KV)] = key_terms[half, x, core].astype(jnp.float32) + key_across[...].astype(jnp.float32)
    for h in range(KVH):
        v1, v2 = turned(rows_f32[pl.ds(64 * h, 32)], rows_f32[pl.ds(64 * h + 32, 32)], True)
        rows_f32[pl.ds(64 * h, 32)] = v1
        rows_f32[pl.ds(64 * h + 32, 32)] = v2
    for c in range(16):
        d_key_t[pl.ds(48 * c, 48)] = jnp.concatenate(
            [
                rows_f32[pl.ds(20 * c, 20)],
                rows_f32[pl.ds(KVW + 20 * c, 20)],
                jnp.zeros((8, TOK), jnp.float32),
            ],
            axis=0,
        ).astype(low)
    attn_grad(d_key_t[...], normed[...], 128, 48, 48)
    share(2)
    back_through(d_key_t[...], 48, 128)
    d_normed = norm_sum[pl.ds(0, TOK)]
    tok = wide_in[...]
    attn_scale = lax.rsqrt(jnp.sum(tok * tok, axis=-1, keepdims=True) * (1.0 / D) + epsilon)
    attn_gain_term = jnp.sum(d_normed * tok * attn_scale, axis=0, keepdims=True)
    gain_out[...] = gain_out[...] + exact(
        jnp.concatenate([attn_gain_term, jnp.zeros((7, WIDE), jnp.float32)], axis=0), pads[...], 1
    )

    def gain_start(axis):
        me = spot[axis]
        gain_slots[axis, me] = gain_out[...]
        own = gain_slots.at[axis, me]
        return [
            remote(own, own, gain_send.at[axis, by - 1], gain_recv.at[axis, by - 1], device(shifted(spot, axis, by), core))
            for by in (1, 2, 3)
        ]

    def gain_end(axis, started):
        for copy in started:
            copy.wait_recv()
        sent.extend(started)
        gain_out[...] = (gain_slots[axis, 0] + gain_slots[axis, 1]) + (gain_slots[axis, 2] + gain_slots[axis, 3])

    gains = gain_start(0)
    shared(2)
    reduce_step(0, 0, 0, (2,))
    reduce_step(0, 0, 1, (0,))
    reduce_step(0, 1, 0, (1,))
    gain_end(0, gains)
    gains = gain_start(1)
    reduce_step(0, 0, 1, (2,))
    scaled = d_normed * attn_gain
    d_input = residual[...] + attn_scale * (
        scaled - tok * attn_scale * attn_scale * (jnp.sum(scaled * tok, axis=-1, keepdims=True) * (1.0 / D))
    )
    input_grad[...] = dot(pads[...], d_input.astype(low), 1, 1).astype(low)
    reduce_step(0, 1, 0, (0,))
    reduce_step(0, 2, 0, (1,))
    gain_end(1, gains)
    gains = gain_start(2)
    reduce_step(0, 1, 0, (2,))
    reduce_step(1, 3, 0)
    down_back = remote(ffn_out.at[pl.ds(320, 160)], down_out, down_sem.at[2], down_sem.at[3], sibling)
    sent.append(down_back)
    reduce_step(0, 2, 0, (0,))

    def narrow(ref, low_row, rows):
        return exact(ref[pl.ds(low_row, rows)], columns_of, 1)

    gain_end(2, gains)
    gain_slots[3, core] = gain_out[...]
    own = gain_slots.at[3, core]
    joined = remote(own, own, last_send.at[3], last_recv.at[3], sibling)
    sent.append(joined)
    gate_grad[...] = narrow(ffn_out, 0, 160)
    up_grad[...] = narrow(ffn_out, 160, 160)
    reduce_step(0, 2, 0, (2,))
    reduce_step(0, 3, 0, (1, 0))
    query_grad[...] = narrow(attn_out, 0, 64)[:60]
    proj_grad[...] = narrow(attn_out, 64, 64)[:60]
    down_back.wait_recv()
    mine_down, their_down = ffn_out[pl.ds(320, 160)], down_out[...]
    all_down = jnp.concatenate(
        [jnp.where(core == 0, mine_down, their_down), jnp.where(core == 0, their_down, mine_down)], axis=0
    ).T
    down_grad[...] = jnp.where(core == 0, all_down[:64], all_down[64:])[:60]
    joined.wait_recv()
    gain_sums[...] = gain_slots[3, 0] + gain_slots[3, 1]
    reduce_step(0, 3, 0, (2,))
    both_grads = narrow(attn_out, 128, 48)
    key_grad[...] = both_grads[:20]
    value_grad[...] = both_grads[20:40]
    for copy in sent:
        copy.wait_send()


def run_layer(*operands):
    low, wide = jnp.bfloat16, jnp.float32
    slots = []
    for kind, parts in enumerate((ATTN_PARTS, FFN_PARTS)):
        for rows in parts:
            for stage, (half, full) in enumerate(reduce_shapes(rows)):
                if 2 - stage < 2 - kind:
                    slots += [pltpu.VMEM((16, 128), low), pltpu.VMEM((3,) + full + (128,), low)]
                else:
                    slots += [pltpu.VMEM((2,) + half + (128,), low), pltpu.VMEM((2,) + full + (128,), low)]
    dma = pltpu.SemaphoreType.DMA
    return pl.pallas_call(
        layer_kernel,
        out_shape=[jax.ShapeDtypeStruct((D, TOK), low)] * 2
        + [
            jax.ShapeDtypeStruct(shape, wide)
            for shape in ((60, 120), (20, 120), (20, 120), (60, 120), (160, 120), (160, 120), (60, 320), (8, D))
        ],
        in_specs=[pl.BlockSpec(memory_space=pltpu.SMEM) if i == 1 else VMEM for i in range(len(operands))],
        out_specs=[VMEM] * 10,
        scratch_shapes=[
            pltpu.VMEM((2, 4, 4, 4, ATTN_ROWS, 128), low),
            pltpu.VMEM((4, 4, 4, FFN_ROWS, 128), low),
            pltpu.VMEM((ATTN_ROWS, 128), low),
            pltpu.VMEM((FFN_ROWS, 128), low),
            pltpu.VMEM((160, 128), low),
            pltpu.VMEM((160, 128), low),
            pltpu.VMEM((D, WIDE), low),
            pltpu.VMEM((TOK, WIDE), wide),
            pltpu.VMEM((8, WIDE), wide),
            pltpu.VMEM((HD // 2, TOK), wide),
            pltpu.VMEM((HD // 2, TOK), wide),
            pltpu.VMEM((4, 16, 512), low),
            pltpu.VMEM((ATTN_ROWS, 128), wide),
            pltpu.VMEM((FFN_ROWS, 128), wide),
            pltpu.VMEM((160, 128), wide),
            pltpu.VMEM((8, D), wide),
            pltpu.VMEM((TOK, WIDE), low),
            pltpu.VMEM((WIDE, TOK), low),
            pltpu.VMEM((WIDE, TOK), wide),
            pltpu.VMEM((KVH, HD, STACK), low),
            pltpu.VMEM((KVH, STACK, HD + 16), low),
            pltpu.VMEM((WIDE_KV, TOK), low),
            pltpu.VMEM((2, 4, 2, WIDE_KV, TOK), low),
            pltpu.VMEM((4, STACK, 512), wide),
            pltpu.VMEM((KVH, STACK, 128), wide),
            pltpu.VMEM((WIDE, TOK), low),
            pltpu.VMEM((TOK, WIDE), wide),
            pltpu.VMEM((2 * TOK, WIDE), low),
            pltpu.VMEM((2 * TOK, WIDE), low),
            pltpu.VMEM((2 * TOK, WIDE), wide),
            pltpu.VMEM((2 * TOK, WIDE), wide),
            pltpu.VMEM((TOK, WIDE), wide),
            pltpu.VMEM((TOK, WIDE), wide),
            pltpu.VMEM((KVH, HD, STACK), low),
            pltpu.VMEM((KVH, STACK, HD), low),
            pltpu.VMEM((STACK, HD), wide),
            pltpu.VMEM((WIDE, TOK), low),
            pltpu.VMEM((2, 4, 2, WIDE_KV, TOK), low),
            pltpu.VMEM((2, 4, WIDE_KV, TOK), low),
            pltpu.VMEM((2, WIDE_KV, TOK), low),
            pltpu.VMEM((2, 2, WIDE_KV, TOK), low),
            pltpu.VMEM((WIDE_KV, TOK), low),
            pltpu.VMEM((768, TOK), low),
            pltpu.VMEM((2, 4, 4, 4, ATTN_ROWS, 128), low),
            pltpu.VMEM((4, 4, 4, ATTN_ROWS, 128), low),
            pltpu.VMEM((4, 4, 8, D), wide),
        ]
        + slots
        + [
            dma((2, 3, 3, 2, 3)),
            dma((2, 3, 3, 2, 3)),
            dma((2,)),
            dma((4,)),
            dma((3, 4)),
            dma((3, 4)),
            dma,
            dma((7,)),
            dma((7,)),
            dma((8,)),
            dma((8,)),
            dma((4,)),
            dma((4,)),
            dma((15,)),
            dma((15,)),
            dma((2, 3, 3, 2, 3)),
            dma((2, 3, 3, 2, 3)),
            dma((3, 3)),
            dma((3, 3)),
            dma((4,)),
            dma((4,)),
        ],
        compiler_params=pltpu.CompilerParams(collective_id=1, has_side_effects=True, vmem_limit_bytes=63 * MIB),
        name="layer",
    )(*operands)


def deliver_kernel(count, *refs):
    for i in range(count):
        refs[count + 1 + i][...] = refs[i][...]
    for i in (0, 1):
        refs[2 * count + 1 + i][...] = refs[count][i : i + 1, :]


def deliver(arrays, gains):
    count = len(arrays)
    return pl.pallas_call(
        functools.partial(deliver_kernel, count),
        out_shape=[jax.ShapeDtypeStruct(a.shape, a.dtype) for a in arrays] + [jax.ShapeDtypeStruct((1, D), gains.dtype)] * 2,
        in_specs=[VMEM] * (count + 1),
        out_specs=[VMEM] * (count + 2),
        name="deliver",
    )(*arrays, gains)


def per_device(
    inputs, doc_offsets, attn_gain, query_weight, key_weight, value_weight, proj_weight,
    ffn_gain, gate_weight, up_weight, down_weight, cotangent,
):
    *results, gain_sums = run_layer(
        inputs[0].T, doc_offsets, attn_gain[None], ffn_gain[None], query_weight.T, key_weight.T, value_weight.T,
        proj_weight.T, gate_weight.T, up_weight.T, down_weight.T, cotangent[0].T,
    )
    layer_out, input_grad, query_g, key_g, value_g, proj_g, gate_g, up_g, down_g, attn_gain_g, ffn_gain_g = deliver(
        results, gain_sums
    )
    return (
        layer_out.T[None], input_grad.T[None], attn_gain_g[0], query_g.T, key_g.T, value_g.T, proj_g.T,
        ffn_gain_g[0], gate_g.T, up_g.T, down_g.T,
    )


def solution(mesh):
    split = P("fsdp", "ctx")
    rows = P("fsdp", "ctx", None)
    return jax.shard_map(
        per_device,
        mesh=mesh,
        in_specs=(rows, P("fsdp", None), P(), split, split, split, split, P(), split, split, split, rows),
        out_specs=(rows, rows, P(), split, split, split, split, P(), split, split, split),
        check_vma=False,
    )
```

```python
import functools

import jax
import jax.numpy as jnp
from jax import lax
from jax.experimental import pallas as pl
from jax.experimental.pallas import tpu as pltpu
from jax.sharding import PartitionSpec as P

D = 960
HEADS = 15
KVH = 5
HD = 64
NDOC = 4
KVW = 320
WIDE = 1024
TOK = 128

GROUP = HEADS // KVH
STACK = GROUP * TOK
WIDE_KV = 2 * KVW

epsilon = 1e-05
masked_score = -1e30

MESH = pl.DeviceIdType.MESH
ANY = pl.BlockSpec(memory_space=pl.ANY)
VMEM = pl.BlockSpec(memory_space=pltpu.VMEM)
MIB = 1024 * 1024

ATTN_PARTS = ((0, 64), (64, 64), (128, 48))
ATTN_ROWS = 176
FFN_PARTS = ((0, 160), (160, 160), (320, 160))
FFN_ROWS = 480
ORDERS = ((0, 1, 2), (1, 2, 0), (2, 0, 1))


def place():
    c = lax.axis_index("ctx")
    f = lax.axis_index("fsdp")
    x = lax.rem(lax.div(c, 2), 4)
    y = lax.div(f, 4) * 2 + lax.div(c, 8)
    return (x, y, lax.rem(f, 4)), lax.rem(c, 2)


def device(spot, core):
    x, y, z = spot
    return ((lax.rem(y, 2) * 4 + x) * 2 + core, lax.div(y, 2) * 4 + z)


def ring(value, by):
    return lax.rem(value + by + 4, 4)


def shifted(spot, axis, by):
    return tuple(ring(v, by) if i == axis else v for i, v in enumerate(spot))


def greet(devices):
    barrier = pltpu.get_barrier_semaphore()
    for target in devices:
        pl.semaphore_signal(barrier, inc=1, device_id=target, device_id_type=MESH)
    pl.semaphore_wait(barrier, len(devices))


def remote(src, dst, send, recv, target):
    copy = pltpu.make_async_remote_copy(
        src_ref=src, dst_ref=dst, send_sem=send, recv_sem=recv, device_id=target, device_id_type=MESH
    )
    copy.start()
    return copy


def view(ref, lead, spot, done, axis, position, rows, half=None):
    index = []
    cut = min(done) if (half is not None and done) else None
    for a in range(3):
        if a == cut:
            index.append(pl.ds(2 * half, 2))
        elif a in done:
            index.append(pl.ds(0, 4))
        elif a == axis:
            index.append(position)
        else:
            index.append(spot[a])
    low, count = rows
    if half is not None and not done:
        first = (count // 32) * 16
        low, count = (low, first) if half == 0 else (low + first, count - first)
    return ref.at[tuple(lead) + tuple(index) + (pl.ds(low, count),)]


def add_into(target, terms):
    lead = target.shape[:-2]
    if not lead:
        total = target[...].astype(jnp.float32)
        for term in terms:
            total += term[...].astype(jnp.float32)
        target[...] = total.astype(target.dtype)
        return
    inner = lead[1] if len(lead) == 2 else 1

    def body(i, carry):
        at = (lax.div(i, inner), lax.rem(i, inner)) if len(lead) == 2 else (i,)
        total = target[at].astype(jnp.float32)
        for term in terms:
            total += term[at].astype(jnp.float32)
        target[at] = total.astype(target.dtype)
        return carry

    lax.fori_loop(0, lead[0] * inner, body, 0)


def reduce_shapes(rows):
    count = rows[1]
    first = (count // 32) * 16
    return (
        ((2, 4, count), (4, 4, count)),
        ((2, count), (4, count)),
        ((count - first,), (count,)),
    )


def dot(left, right, left_dim=1, right_dim=0):
    return lax.dot_general(left, right, (((left_dim,), (right_dim,)), ((), ())), preferred_element_type=jnp.float32)


def layer_kernel(
    inputs, doc_offsets, attn_gain_in, ffn_gain_in, query_weight, key_weight, value_weight, proj_weight, gate_weight, up_weight, down_weight, cotangent,
    layer_out, input_grad, query_grad, key_grad, value_grad, proj_grad, gate_grad, up_grad, down_grad, gain_sums,
    attn_w, ffn_w, attn_block, ffn_own, down_away, down_in, pads, wide_in, gain_rows, cosine, sine, segments,
    attn_out, ffn_out, down_out, gain_out,
    normed, normed_t, rows_f32, query_t, query, key_own, keys, scores, mixed, mixed_t, residual,
    tokens, cots, out_sum, norm_sum, out_in, norm_in,
    d_mixed_t, d_mixed, d_query, d_query_t, key_terms, key_pair, key_far, key_near, key_across, d_key_t,
    attn_g, pair_in, gain_slots,
    *scratch,
):
    slots = scratch[:36]
    (
        send, recv, own_sem, down_sem, pair_send, pair_recv,
        key_own_sem, key_send, key_recv, kpair_send, kpair_recv,
        ffn_send, ffn_recv, kg_send, kg_recv, r_send, r_recv, gain_send, gain_recv, last_send, last_recv,
    ) = scratch[36:]
    low = jnp.bfloat16
    spot, core = place()
    x, y, z = spot
    half = lax.rem(y, 2)
    sibling = device(spot, 1 - core)
    across = device((x, y + 1 - 2 * half, z), core)
    chunks = half * 2 + lax.div(x, 2) + 1
    sent = []

    def hot(rows, columns, shift):
        row = lax.broadcasted_iota(jnp.int32, (rows, columns), 0)
        column = lax.broadcasted_iota(jnp.int32, (rows, columns), 1)
        return column == row + shift(row)

    by_sixty = lambda row: lax.shift_right_logical(row * 1093, 16) * 4
    columns_of = hot(120, 128, by_sixty).astype(low)
    zeros = lambda rows: jnp.zeros((rows, 128), jnp.float32)
    turn = lambda ref: dot(ref[...], columns_of)
    attn_block[pl.ds(128, 48)] = jnp.concatenate([turn(key_weight), turn(value_weight), zeros(8)], axis=0).astype(low)
    attn_block[pl.ds(0, 64)] = jnp.concatenate([turn(query_weight), zeros(4)], axis=0).astype(low)
    attn_block[pl.ds(64, 64)] = jnp.concatenate([turn(proj_weight), zeros(4)], axis=0).astype(low)
    ffn_own[pl.ds(0, 160)] = turn(gate_weight).astype(low)
    ffn_own[pl.ds(160, 160)] = turn(up_weight).astype(low)
    placed = hot(60, 128, lambda row: 64 * core).astype(low)
    down_both = dot(down_weight[...], placed, 0, 0)
    down_away[...] = jnp.where(core == 0, down_both[160:], down_both[:160]).astype(low)
    ffn_own[pl.ds(320, 160)] = jnp.where(core == 0, down_both[:160], down_both[160:]).astype(low)

    greet([device(shifted(spot, a, by), core) for a in range(3) for by in (1, 2, 3)] + [sibling])
    down_copy = remote(down_away, down_in, down_sem.at[0], down_sem.at[1], sibling)
    sent.append(down_copy)
    own_attn = pltpu.make_async_copy(attn_block, attn_w.at[core, x, y, z], own_sem.at[0])
    own_attn.start()
    waiting, gathered, paired = {}, [], {}

    def pass_on(part, number, position):
        order = ORDERS[part]
        piece = view(attn_w, (core,), spot, order[:2], order[2], position, ATTN_PARTS[part])
        paired[part, number] = remote(piece, piece, pair_send.at[part, number], pair_recv.at[part, number], sibling)

    def direct(kind, stage):
        return stage < 2 - kind

    def gather_step(kind, stage, second, some=(2, 0, 1)):
        for part in some:
            axis, done = ORDERS[part][stage], ORDERS[part][:stage]
            if kind == 0:
                whole, lead, rows, block = attn_w, (core,), ATTN_PARTS[part], attn_block
            else:
                whole, lead, rows, block = ffn_w, (), FFN_PARTS[part], ffn_own
            for copy in waiting.pop((kind, part), ()):
                copy.wait_recv()
            me = spot[axis]
            copies = []
            for way, by in enumerate((1, -1, 2) if direct(kind, stage) else (1, -1)):
                target = device(shifted(spot, axis, by), core)
                if second:
                    source = goal = view(whole, lead, spot, done, axis, ring(me, -by), rows, half=way)
                else:
                    source = goal = view(whole, lead, spot, done, axis, me, rows)
                    if stage == 0:
                        source = block.at[pl.ds(rows[0], rows[1])]
                copies.append(
                    remote(
                        source, goal,
                        send.at[kind, part, stage, second, way], recv.at[kind, part, stage, second, way], target,
                    )
                )
            waiting[kind, part] = copies
            (sent if kind == 0 else gathered).extend(copies)
            if kind == 0 and stage == 2:
                if second:
                    pass_on(part, 1, ring(me, 1))
                    pass_on(part, 2, ring(me, -1))
                else:
                    pass_on(part, 0, me)

    def settle(kind, part):
        for copy in waiting.pop((kind, part), ()):
            copy.wait_recv()

    gather_step(0, 0, 0)

    def fill_pads(i, carry):
        start = pl.multiple_of(i * 160, 160)
        pads[pl.ds(start, 160)] = hot(160, WIDE, lambda row: start + by_sixty(row + start)).astype(low)
        return carry

    lax.fori_loop(0, 6, fill_pads, 0)
    wide_in[...] = dot(inputs[...], pads[...], 0, 0)
    cots[pl.ds(0, TOK)] = dot(cotangent[...], pads[...], 0, 0).astype(low)
    cot_copy = remote(cots.at[pl.ds(0, TOK)], cots.at[pl.ds(TOK, TOK)], ffn_send.at[0], ffn_recv.at[0], sibling)

    def exact(array, places, dim):
        total = jnp.zeros((), jnp.float32)
        for _ in range(3):
            piece = array.astype(low)
            array = array - piece.astype(jnp.float32)
            total = total + dot(piece, places, 1, dim)
        return total

    gain_rows[...] = exact(
        jnp.concatenate([attn_gain_in[...], ffn_gain_in[...], jnp.zeros((6, D), jnp.float32)], axis=0), pads[...], 0
    )
    attn_gain, ffn_gain = gain_rows[0:1, :], gain_rows[1:2, :]
    down_copy.wait_recv()
    ffn_own[pl.ds(320, 160)] = ffn_own[pl.ds(320, 160)] + down_in[...]
    own_ffn = pltpu.make_async_copy(ffn_own, ffn_w.at[x, y, z], own_sem.at[1])
    own_ffn.start()
    own_attn.wait()
    gather_step(0, 1, 0)
    gather_step(1, 0, 0)
    tok = wide_in[...]
    attn_scale = lax.rsqrt(jnp.sum(tok * tok, axis=-1, keepdims=True) * (1.0 / D) + epsilon)
    wide_normed = tok * attn_scale * attn_gain
    normed[...] = wide_normed.astype(low)
    normed_t[...] = wide_normed.T.astype(low)
    own_ffn.wait()
    gather_step(0, 2, 0)
    gather_step(1, 1, 0)

    first_row = (half * 8 + x * 2 + core) * TOK

    def document(index):
        number, start = jnp.zeros_like(index), jnp.zeros_like(index)
        for i in range(1, NDOC):
            after = index >= doc_offsets[0, i]
            number += jnp.where(after, 1, 0)
            start = jnp.where(after, doc_offsets[0, i], start)
        return number, start

    table_token = first_row + lax.broadcasted_iota(jnp.int32, (HD // 2, TOK), 1)
    row = lax.broadcasted_iota(jnp.int32, (HD // 2, TOK), 0)
    rates = jnp.zeros((HD // 2, TOK), jnp.float32)
    for i in range(HD // 2):
        rates = jnp.where(row == i, 10000.0 ** (-2.0 * i / HD), rates)
    angles = (table_token - document(table_token)[1]).astype(jnp.float32) * rates
    cosine[...] = jnp.cos(angles)
    sine[...] = jnp.sin(angles)
    row = lax.broadcasted_iota(jnp.int32, (16, 512), 0)
    for j in range(4):
        number = document(512 * j + lax.broadcasted_iota(jnp.int32, (16, 512), 1))[0]
        segments[j] = jnp.where(number == row, 1.0, 0.0).astype(low)
    row = lax.broadcasted_iota(jnp.int32, (16, STACK), 0)
    own_token = first_row + jnp.bitwise_and(lax.broadcasted_iota(jnp.int32, (16, STACK), 1), TOK - 1)
    apart = jnp.where((document(own_token)[0] != row) & (row < NDOC), masked_score, 0.0)
    last_key = first_row + jnp.bitwise_and(lax.broadcasted_iota(jnp.int32, (STACK, 512), 0), TOK - 1)

    gather_step(0, 2, 1)
    for part in (2, 0, 1):
        settle(0, part)
        pass_on(part, 3, ring(spot[ORDERS[part][2]], 2))
    sent.extend(paired.values())

    def settle_pairs(part):
        for number in range(4):
            paired[part, number].wait_recv()

    def weight_rows(where, rows):
        y_lo, p = where
        return jnp.concatenate(
            [
                jnp.concatenate([attn_w[p, i, 2 * (f // 4) + y_lo, f % 4, rows] for f in range(8)], axis=1)
                for i in range(4)
            ],
            axis=0,
        )

    groups = [(y_lo, p) for y_lo in (0, 1) for p in (0, 1)]

    def shard(where, i):
        return (where[0] * 4 + i) * 2 + where[1]

    def turned(v1, v2, back):
        c, s = cosine[...], (-sine[...] if back else sine[...])
        return v1 * c - v2 * s, v2 * c + v1 * s

    gather_step(1, 1, 1)
    settle_pairs(2)
    for where in groups:
        term = dot(weight_rows(where, pl.ds(128, 48)), normed_t[...])
        for i in range(4):
            c = shard(where, i)
            rows_f32[pl.ds(20 * c, 20)] = term[48 * i : 48 * i + 20]
            rows_f32[pl.ds(KVW + 20 * c, 20)] = term[48 * i + 20 : 48 * i + 40]
    for h in range(KVH):
        v1, v2 = turned(rows_f32[pl.ds(64 * h, 32)], rows_f32[pl.ds(64 * h + 32, 32)], False)
        key_own[pl.ds(64 * h, 32)] = v1.astype(low)
        key_own[pl.ds(64 * h + 32, 32)] = v2.astype(low)
    key_own[pl.ds(KVW, KVW)] = rows_f32[pl.ds(KVW, KVW)].astype(low)

    mine = keys.at[half, x, core]
    own_keys = pltpu.make_async_copy(key_own, mine, key_own_sem)
    own_keys.start()
    kpairs = []

    def pass_keys(ref):
        kpairs.append(remote(ref, ref, kpair_send.at[len(kpairs)], kpair_recv.at[len(kpairs)], sibling))

    def key_copy(source, goal, number, target):
        return remote(source, goal, key_send.at[number], key_recv.at[number], target)

    neighbours = [device(shifted(spot, 0, by), core) for by in (1, -1)]
    over = key_copy(key_own, mine, 0, across)
    first = [key_copy(key_own, mine, 1 + way, neighbours[way]) for way in (0, 1)]
    kpairs.append(remote(key_own, mine, kpair_send.at[0], kpair_recv.at[0], sibling))

    settle_pairs(0)
    for where in groups:
        term = dot(weight_rows(where, pl.ds(0, 64)), normed_t[...])
        for i in range(4):
            rows_f32[pl.ds(60 * shard(where, i), 60)] = term[64 * i : 64 * i + 60]

    gather_step(1, 2, 0, (0,))
    over.wait_recv()
    other = keys.at[1 - half, x, core]
    second = [key_copy(other, other, 3 + way, neighbours[way]) for way in (0, 1)]
    pass_keys(other)

    def heads(h, carry):
        pieces = []
        for g in range(GROUP):
            at = pl.multiple_of((h * GROUP + g) * HD, HD)
            v1, v2 = turned(rows_f32[pl.ds(at, 32)], rows_f32[pl.ds(pl.multiple_of(at + 32, 32), 32)], False)
            pieces.append(jnp.concatenate([v1, v2], axis=0) * (HD ** -0.5))
        wide = jnp.concatenate(pieces, axis=1)
        query_t[h] = wide.astype(low)
        query[h] = jnp.concatenate([wide, apart], axis=0).T.astype(low)
        return carry

    gather_step(1, 2, 0, (2,))
    lax.fori_loop(0, KVH, heads, 0)

    last = []
    for way, by in enumerate((1, -1)):
        first[way].wait_recv()
        ref = keys.at[half, ring(x, -by), core]
        if way == 0:
            last.append(key_copy(ref, ref, 5, neighbours[0]))
        pass_keys(ref)
    for way, by in enumerate((1, -1)):
        second[way].wait_recv()
        ref = keys.at[1 - half, ring(x, -by), core]
        if way == 1:
            last.append(key_copy(ref, ref, 6, neighbours[1]))
        pass_keys(ref)
    gather_step(1, 2, 0, (1,))
    for h in (0, 1):
        last[h].wait_recv()
        pass_keys(keys.at[(half, 1 - half)[h], ring(x, 2), core])
    own_keys.wait()
    for copy in kpairs:
        copy.wait_recv()
    sent.extend([over] + first + second + last + kpairs)

    def key_chunk(j, at):
        rows = pl.ds(pl.multiple_of(at, HD), HD)
        y_lo, i = lax.div(j, 2), 2 * lax.rem(j, 2)
        return jnp.concatenate([keys[y_lo, i + n // 2, n % 2, rows, :] for n in range(4)], axis=1)

    def block_scores(h, j, newest):
        block = dot(query[h], jnp.concatenate([key_chunk(j, h * HD), segments[j]], axis=0))
        if newest:
            index = j * 512 + lax.broadcasted_iota(jnp.int32, (STACK, 512), 1)
            block = jnp.where(index <= last_key, block, masked_score)
        return block

    def quarters(block, joined):
        return joined(
            joined(block[:, :128], block[:, 128:256]), joined(block[:, 256:384], block[:, 384:])
        )

    def forward_head(h, carry):
        def tops(newest, j, top):
            block = block_scores(h, j, newest)
            scores[j] = block
            return jnp.maximum(top, quarters(block, jnp.maximum))

        top = tops(True, chunks - 1, jnp.full((STACK, 128), masked_score, jnp.float32))
        top = lax.fori_loop(0, chunks - 1, functools.partial(tops, False), top)
        top = jnp.max(top, axis=1, keepdims=True)
        mixed[h, :, :HD] = jnp.zeros((STACK, HD), jnp.float32)

        def weigh(j, total):
            raised = jnp.exp(scores[j] - top)
            mixed[h, :, :HD] += dot(raised.astype(low), key_chunk(j, KVW + h * HD), 1, 1)
            return total + quarters(raised, jnp.add)

        total = lax.fori_loop(0, chunks, weigh, jnp.zeros((STACK, 128), jnp.float32))
        total = jnp.sum(total, axis=1, keepdims=True)
        mixed[h, :, HD : HD + 1] = top + jnp.log(total)
        out = mixed[h, :, :HD] / total
        mixed[h, :, :HD] = out
        out_t = out.T
        for g in range(GROUP):
            rows_f32[pl.ds(pl.multiple_of((h * GROUP + g) * HD, HD), HD)] = out_t[:, 128 * g : 128 * g + 128]
        return carry

    lax.fori_loop(0, 3, forward_head, 0)
    gather_step(1, 2, 1)
    lax.fori_loop(3, 5, forward_head, 0)

    def widen(goal):
        for c in range(16):
            piece = jnp.concatenate([rows_f32[pl.ds(60 * c, 60)], jnp.zeros((4, TOK), jnp.float32)], axis=0)
            goal[pl.ds(64 * c, 64)] = piece.astype(low)

    widen(mixed_t)
    settle_pairs(1)
    for where in groups:
        term = dot(weight_rows(where, pl.ds(64, 64)), mixed_t[...])
        for i in range(4):
            rows_f32[pl.ds(64 * shard(where, i), 64)] = term[64 * i : 64 * i + 64]
    residual[...] = wide_in[...] + rows_f32[...].T

    res = residual[...]
    ffn_scale = lax.rsqrt(jnp.sum(res * res, axis=-1, keepdims=True) * (1.0 / D) + epsilon)
    tokens[pl.ds(0, TOK)] = (res * ffn_scale * ffn_gain).astype(low)
    token_copy = remote(tokens.at[pl.ds(0, TOK)], tokens.at[pl.ds(TOK, TOK)], ffn_send.at[1], ffn_recv.at[1], sibling)
    out_sum[...] = jnp.zeros_like(out_sum)
    norm_sum[...] = jnp.zeros_like(norm_sum)
    cot_copy.wait_recv()
    for part in (0, 1, 2):
        settle(1, part)
    for copy in gathered:
        copy.wait_send()
    token_copy.wait_recv()

    def ffn_at(part, block, lane):
        high, slow = lax.div(block, 4), lax.rem(block, 4)
        if part == 2:
            return (lane % 4, high * 2 + lane // 4, slow, pl.ds(320, 160))
        return (slow, (lane // 4) * 2 + high, lane % 4, pl.ds(160 * part, 160))

    def ffn_chunk(j, carry):
        gate_rows, up_rows, down_rows = [
            jnp.concatenate(
                [
                    jnp.concatenate([ffn_w[ffn_at(part, 2 * j + u, lane)] for lane in range(8)], axis=1)
                    for u in (0, 1)
                ],
                axis=0,
            )
            for part in (0, 1, 2)
        ]
        both, cot_both = tokens[...], cots[...]
        gate_value = dot(both, gate_rows, 1, 1)
        up_value = dot(both, up_rows, 1, 1)
        d_hidden = dot(cot_both, down_rows, 1, 1)
        sigmoid = 1.0 / (1.0 + jnp.exp(-gate_value))
        silu = gate_value * sigmoid
        hidden = (silu * up_value).astype(low)
        d_gate = (d_hidden * up_value * sigmoid * (1.0 + gate_value * (1.0 - sigmoid))).astype(low)
        d_up = (d_hidden * silu).astype(low)
        out_sum[...] += dot(hidden, down_rows)
        norm_sum[...] += dot(d_gate, gate_rows) + dot(d_up, up_rows)
        for part, (left, right) in enumerate(((d_gate, both), (d_up, both), (hidden, cot_both))):
            term = dot(left, right, 0, 0).astype(low)
            for u in (0, 1):
                for lane in range(8):
                    ffn_w[ffn_at(part, 2 * j + u, lane)] = term[160 * u : 160 * u + 160, 128 * lane : 128 * lane + 128]
        return carry

    lax.fori_loop(0, 4, ffn_chunk, 0)
    theirs = pl.ds(TOK, TOK)
    norm_copy = remote(norm_sum.at[theirs], norm_in, ffn_send.at[2], ffn_recv.at[2], sibling)
    out_copy = remote(out_sum.at[theirs], out_in, ffn_send.at[3], ffn_recv.at[3], sibling)
    sent.extend([cot_copy, token_copy, norm_copy, out_copy])

    def slot(kind, part, stage, second, way):
        ref = slots[((kind * 3 + part) * 3 + stage) * 2 + second]
        return ref.at[way]

    def reduce_step(kind, stage, second, some=(0, 1, 2)):
        whole, lead, parts = (attn_g, (core,), ATTN_PARTS) if kind == 0 else (ffn_w, (), FFN_PARTS)
        for part in some:
            rows = parts[part]
            if stage < 3:
                axis, done = ORDERS[part][2 - stage], ORDERS[part][: 2 - stage]
            arrived = waiting.pop((2 + kind, part), ())
            for copy in arrived:
                copy.wait_recv()
            if arrived and not second:
                before, full = ORDERS[part][3 - stage], ORDERS[part][: 3 - stage]
                add_into(
                    view(whole, lead, spot, full, before, spot[before], rows),
                    [slot(kind, part, stage - 1, 1, way) for way in range(3 if direct(kind, 3 - stage) else 2)],
                )
            if stage == 3:
                goal = attn_out if kind == 0 else ffn_out
                goal[pl.ds(rows[0], rows[1])] = whole[lead + spot + (pl.ds(rows[0], rows[1]),)].astype(jnp.float32)
                continue
            straight = direct(kind, 2 - stage)
            me = spot[axis]
            copies = []
            for way, by in enumerate((1, -1, 2) if straight else (1, -1)):
                target = device(shifted(spot, axis, by), core)
                if straight:
                    source = view(whole, lead, spot, done, axis, ring(me, by), rows)
                elif second:
                    add_into(
                        view(whole, lead, spot, done, axis, ring(me, by), rows, half=way),
                        [slot(kind, part, stage, 0, way)],
                    )
                    source = view(whole, lead, spot, done, axis, ring(me, by), rows)
                else:
                    source = view(whole, lead, spot, done, axis, ring(me, 2), rows, half=way)
                copies.append(
                    remote(
                        source, slot(kind, part, stage, 1 if straight else second, way),
                        r_send.at[kind, part, stage, second, way], r_recv.at[kind, part, stage, second, way], target,
                    )
                )
            waiting[2 + kind, part] = copies
            sent.extend(copies)

    reduce_step(1, 0, 0)
    norm_copy.wait_recv()
    d_normed = norm_sum[pl.ds(0, TOK)] + norm_in[...]
    res = residual[...]
    ffn_scale = lax.rsqrt(jnp.sum(res * res, axis=-1, keepdims=True) * (1.0 / D) + epsilon)
    ffn_gain_term = jnp.sum(d_normed * res * ffn_scale, axis=0, keepdims=True)
    gain_out[...] = exact(jnp.concatenate([jnp.zeros_like(ffn_gain_term), ffn_gain_term, jnp.zeros((6, WIDE), jnp.float32)], axis=0), pads[...], 1)
    scaled = d_normed * ffn_gain
    d_residual = cots[pl.ds(0, TOK)].astype(jnp.float32) + ffn_scale * (
        scaled - res * ffn_scale * ffn_scale * (jnp.sum(scaled * res, axis=-1, keepdims=True) * (1.0 / D))
    )
    out_copy.wait_recv()
    layer_out[...] = dot(
        pads[...], (res + out_sum[pl.ds(0, TOK)] + out_in[...]).astype(low), 1, 1
    ).astype(low)
    residual[...] = d_residual
    d_branch = d_residual.astype(low)
    d_branch_t = d_residual.T.astype(low)

    norm_sum[pl.ds(0, TOK)] = jnp.zeros((TOK, WIDE), jnp.float32)
    for where in groups:
        picked = jnp.concatenate(
            [d_branch[:, 64 * shard(where, i) : 64 * shard(where, i) + 64] for i in range(4)], axis=1
        )
        norm_sum[pl.ds(0, TOK)] += dot(picked, weight_rows(where, pl.ds(64, 64)))
    d_wide = norm_sum[pl.ds(0, TOK)].T
    for c in range(16):
        rows_f32[pl.ds(60 * c, 60)] = d_wide[64 * c : 64 * c + 60]

    def attn_grad(left_t, right, offset, count, width):
        for where in groups:
            term = dot(
                jnp.concatenate([left_t[width * shard(where, i) : width * shard(where, i) + width] for i in range(4)], axis=0),
                right,
            ).astype(low)
            y_lo, p = where
            for i in range(4):
                for f in range(8):
                    attn_g[p, i, 2 * (f // 4) + y_lo, f % 4, pl.ds(offset, count)] = term[
                        width * i : width * i + count, 128 * f : 128 * f + 128
                    ]

    gpairs = []

    def share(part):
        rows = pl.ds(*ATTN_PARTS[part])
        gpairs.append(
            remote(
                attn_g.at[1 - core, :, :, :, rows], pair_in.at[:, :, :, rows], last_send.at[part], last_recv.at[part], sibling
            )
        )

    def shared(part):
        rows = pl.ds(*ATTN_PARTS[part])
        gpairs[0].wait_recv()
        sent.append(gpairs.pop(0))

        def body(i, carry):
            at = (lax.div(i, 16), lax.rem(lax.div(i, 4), 4), lax.rem(i, 4), rows)
            goal = (core,) + at
            attn_g[goal] = (attn_g[goal].astype(jnp.float32) + pair_in[at].astype(jnp.float32)).astype(low)
            return carry

        lax.fori_loop(0, 64, body, 0)

    def d_heads(h, carry):
        pieces = [rows_f32[pl.ds(pl.multiple_of((h * GROUP + g) * HD, HD), HD)] for g in range(GROUP)]
        wide = jnp.concatenate(pieces, axis=1)
        d_mixed_t[h] = wide.astype(low)
        d_mixed[h] = wide.T.astype(low)
        return carry

    lax.fori_loop(0, KVH, d_heads, 0)
    mixed_rows = mixed_t[...].astype(jnp.float32).T.astype(low)
    attn_grad(d_branch_t, mixed_rows, 64, 64, 64)
    share(1)
    reduce_step(1, 0, 1)

    def clear(j, carry):
        key_terms[lax.div(j, 4), lax.rem(j, 4)] = jnp.zeros((2, WIDE_KV, TOK), low)
        return carry

    lax.fori_loop(2 * chunks, 8, clear, 0)

    def backward_head(h, carry):
        delta = jnp.sum(d_mixed[h].astype(jnp.float32) * mixed[h, :, :HD], axis=1, keepdims=True)
        d_query[...] = jnp.zeros_like(d_query)

        def visit(newest, j, inner):
            shares = jnp.exp(block_scores(h, j, newest) - mixed[h, :, HD : HD + 1])
            d_shares = dot(d_mixed[h], key_chunk(j, KVW + h * HD))
            d_scores = (shares * (d_shares - delta)).astype(low)
            d_query[...] += dot(d_scores, key_chunk(j, h * HD), 1, 1)
            d_key = dot(query_t[h], d_scores).astype(low)
            d_value = dot(d_mixed_t[h], shares.astype(low)).astype(low)
            y_lo, i = lax.div(j, 2), 2 * lax.rem(j, 2)
            key_rows = pl.ds(pl.multiple_of(h * HD, HD), HD)
            value_rows = pl.ds(pl.multiple_of(KVW + h * HD, HD), HD)
            for n in range(4):
                key_terms[y_lo, i + n // 2, n % 2, key_rows] = d_key[:, 128 * n : 128 * n + 128]
                key_terms[y_lo, i + n // 2, n % 2, value_rows] = d_value[:, 128 * n : 128 * n + 128]
            return inner

        visit(True, chunks - 1, 0)
        lax.fori_loop(0, chunks - 1, functools.partial(visit, False), 0)
        d_wide = d_query[...].T * (HD ** -0.5)
        for g in range(GROUP):
            at = pl.multiple_of((h * GROUP + g) * HD, HD)
            v1, v2 = turned(d_wide[:32, 128 * g : 128 * g + 128], d_wide[32:, 128 * g : 128 * g + 128], True)
            rows_f32[pl.ds(at, 32)] = v1
            rows_f32[pl.ds(pl.multiple_of(at + 32, 32), 32)] = v2
        return carry

    lax.fori_loop(0, 2, backward_head, 0)
    shared(1)
    reduce_step(0, 0, 0, (1,))
    lax.fori_loop(2, 5, backward_head, 0)

    copies = []

    def kg(source, goal, target):
        number = len(copies)
        copies.append(remote(source, goal, kg_send.at[number], kg_recv.at[number], target))
        return copies[-1]

    for by in (2, 1, 3, 0):
        for h in (0, 1):
            kg(key_terms.at[h, ring(x, by), 1 - core], key_pair.at[h, ring(x, by)], sibling)

    def add(goal, *sources):
        total = goal[...].astype(jnp.float32)
        for source in sources:
            total += source[...].astype(jnp.float32)
        goal[...] = total.astype(low)

    def block(h, at):
        return key_terms.at[h, at, core]

    widen(d_query_t)
    for h in (0, 1):
        copies[h].wait_recv()
        add(block(h, ring(x, 2)), key_pair.at[h, ring(x, 2)])
    far = [kg(block(way, ring(x, 2)), key_far.at[way], neighbours[way]) for way in (0, 1)]
    attn_grad(d_query_t[...], normed[...], 0, 64, 64)
    for copy in copies[2:8]:
        copy.wait_recv()
    share(0)
    for by in (1, 3, 0):
        for h in (0, 1):
            add(block(h, ring(x, by)), key_pair.at[h, ring(x, by)])
    reduce_step(1, 1, 0)
    for way, by in enumerate((1, -1)):
        far[way].wait_recv()
        add(block(way, ring(x, by)), key_far.at[way])
    near = [
        kg(block(h, ring(x, by)), key_near.at[way, h], neighbours[way])
        for h in (1 - half, half)
        for way, by in enumerate((1, -1))
    ]
    reduce_step(1, 1, 1)
    reduce_step(0, 0, 1, (1,))
    shared(0)
    reduce_step(0, 0, 0, (0,))
    for copy in near[:2]:
        copy.wait_recv()
    add(block(1 - half, x), key_near.at[0, 1 - half], key_near.at[1, 1 - half])
    final = kg(block(1 - half, x), key_across, across)
    for copy in near[2:]:
        copy.wait_recv()
    add(block(half, x), key_near.at[0, half], key_near.at[1, half])
    reduce_step(1, 2, 0)
    norm_sum[pl.ds(0, TOK)] = jnp.zeros((TOK, WIDE), jnp.float32)

    def back_through(left_t, width, offset):
        for where in groups:
            picked = jnp.concatenate(
                [left_t[width * shard(where, i) : width * shard(where, i) + width] for i in range(4)], axis=0
            )
            norm_sum[pl.ds(0, TOK)] += dot(picked, weight_rows(where, pl.ds(offset, width)), 0, 0)

    back_through(d_query_t[...], 64, 0)
    final.wait_recv()
    sent.extend(copies)
    rows_f32[pl.ds(0, WIDE_KV)] = key_terms[half, x, core].astype(jnp.float32) + key_across[...].astype(jnp.float32)
    for h in range(KVH):
        v1, v2 = turned(rows_f32[pl.ds(64 * h, 32)], rows_f32[pl.ds(64 * h + 32, 32)], True)
        rows_f32[pl.ds(64 * h, 32)] = v1
        rows_f32[pl.ds(64 * h + 32, 32)] = v2
    for c in range(16):
        d_key_t[pl.ds(48 * c, 48)] = jnp.concatenate(
            [
                rows_f32[pl.ds(20 * c, 20)],
                rows_f32[pl.ds(KVW + 20 * c, 20)],
                jnp.zeros((8, TOK), jnp.float32),
            ],
            axis=0,
        ).astype(low)
    attn_grad(d_key_t[...], normed[...], 128, 48, 48)
    share(2)
    back_through(d_key_t[...], 48, 128)
    d_normed = norm_sum[pl.ds(0, TOK)]
    tok = wide_in[...]
    attn_scale = lax.rsqrt(jnp.sum(tok * tok, axis=-1, keepdims=True) * (1.0 / D) + epsilon)
    attn_gain_term = jnp.sum(d_normed * tok * attn_scale, axis=0, keepdims=True)
    gain_out[...] = gain_out[...] + exact(
        jnp.concatenate([attn_gain_term, jnp.zeros((7, WIDE), jnp.float32)], axis=0), pads[...], 1
    )

    def gain_start(axis):
        me = spot[axis]
        gain_slots[axis, me] = gain_out[...]
        own = gain_slots.at[axis, me]
        return [
            remote(own, own, gain_send.at[axis, by - 1], gain_recv.at[axis, by - 1], device(shifted(spot, axis, by), core))
            for by in (1, 2, 3)
        ]

    def gain_end(axis, started):
        for copy in started:
            copy.wait_recv()
        sent.extend(started)
        gain_out[...] = (gain_slots[axis, 0] + gain_slots[axis, 1]) + (gain_slots[axis, 2] + gain_slots[axis, 3])

    gains = gain_start(0)
    shared(2)
    reduce_step(0, 0, 0, (2,))
    reduce_step(0, 0, 1, (0,))
    reduce_step(0, 1, 0, (1,))
    gain_end(0, gains)
    gains = gain_start(1)
    reduce_step(0, 0, 1, (2,))
    scaled = d_normed * attn_gain
    d_input = residual[...] + attn_scale * (
        scaled - tok * attn_scale * attn_scale * (jnp.sum(scaled * tok, axis=-1, keepdims=True) * (1.0 / D))
    )
    input_grad[...] = dot(pads[...], d_input.astype(low), 1, 1).astype(low)
    reduce_step(0, 1, 0, (0,))
    reduce_step(0, 2, 0, (1,))
    gain_end(1, gains)
    gains = gain_start(2)
    reduce_step(0, 1, 0, (2,))
    reduce_step(1, 3, 0)
    down_back = remote(ffn_out.at[pl.ds(320, 160)], down_out, down_sem.at[2], down_sem.at[3], sibling)
    sent.append(down_back)
    reduce_step(0, 2, 0, (0,))

    def narrow(ref, low_row, rows):
        return exact(ref[pl.ds(low_row, rows)], columns_of, 1)

    gain_end(2, gains)
    gain_slots[3, core] = gain_out[...]
    own = gain_slots.at[3, core]
    joined = remote(own, own, last_send.at[3], last_recv.at[3], sibling)
    sent.append(joined)
    gate_grad[...] = narrow(ffn_out, 0, 160)
    up_grad[...] = narrow(ffn_out, 160, 160)
    reduce_step(0, 2, 0, (2,))
    reduce_step(0, 3, 0, (1, 0))
    query_grad[...] = narrow(attn_out, 0, 64)[:60]
    proj_grad[...] = narrow(attn_out, 64, 64)[:60]
    down_back.wait_recv()
    mine_down, their_down = ffn_out[pl.ds(320, 160)], down_out[...]
    all_down = jnp.concatenate(
        [jnp.where(core == 0, mine_down, their_down), jnp.where(core == 0, their_down, mine_down)], axis=0
    ).T
    down_grad[...] = jnp.where(core == 0, all_down[:64], all_down[64:])[:60]
    joined.wait_recv()
    gain_sums[...] = gain_slots[3, 0] + gain_slots[3, 1]
    reduce_step(0, 3, 0, (2,))
    both_grads = narrow(attn_out, 128, 48)
    key_grad[...] = both_grads[:20]
    value_grad[...] = both_grads[20:40]
    for copy in sent:
        copy.wait_send()


def run_layer(*operands):
    low, wide = jnp.bfloat16, jnp.float32
    slots = []
    for kind, parts in enumerate((ATTN_PARTS, FFN_PARTS)):
        for rows in parts:
            for stage, (half, full) in enumerate(reduce_shapes(rows)):
                if 2 - stage < 2 - kind:
                    slots += [pltpu.VMEM((16, 128), low), pltpu.VMEM((3,) + full + (128,), low)]
                else:
                    slots += [pltpu.VMEM((2,) + half + (128,), low), pltpu.VMEM((2,) + full + (128,), low)]
    dma = pltpu.SemaphoreType.DMA
    return pl.pallas_call(
        layer_kernel,
        out_shape=[jax.ShapeDtypeStruct((D, TOK), low)] * 2
        + [
            jax.ShapeDtypeStruct(shape, wide)
            for shape in ((60, 120), (20, 120), (20, 120), (60, 120), (160, 120), (160, 120), (60, 320), (8, D))
        ],
        in_specs=[pl.BlockSpec(memory_space=pltpu.SMEM) if i == 1 else VMEM for i in range(len(operands))],
        out_specs=[VMEM] * 10,
        scratch_shapes=[
            pltpu.VMEM((2, 4, 4, 4, ATTN_ROWS, 128), low),
            pltpu.VMEM((4, 4, 4, FFN_ROWS, 128), low),
            pltpu.VMEM((ATTN_ROWS, 128), low),
            pltpu.VMEM((FFN_ROWS, 128), low),
            pltpu.VMEM((160, 128), low),
            pltpu.VMEM((160, 128), low),
            pltpu.VMEM((D, WIDE), low),
            pltpu.VMEM((TOK, WIDE), wide),
            pltpu.VMEM((8, WIDE), wide),
            pltpu.VMEM((HD // 2, TOK), wide),
            pltpu.VMEM((HD // 2, TOK), wide),
            pltpu.VMEM((4, 16, 512), low),
            pltpu.VMEM((ATTN_ROWS, 128), wide),
            pltpu.VMEM((FFN_ROWS, 128), wide),
            pltpu.VMEM((160, 128), wide),
            pltpu.VMEM((8, D), wide),
            pltpu.VMEM((TOK, WIDE), low),
            pltpu.VMEM((WIDE, TOK), low),
            pltpu.VMEM((WIDE, TOK), wide),
            pltpu.VMEM((KVH, HD, STACK), low),
            pltpu.VMEM((KVH, STACK, HD + 16), low),
            pltpu.VMEM((WIDE_KV, TOK), low),
            pltpu.VMEM((2, 4, 2, WIDE_KV, TOK), low),
            pltpu.VMEM((4, STACK, 512), wide),
            pltpu.VMEM((KVH, STACK, 128), wide),
            pltpu.VMEM((WIDE, TOK), low),
            pltpu.VMEM((TOK, WIDE), wide),
            pltpu.VMEM((2 * TOK, WIDE), low),
            pltpu.VMEM((2 * TOK, WIDE), low),
            pltpu.VMEM((2 * TOK, WIDE), wide),
            pltpu.VMEM((2 * TOK, WIDE), wide),
            pltpu.VMEM((TOK, WIDE), wide),
            pltpu.VMEM((TOK, WIDE), wide),
            pltpu.VMEM((KVH, HD, STACK), low),
            pltpu.VMEM((KVH, STACK, HD), low),
            pltpu.VMEM((STACK, HD), wide),
            pltpu.VMEM((WIDE, TOK), low),
            pltpu.VMEM((2, 4, 2, WIDE_KV, TOK), low),
            pltpu.VMEM((2, 4, WIDE_KV, TOK), low),
            pltpu.VMEM((2, WIDE_KV, TOK), low),
            pltpu.VMEM((2, 2, WIDE_KV, TOK), low),
            pltpu.VMEM((WIDE_KV, TOK), low),
            pltpu.VMEM((768, TOK), low),
            pltpu.VMEM((2, 4, 4, 4, ATTN_ROWS, 128), low),
            pltpu.VMEM((4, 4, 4, ATTN_ROWS, 128), low),
            pltpu.VMEM((4, 4, 8, D), wide),
        ]
        + slots
        + [
            dma((2, 3, 3, 2, 3)),
            dma((2, 3, 3, 2, 3)),
            dma((2,)),
            dma((4,)),
            dma((3, 4)),
            dma((3, 4)),
            dma,
            dma((7,)),
            dma((7,)),
            dma((8,)),
            dma((8,)),
            dma((4,)),
            dma((4,)),
            dma((15,)),
            dma((15,)),
            dma((2, 3, 3, 2, 3)),
            dma((2, 3, 3, 2, 3)),
            dma((3, 3)),
            dma((3, 3)),
            dma((4,)),
            dma((4,)),
        ],
        compiler_params=pltpu.CompilerParams(collective_id=1, has_side_effects=True, vmem_limit_bytes=63 * MIB),
        name="layer",
    )(*operands)


def deliver_kernel(count, *refs):
    for i in range(count):
        refs[count + 1 + i][...] = refs[i][...]
    for i in (0, 1):
        refs[2 * count + 1 + i][...] = refs[count][i : i + 1, :]


def deliver(arrays, gains):
    count = len(arrays)
    return pl.pallas_call(
        functools.partial(deliver_kernel, count),
        out_shape=[jax.ShapeDtypeStruct(a.shape, a.dtype) for a in arrays] + [jax.ShapeDtypeStruct((1, D), gains.dtype)] * 2,
        in_specs=[VMEM] * (count + 1),
        out_specs=[VMEM] * (count + 2),
        name="deliver",
    )(*arrays, gains)


def per_device(
    inputs, doc_offsets, attn_gain, query_weight, key_weight, value_weight, proj_weight,
    ffn_gain, gate_weight, up_weight, down_weight, cotangent,
):
    *results, gain_sums = run_layer(
        inputs[0].T, doc_offsets, attn_gain[None], ffn_gain[None], query_weight.T, key_weight.T, value_weight.T,
        proj_weight.T, gate_weight.T, up_weight.T, down_weight.T, cotangent[0].T,
    )
    layer_out, input_grad, query_g, key_g, value_g, proj_g, gate_g, up_g, down_g, attn_gain_g, ffn_gain_g = deliver(
        results, gain_sums
    )
    return (
        layer_out.T[None], input_grad.T[None], attn_gain_g[0], query_g.T, key_g.T, value_g.T, proj_g.T,
        ffn_gain_g[0], gate_g.T, up_g.T, down_g.T,
    )


def solution(mesh):
    split = P("fsdp", "ctx")
    rows = P("fsdp", "ctx", None)
    return jax.shard_map(
        per_device,
        mesh=mesh,
        in_specs=(rows, P("fsdp", None), P(), split, split, split, split, P(), split, split, split, rows),
        out_specs=(rows, rows, P(), split, split, split, split, P(), split, split, split),
        check_vma=False,
    )
```
